32 devices in a mesh: rep: 2 (over x), tp: 16 (over z, y, core).
Axes of the slice: x: 2, y: 2, z: 4, core: 2. Of those that a mesh axis runs over, the one named last changes fastest.
Arguments:
- tokens: bfloat16 [512, 8192], P(('rep', 'tp')), parts along dimension 0, may hold values from -6 to 6
- gate_matrix: bfloat16 [8192, 14336], P(None, 'tp'), may hold values from -0.0625 to 0.0625
- up_matrix: bfloat16 [8192, 14336], P(None, 'tp'), may hold values from -0.0625 to 0.0625
- down_matrix: bfloat16 [14336, 8192], P('tp'), may hold values from -0.046875 to 0.046875
- shrink_matrices: bfloat16 [16, 8192, 128], P('rep', None, 'tp'), parts along dimension 0, may hold values from -0.0625 to 0.0625
- expand_matrices: bfloat16 [16, 128, 14336], P('rep', None, 'tp'), parts along dimension 0, may hold values from -0.75 to 0.75
- adapter_per_block: int32 [4], P('rep'), parts along dimension 0, may hold values from 0 to 7
- block_token_count: int32 [4], P('rep'), parts along dimension 0, may hold values from 32 to 128, as said below
Outputs:
- mixed_out: bfloat16 [512, 8192], P(('rep', 'tp')), parts along dimension 0
The draws below stay inside these ranges and needn't reach their ends.
There are 2 independent parts, one for each index of `rep`. The reference program is written for one: setup_inputs(seed, part) draws one part's arguments, and reference() takes and returns one part's arrays. A program takes and returns all parts, laid end to end along the dimension named above; an argument that names none is the same for every part. Nothing has to cross between parts.
Inputs may be any that keep to these rules, and one draw needn't show every extreme that they name: `block_token_count`: every block holds at least a quarter of 128 live rows, and some block is full.
All inputs are finite; a program needn't handle non-finite values.
Results may differ from the reference program's by a relative error of at most 0.014.
Values may be sent and summed in bfloat16 or wider, within the bound.
No kernel may reach another device: no remote copies, remote signals or barrier semaphores. Data moves between devices by JAX's collectives and lax.ppermute only.
A program may use at most 128 MiB of HBM per device.

```python
import jax
import jax.numpy as jnp
from jax import lax

MODEL_WIDTH = 8192
HIDDEN_UNITS = 14336
ADAPTER_RANK = 64
ADAPTER_COUNT = 8
BLOCK = 128
TOKENS = 256
BLOCKS = 2
GROUP = 896
N_TP = 16


def draw_block_token_count(key, part):
    key = jax.random.fold_in(key, 7)
    first_key, second_key = jax.random.split(key)
    live_rows = jax.random.randint(first_key, (BLOCKS,), BLOCK // 4, BLOCK + 1)
    full_spot = jax.random.randint(second_key, (), 0, BLOCKS)
    return jnp.where(jnp.arange(BLOCKS) == full_spot, BLOCK, live_rows).astype(jnp.int32)


def levels(key, shape, cuts, least, largest):
    gain = 1.0
    for dim, parts in cuts:
        heights = jax.random.uniform(jax.random.fold_in(jax.random.fold_in(key, 6), dim), (parts,), jnp.float32, least / len(cuts), largest / len(cuts))
        gain = gain * jnp.repeat(jnp.exp(heights), shape[dim] // parts).reshape((-1,) + (1,) * (len(shape) - 1 - dim))
    return gain


def normal_values(own_key, shape, width, bound, cuts=(), kind=jnp.bfloat16):
    drawn = jax.random.normal(own_key, shape, jnp.float32) * width
    if len(cuts) > 0:
        drawn = levels(own_key, shape, cuts, -0.22, 0.18) * drawn
    return jnp.clip(drawn, min=-bound, max=bound).astype(kind)


def setup_inputs(seed: int = 0, part: int = 0) -> dict:
    key_list = jax.random.split(jax.random.key(seed), 9)
    part_keys = jax.random.split(jax.random.fold_in(key_list[8], part), 9)
    tokens = normal_values(part_keys[0], (TOKENS, MODEL_WIDTH), 1.0, 6.0, ((0, 16),))
    gate_matrix = normal_values(key_list[1], (MODEL_WIDTH, HIDDEN_UNITS), MODEL_WIDTH ** -0.5, 0.0625, ((1, 16),))
    up_matrix = normal_values(key_list[2], (MODEL_WIDTH, HIDDEN_UNITS), MODEL_WIDTH ** -0.5, 0.0625, ((1, 16),))
    down_matrix = normal_values(key_list[3], (HIDDEN_UNITS, MODEL_WIDTH), HIDDEN_UNITS ** -0.5, 0.046875, ((0, 16),))
    shrink_matrices = normal_values(part_keys[4], (ADAPTER_COUNT, MODEL_WIDTH, 2 * ADAPTER_RANK), MODEL_WIDTH ** -0.5, 0.0625, ((2, 16),))
    expand_matrices = normal_values(part_keys[5], (ADAPTER_COUNT, 2 * ADAPTER_RANK, HIDDEN_UNITS), ADAPTER_RANK ** -0.5, 0.75, ((2, 16),))
    adapter_per_block = jax.random.randint(part_keys[6], (BLOCKS,), 0, ADAPTER_COUNT).astype(jnp.int32)
    block_token_count = draw_block_token_count(jax.random.fold_in(jax.random.fold_in(key_list[8], part), 71), part)
    return {"tokens": tokens, "gate_matrix": gate_matrix, "up_matrix": up_matrix, "down_matrix": down_matrix, "shrink_matrices": shrink_matrices, "expand_matrices": expand_matrices, "adapter_per_block": adapter_per_block, "block_token_count": block_token_count}


def reference(tokens, gate_matrix, up_matrix, down_matrix, shrink_matrices, expand_matrices, adapter_per_block, block_token_count):
    input_blocks = tokens.reshape(BLOCKS, BLOCK, MODEL_WIDTH).astype(jnp.float32)
    selected_shrink = shrink_matrices[adapter_per_block].astype(jnp.float32)
    rank_value = jnp.einsum('xsj,xjg->xsg', input_blocks, selected_shrink).astype(jnp.bfloat16)
    selected_expand = expand_matrices[adapter_per_block].astype(jnp.float32)
    rank_wide = rank_value.astype(jnp.float32)
    gate_delta = jnp.einsum('bkr,brf->bkf', rank_wide[:, :, :ADAPTER_RANK], selected_expand[:, :ADAPTER_RANK, :]).reshape(TOKENS, HIDDEN_UNITS)
    up_delta = jnp.einsum('bkr,brf->bkf', rank_wide[:, :, ADAPTER_RANK:], selected_expand[:, ADAPTER_RANK:, :]).reshape(TOKENS, HIDDEN_UNITS)
    gate = jnp.dot(tokens, gate_matrix, preferred_element_type=jnp.float32) + gate_delta
    up_val = jnp.dot(tokens, up_matrix, preferred_element_type=jnp.float32) + up_delta
    hidden = (jax.nn.silu(gate) * up_val).astype(jnp.bfloat16)

    def add_group(summed, group_index):
        offset = group_index * GROUP
        left_part = lax.dynamic_slice_in_dim(hidden, offset, GROUP, 1)
        right_part = lax.dynamic_slice_in_dim(down_matrix, offset, GROUP, 0)
        term = jnp.dot(left_part, right_part, preferred_element_type=jnp.float32).astype(jnp.bfloat16)
        term = lax.optimization_barrier(term)
        return summed + term.astype(jnp.float32), None

    summed, _ = lax.scan(add_group, jnp.zeros((TOKENS, MODEL_WIDTH), jnp.float32), jnp.arange(N_TP, dtype=jnp.int32))
    row_ids = jnp.arange(TOKENS, dtype=jnp.int32)
    owner_block = row_ids // BLOCK
    live_rows = block_token_count[owner_block]
    live_mask = (row_ids % BLOCK) < live_rows
    return jnp.where(live_mask[:, None], summed, jnp.zeros_like(summed)).astype(jnp.bfloat16)
```

```python
import functools

import jax
import jax.numpy as jnp
import numpy as np
from jax import lax
from jax.experimental import pallas as pl
from jax.experimental.pallas import tpu as pltpu
from jax.sharding import Mesh, PartitionSpec as P

F32 = jnp.float32
BF16 = jnp.bfloat16
VMEM_LIMIT = 56 * 1024 * 1024
SWAP = [(0, 1), (1, 0)]


def largest_tile(size, limit):
    tile = limit
    while size % tile:
        tile //= 2
    return tile


def gate_up_kernel(own_ref, sib_ref, wg_ref, wu_ref, g_ref, u_ref):
    @pl.when(pl.program_id(0) == 0)
    def _():
        g_ref[...] = jnp.zeros_like(g_ref)
        u_ref[...] = jnp.zeros_like(u_ref)

    half = own_ref.shape[0]
    rows = jnp.concatenate([own_ref[...], sib_ref[...]], axis=0)
    g_ref[...] += jnp.dot(rows, wg_ref[...], preferred_element_type=F32)
    u_ref[...] += jnp.dot(rows, wu_ref[...], preferred_element_type=F32)


def gate_up(own, sib, gate_matrix, up_matrix, first):
    half, depth = own.shape
    width = gate_matrix.shape[1]
    tile = largest_tile(depth, 1024)
    steps = depth // tile
    offset = first // tile
    out = jax.ShapeDtypeStruct((2 * half, width), F32)
    return pl.pallas_call(
        gate_up_kernel,
        grid=(steps,),
        in_specs=[
            pl.BlockSpec((half, tile), lambda k: (0, k)),
            pl.BlockSpec((half, tile), lambda k: (0, k)),
            pl.BlockSpec((tile, width), lambda k: (k + offset, 0)),
            pl.BlockSpec((tile, width), lambda k: (k + offset, 0)),
        ],
        out_specs=[pl.BlockSpec((2 * half, width), lambda k: (0, 0))] * 2,
        out_shape=[out, out],
        compiler_params=pltpu.CompilerParams(vmem_limit_bytes=VMEM_LIMIT),
        cost_estimate=pl.CostEstimate(
            flops=8 * half * depth * width,
            bytes_accessed=4 * depth * width + 4 * half * depth,
            transcendentals=0,
        ),
        name="gate_up",
    )(own, sib, gate_matrix, up_matrix)


def finish_kernel(parts, adapter_ref, *refs):
    g_refs, u_refs = refs[:parts], refs[parts : 2 * parts]
    rank_ref, expand_ref, hidden_ref = refs[2 * parts :]
    _, _, rows, width = hidden_ref.shape
    rank = rank_ref[...].reshape(2 * rows, rank_ref.shape[-1])
    half = rank.shape[1] // 2
    gate = jnp.dot(rank[:, :half], expand_ref[0, :half], preferred_element_type=F32)
    up = jnp.dot(rank[:, half:], expand_ref[0, half:], preferred_element_type=F32)
    for g_ref in g_refs:
        gate += g_ref[...].reshape(2 * rows, width)
    for u_ref in u_refs:
        up += u_ref[...].reshape(2 * rows, width)
    hidden = gate / (1.0 + jnp.exp(-gate)) * up
    hidden_ref[...] = hidden.astype(BF16).reshape(hidden_ref.shape)


def finish(gates, ups, rank, expand, adapters):
    blocks = adapters.shape[0]
    total, width = gates[0].shape
    rows = total // (2 * blocks)
    ranks = rank.shape[1]
    parts = len(gates)

    def by_block(x):
        return x.reshape(2, blocks, rows, x.shape[-1])

    wide = pl.BlockSpec((2, 1, rows, width), lambda b, ids: (0, b, 0, 0))
    hidden = pl.pallas_call(
        functools.partial(finish_kernel, parts),
        grid_spec=pltpu.PrefetchScalarGridSpec(
            num_scalar_prefetch=1,
            grid=(blocks,),
            in_specs=[wide] * (2 * parts)
            + [
                pl.BlockSpec((2, 1, rows, ranks), lambda b, ids: (0, b, 0, 0)),
                pl.BlockSpec((1, ranks, width), lambda b, ids: (ids[b], 0, 0)),
            ],
            out_specs=wide,
        ),
        out_shape=jax.ShapeDtypeStruct((2, blocks, rows, width), BF16),
        compiler_params=pltpu.CompilerParams(vmem_limit_bytes=VMEM_LIMIT),
        name="finish",
    )(adapters, *map(by_block, gates), *map(by_block, ups), by_block(rank), expand)
    return hidden.reshape(total, width)


def down_kernel(hidden_ref, w_ref, mine_ref, sib_ref):
    product = jnp.dot(hidden_ref[...], w_ref[...], preferred_element_type=F32).astype(BF16)
    half = product.shape[0] // 2
    mine_ref[...] = product[:half]
    sib_ref[...] = product[half:]


def down(hidden, down_matrix, first, columns):
    total, depth = hidden.shape
    tile = largest_tile(columns, 1024)
    offset = first // tile
    out = jax.ShapeDtypeStruct((total // 2, columns), BF16)
    return pl.pallas_call(
        down_kernel,
        grid=(columns // tile,),
        in_specs=[
            pl.BlockSpec((total, depth), lambda n: (0, 0)),
            pl.BlockSpec((depth, tile), lambda n: (0, n + offset)),
        ],
        out_specs=[pl.BlockSpec((total // 2, tile), lambda n: (0, n))] * 2,
        out_shape=[out, out],
        compiler_params=pltpu.CompilerParams(vmem_limit_bytes=VMEM_LIMIT),
        cost_estimate=pl.CostEstimate(
            flops=2 * total * depth * columns,
            bytes_accessed=2 * depth * columns + 2 * total * columns,
            transcendentals=0,
        ),
        name="down",
    )(hidden, down_matrix)


def ring_of(chips):
    return list(range(0, chips, 2)) + list(range(chips - 1, 0, -2))


def per_device(
    chips,
    tokens,
    gate_matrix,
    up_matrix,
    down_matrix,
    shrink_matrices,
    expand_matrices,
    adapter_per_block,
    block_token_count,
):
    chip, core = lax.axis_index("chip"), lax.axis_index("core")
    rows, model = tokens.shape
    blocks = adapter_per_block.shape[0]
    span = shrink_matrices.shape[2]
    half = chips * rows
    total = 2 * half
    block_rows = total // blocks
    ring = ring_of(chips)
    place = jnp.asarray(np.argsort(ring), jnp.int32)[chip]
    ring_table = jnp.asarray(ring, jnp.int32)
    rightward = [(ring[i], ring[(i + 1) % chips]) for i in range(chips)]
    leftward = [(b, a) for a, b in rightward]

    parts = 2
    depth = model // parts
    shrink = jnp.swapaxes(shrink_matrices, 1, 2)[adapter_per_block]
    gates, ups = [], []
    rank = jnp.zeros((total, blocks * span), F32)
    gathered = []
    for part in range(parts):
        piece = tokens[:, part * depth : (part + 1) * depth]
        own = lax.all_gather(piece, "chip", axis=0, tiled=True)
        sib = lax.ppermute(own, "core", SWAP)
        gathered.append((own, sib))
        pick = shrink[:, :, part * depth : (part + 1) * depth].reshape(blocks * span, depth)
        pair = [
            lax.dot_general(x, pick, (((1,), (1,)), ((), ())), preferred_element_type=F32)
            for x in (own, sib)
        ]
        rank = rank + jnp.concatenate(pair, axis=0)
    row_block = (jnp.arange(total) % half) * 2 // block_rows
    wanted = row_block[:, None] == jnp.arange(blocks)[None, :]
    rank = jnp.sum(
        jnp.where(wanted[:, :, None], rank.reshape(total, blocks, span), 0.0), axis=1
    ).astype(BF16).T

    other = lax.ppermute(rank, "core", SWAP)
    other = jnp.concatenate([other[:, half:], other[:, :half]], axis=1)
    pair = jnp.where(core == 0, jnp.stack([rank, other]), jnp.stack([other, rank]))
    pair = pair.reshape(2 * span, total)
    ranks = [pair]
    for shift in range(1, chips):
        ranks.append(lax.ppermute(pair, "chip", [(i, (i + shift) % chips) for i in range(chips)]))
    stacked = jnp.stack(ranks)
    order = (chip - jnp.arange(chips)) % chips
    rank_full = stacked[order].reshape(chips * 2 * span, total).T

    for part, (own, sib) in enumerate(gathered):
        g, u = gate_up(own, sib, gate_matrix, up_matrix, part * depth)
        gates.append(g)
        ups.append(u)
    hidden = finish(gates, ups, rank_full, expand_matrices, adapter_per_block)

    results = []
    columns = model // 2
    steps = chips // 2
    for side in range(2):
        mine, sib = down(hidden, down_matrix, side * columns, columns)
        came = lax.ppermute(sib, "core", SWAP)
        mine = mine.reshape(chips, rows, columns)
        came = came.reshape(chips, rows, columns)

        def take(offset):
            at = ring_table[(place + offset) % chips]
            return lax.dynamic_index_in_dim(mine, at, 0, False).astype(
                F32
            ) + lax.dynamic_index_in_dim(came, at, 0, False).astype(F32)

        result = take(0)
        for sign, links in ((1, rightward), (-1, leftward)):
            far = steps if (sign == 1) == (side == 0) else steps - 1
            carry = None
            for offset in range(far, 0, -1):
                value = take(sign * offset)
                if carry is not None:
                    value = value + carry.astype(F32)
                carry = lax.ppermute(value.astype(BF16), "chip", links)
            result = result + carry.astype(F32)
        results.append(result)
    summed = jnp.concatenate(results, axis=1)

    first = (2 * chip + core) * rows
    own_block = first // block_rows
    live = block_token_count[own_block]
    row_ids = first % block_rows + jnp.arange(rows, dtype=jnp.int32)
    return jnp.where((row_ids < live)[:, None], summed, 0.0).astype(BF16)


def solution(mesh):
    groups, members = mesh.devices.shape
    chips = members // 2
    fine = Mesh(mesh.devices.reshape(groups, chips, 2), ("rep", "chip", "core"))
    tp = ("chip", "core")
    return jax.shard_map(
        functools.partial(per_device, chips),
        mesh=fine,
        in_specs=(
            P(("rep", "chip", "core"), None),
            P(None, tp),
            P(None, tp),
            P(tp, None),
            P("rep", None, tp),
            P("rep", None, tp),
            P("rep"),
            P("rep"),
        ),
        out_specs=P(("rep", "chip", "core"), None),
        check_vma=False,
    )
```

```python
import functools

import jax
import jax.numpy as jnp
import numpy as np
from jax import lax
from jax.experimental import pallas as pl
from jax.experimental.pallas import tpu as pltpu
from jax.sharding import PartitionSpec as P

F32 = jnp.float32
BF16 = jnp.bfloat16
VMEM_LIMIT = 40 * 1024 * 1024


def largest_tile(size, limit):
    tile = limit
    while size % tile:
        tile //= 2
    return tile


def params():
    return pltpu.CompilerParams(vmem_limit_bytes=VMEM_LIMIT)


def cost(flops, moved):
    return pl.CostEstimate(flops=flops, bytes_accessed=moved, transcendentals=0)


def ring_of(chips):
    return list(range(0, chips, 2)) + list(range(chips - 1, 0, -2))


def layout(members, rows, block_rows):
    chips = members // 2
    ring = ring_of(chips)
    reach = chips // 2
    table = []
    for device in range(members):
        chip, core = divmod(device, 2)
        place = ring.index(chip)

        def row(side, distance, half):
            sign = 1 if side == 0 else -1
            return (2 * ring[(place + sign * distance) % chips] + half) * rows

        arrive = [row(core, 0, core), row(core, 0, 1 - core)]
        for side in (core, 1 - core):
            for step in range(1, reach + 1):
                arrive.append(row(1 - side, step, side))
                if step < reach:
                    arrive.append(row(1 - side, step, 1 - side))
        leave = []
        for side in (core, 1 - core):
            leave.append(row(side, reach, side))
            for step in range(reach - 1, 0, -1):
                leave += [row(side, step, side), row(side, step, 1 - side)]
            leave.append(row(side, 0, side))
        own = device * rows
        table.append(arrive + leave + [own // block_rows, own % block_rows, device])
    return np.asarray(table, np.int32)


def around(members):
    ring = ring_of(members // 2)
    size = len(ring)
    pairs = []
    for i in range(size):
        pairs.append((2 * ring[i], 2 * ring[(i + 1) % size]))
        pairs.append((2 * ring[i] + 1, 2 * ring[i - 1] + 1))
    return pairs


def crossing(members, bit):
    return [(i, i ^ bit) for i in range(members)]


def rank_kernel(members, blocks, table_ref, ids_ref, *refs):
    pieces, shrinks = refs[:members], refs[members : members + blocks]
    all_ref, rank_ref, total = refs[members + blocks :]
    step = pl.program_id(0)
    rows = pieces[0].shape[0]
    for index, piece in enumerate(pieces):
        start = pl.multiple_of(table_ref[index], rows)
        all_ref[pl.ds(start, rows), :] = piece[...]
    span = all_ref.shape[0] // blocks
    parts = [
        lax.dot_general(
            shrinks[b][0],
            all_ref[b * span : (b + 1) * span, :],
            (((1,), (1,)), ((), ())),
            preferred_element_type=F32,
        )
        for b in range(blocks)
    ]
    part = jnp.concatenate(parts, axis=1)

    @pl.when(step == 0)
    def _():
        total[...] = part

    @pl.when(step > 0)
    def _():
        total[...] += part

    rank_ref[...] = total[...].astype(BF16)


def rank_and_rows(table, adapters, pieces, shrink):
    members = len(pieces)
    rows, model = pieces[0].shape
    blocks = adapters.shape[0]
    span = shrink.shape[1]
    total = members * rows
    tile = largest_tile(model, 1024)

    def chosen(b):
        return pl.BlockSpec((1, span, tile), lambda k, table, ids: (ids[b], 0, k))

    return pl.pallas_call(
        functools.partial(rank_kernel, members, blocks),
        grid_spec=pltpu.PrefetchScalarGridSpec(
            num_scalar_prefetch=2,
            grid=(model // tile,),
            in_specs=[pl.BlockSpec((rows, tile), lambda k, table, ids: (0, k))] * members
            + [chosen(b) for b in range(blocks)],
            out_specs=[
                pl.BlockSpec((total, tile), lambda k, table, ids: (0, k)),
                pl.BlockSpec((span, total), lambda k, table, ids: (0, 0)),
            ],
            scratch_shapes=[pltpu.VMEM((span, total), F32)],
        ),
        out_shape=[
            jax.ShapeDtypeStruct((total, model), BF16),
            jax.ShapeDtypeStruct((span, total), BF16),
        ],
        compiler_params=params(),
        cost_estimate=cost(2 * total * model * span, 4 * total * model),
        name="rank",
    )(table, adapters, *pieces, *([shrink] * blocks))


def product_kernel(rows_ref, *refs):
    w_refs, out_ref = refs[:-1], refs[-1]
    depth = w_refs[0].shape[0]
    part = 0.0
    for index, w_ref in enumerate(w_refs):
        columns = rows_ref[:, index * depth : (index + 1) * depth]
        part += jnp.dot(columns, w_ref[...], preferred_element_type=F32)

    @pl.when(pl.program_id(0) == 0)
    def _():
        out_ref[...] = part

    @pl.when(pl.program_id(0) > 0)
    def _():
        out_ref[...] += part


def product(tokens, matrix, part, parts):
    total, model = tokens.shape
    width = matrix.shape[1]
    depth = model // parts
    tile = largest_tile(depth, 1024)
    steps = depth // tile
    split = 4

    def piece(index):
        return pl.BlockSpec(
            (tile // split, width), lambda k: ((k + part * steps) * split + index, 0)
        )

    return pl.pallas_call(
        product_kernel,
        grid=(steps,),
        in_specs=[pl.BlockSpec((total, tile), lambda k: (0, k + part * steps))]
        + [piece(index) for index in range(split)],
        out_specs=pl.BlockSpec((total, width), lambda k: (0, 0)),
        out_shape=jax.ShapeDtypeStruct((total, width), F32),
        compiler_params=params(),
        cost_estimate=cost(2 * total * depth * width, 2 * depth * (width + total)),
        name="product",
    )(tokens, *([matrix] * split))


def finish_kernel(parts, span, table_ref, ids_ref, *refs):
    g_refs, u_refs = refs[:parts], refs[parts : 2 * parts]
    rank_ref, expand_ref, hidden_ref = refs[2 * parts :]
    ranks = rank_ref.shape[0]
    device = table_ref[table_ref.shape[0] - 1]
    shape = (ranks, ranks)
    want = lax.broadcasted_iota(jnp.int32, shape, 0)
    have = lax.broadcasted_iota(jnp.int32, shape, 1)
    origin = ((have // span) ^ device) * span + have % span
    order = jnp.where(want == origin, 1.0, 0.0).astype(BF16)
    rank = jnp.dot(order, rank_ref[...], preferred_element_type=F32).T.astype(BF16)
    half = ranks // 2
    gate = jnp.dot(rank[:, :half], expand_ref[0, :half], preferred_element_type=F32)
    up = jnp.dot(rank[:, half:], expand_ref[0, half:], preferred_element_type=F32)
    for g_ref in g_refs:
        gate += g_ref[...]
    for u_ref in u_refs:
        up += u_ref[...]
    hidden_ref[...] = (gate / (1.0 + jnp.exp(-gate)) * up).astype(BF16)


def finish(table, adapters, gates, ups, rank, expand, span):
    blocks = adapters.shape[0]
    total, width = gates[0].shape
    rows = total // blocks
    ranks = rank.shape[0]
    parts = len(gates)
    wide = pl.BlockSpec((rows, width), lambda b, table, ids: (b, 0))
    return pl.pallas_call(
        functools.partial(finish_kernel, parts, span),
        grid_spec=pltpu.PrefetchScalarGridSpec(
            num_scalar_prefetch=2,
            grid=(blocks,),
            in_specs=[wide] * (2 * parts)
            + [
                pl.BlockSpec((ranks, rows), lambda b, table, ids: (0, b)),
                pl.BlockSpec((1, ranks, width), lambda b, table, ids: (ids[b], 0, 0)),
            ],
            out_specs=wide,
        ),
        out_shape=jax.ShapeDtypeStruct((total, width), BF16),
        compiler_params=params(),
        name="finish",
    )(table, adapters, *gates, *ups, rank, expand)


def down_kernel(first, groups, rows, split, table_ref, hidden_ref, *refs):
    w_refs, outs, product_ref = refs[:split], refs[split:-1], refs[-1]
    depth = w_refs[0].shape[0]
    part = 0.0
    for index, w_ref in enumerate(w_refs):
        columns = hidden_ref[:, index * depth : (index + 1) * depth]
        part += jnp.dot(columns, w_ref[...], preferred_element_type=F32)
    product_ref[...] = part.astype(BF16)
    at = first
    for out, group in zip(outs, groups, strict=True):
        for index in range(group):
            start = pl.multiple_of(table_ref[at], rows)
            out[index * rows : (index + 1) * rows, :] = product_ref[pl.ds(start, rows), :]
            at += 1


def down(table, first, hidden, down_matrix, groups, rows):
    total, depth = hidden.shape
    columns = down_matrix.shape[1]
    tile = largest_tile(columns, 1024)
    split = max(s for s in (1, 2, 4, 7) if depth % (s * 128) == 0 or s == 1)

    def piece(index):
        return pl.BlockSpec((depth // split, tile), lambda n, table: (index, n))

    return pl.pallas_call(
        functools.partial(down_kernel, first, groups, rows, split),
        grid_spec=pltpu.PrefetchScalarGridSpec(
            num_scalar_prefetch=1,
            grid=(columns // tile,),
            in_specs=[
                pl.BlockSpec((total, depth), lambda n, table: (0, 0)),
            ]
            + [piece(index) for index in range(split)],
            out_specs=[
                pl.BlockSpec((group * rows, tile), lambda n, table: (0, n)) for group in groups
            ],
            scratch_shapes=[pltpu.VMEM((total, tile), BF16)],
        ),
        out_shape=[jax.ShapeDtypeStruct((group * rows, columns), BF16) for group in groups],
        compiler_params=params(),
        cost_estimate=cost(
            2 * total * depth * columns, 2 * depth * columns + 2 * total * columns
        ),
        name="down",
    )(table, hidden, *([down_matrix] * split))


def last_kernel(table_ref, counts_ref, *refs):
    out_ref = refs[-1]
    summed = refs[0][...].astype(F32)
    for ref in refs[1:-1]:
        summed += ref[...].astype(F32)
    size = table_ref.shape[0]
    live = counts_ref[table_ref[size - 3]] - table_ref[size - 2]
    row = lax.broadcasted_iota(jnp.int32, summed.shape, 0)
    out_ref[...] = jnp.where(row < live, summed, 0.0).astype(BF16)


def last(table, counts, terms):
    shape = terms[0].shape
    return pl.pallas_call(
        last_kernel,
        grid_spec=pltpu.PrefetchScalarGridSpec(
            num_scalar_prefetch=2,
            grid=(1,),
            in_specs=[pl.BlockSpec(shape, lambda i, table, counts: (0, 0))] * len(terms),
            out_specs=pl.BlockSpec(shape, lambda i, table, counts: (0, 0)),
        ),
        out_shape=jax.ShapeDtypeStruct(shape, BF16),
        compiler_params=params(),
        name="last",
    )(table, counts, *terms)


def added(*terms):
    total = terms[0].astype(F32)
    for term in terms[1:]:
        total = total + term.astype(F32)
    return total.astype(BF16)


def per_device(
    members,
    tokens,
    gate_matrix,
    up_matrix,
    down_matrix,
    shrink_matrices,
    expand_matrices,
    adapter_per_block,
    block_token_count,
):
    rows, model = tokens.shape
    blocks = adapter_per_block.shape[0]
    span = shrink_matrices.shape[2]
    reach = members // 4
    block_rows = members * rows // blocks
    table = jnp.asarray(layout(members, rows, block_rows))[lax.axis_index("tp")]
    ring = around(members)
    swap = crossing(members, 1)

    def step(x):
        return lax.ppermute(x, "tp", ring)

    def cross(x, bit=1):
        return lax.ppermute(x, "tp", crossing(members, bit))

    first, second = tokens, cross(tokens)
    pieces, mine, theirs = [first, second], [], []
    for distance in range(1, reach + 1):
        first = step(first)
        mine.append(first)
        theirs.append(cross(first))
        if distance < reach:
            second = step(second)
            mine.append(second)
            theirs.append(cross(second))
    pieces = pieces + mine + theirs

    shrink = jnp.swapaxes(shrink_matrices, 1, 2)
    everyone, rank = rank_and_rows(table, adapter_per_block, pieces, shrink)
    bit = 1
    while bit < members:
        rank = jnp.concatenate([rank, cross(rank, bit)], axis=0)
        bit *= 2

    parts = 2
    gates = [product(everyone, gate_matrix, part, parts) for part in range(parts)]
    ups = [product(everyone, up_matrix, part, parts) for part in range(parts)]
    hidden = finish(table, adapter_per_block, gates, ups, rank, expand_matrices, span)

    slots = 2 * reach
    groups = [1] * slots + [1] + [2] * (reach - 1) + [1]
    outs = down(table, members, hidden, down_matrix, groups, rows)
    keep, give = outs[:slots], outs[slots:]
    came = [cross(x) for x in give]
    first = step(added(keep[0], came[0]))
    second = None
    for index in range(1, reach):
        pair = came[index]
        here = [keep[2 * index], pair[rows:]] + ([] if second is None else [second])
        second = step(added(*here))
        first = step(added(keep[2 * index - 1], pair[:rows], first))
    return last(table, block_token_count, [keep[-1], came[-1], first, cross(second)])


def solution(mesh):
    members = mesh.shape["tp"]
    return jax.shard_map(
        functools.partial(per_device, members),
        mesh=mesh,
        in_specs=(
            P(("rep", "tp"), None),
            P(None, "tp"),
            P(None, "tp"),
            P("tp", None),
            P("rep", None, "tp"),
            P("rep", None, "tp"),
            P("rep"),
            P("rep"),
        ),
        out_specs=P(("rep", "tp"), None),
        check_vma=False,
    )
```

```python
import functools

import jax
import jax.numpy as jnp
import numpy as np
from jax import lax
from jax.experimental import pallas as pl
from jax.experimental.pallas import tpu as pltpu
from jax.sharding import PartitionSpec as P

F32 = jnp.float32
BF16 = jnp.bfloat16
VMEM_LIMIT = 20 * 1024 * 1024


def largest_tile(size, limit):
    tile = limit
    while size % tile:
        tile //= 2
    return tile


def params():
    return pltpu.CompilerParams(vmem_limit_bytes=VMEM_LIMIT)


def cost(flops, moved):
    return pl.CostEstimate(flops=flops, bytes_accessed=moved, transcendentals=0)


def ring_of(chips):
    return list(range(0, chips, 2)) + list(range(chips - 1, 0, -2))


def layout(members, rows, block_rows):
    chips = members // 2
    ring = ring_of(chips)
    reach = chips // 2
    table = []
    for device in range(members):
        chip, core = divmod(device, 2)
        place = ring.index(chip)

        def row(side, distance, half):
            sign = 1 if side == 0 else -1
            return (2 * ring[(place + sign * distance) % chips] + half) * rows

        arrive = [row(core, 0, core), row(core, 0, 1 - core)]
        for side in (core, 1 - core):
            for step in range(1, reach + 1):
                arrive.append(row(1 - side, step, side))
                if step < reach:
                    arrive.append(row(1 - side, step, 1 - side))
        leave = []
        for side in (core, 1 - core):
            leave.append(row(side, reach, side))
            for step in range(reach - 1, 0, -1):
                leave += [row(side, step, side), row(side, step, 1 - side)]
            leave.append(row(side, 0, side))
        own = device * rows
        table.append(arrive + leave + [own // block_rows, own % block_rows, device])
    return np.asarray(table, np.int32)


def around(members):
    ring = ring_of(members // 2)
    size = len(ring)
    pairs = []
    for i in range(size):
        pairs.append((2 * ring[i], 2 * ring[(i + 1) % size]))
        pairs.append((2 * ring[i] + 1, 2 * ring[i - 1] + 1))
    return pairs


def crossing(members, bit):
    return [(i, i ^ bit) for i in range(members)]


def whole(count):
    return [pl.BlockSpec(memory_space=pltpu.VMEM)] * count


SCALARS = pl.BlockSpec(memory_space=pltpu.SMEM)
FAR = pl.BlockSpec(memory_space=pl.ANY)


def rank_kernel(numbers, block_rows, blocks, at, span, table_ref, shrink_ref, *refs):
    out_ref = refs[-1]
    pieces = refs[:-1]
    rows = pieces[0].shape[0]
    lhs = jnp.concatenate([piece[...] for piece in pieces], axis=0)
    found = [
        lax.dot_general(
            lhs, shrink_ref[table_ref[at + b]], (((1,), (1,)), ((), ())), preferred_element_type=F32
        )
        for b in range(blocks)
    ]
    for index, number in enumerate(numbers):
        block = table_ref[number] // block_rows
        part = slice(index * rows, (index + 1) * rows)
        value = found[0][part]
        for b in range(1, blocks):
            value = jnp.where(block == b, found[b][part], value)
        out_ref[part, :] = value


def rank_of(table, at, blocks, block_rows, numbers, pieces, shrink):
    rows, model = pieces[0].shape
    span = shrink.shape[1]
    total = rows * len(pieces)
    return pl.pallas_call(
        functools.partial(rank_kernel, numbers, block_rows, blocks, at, span),
        in_specs=[SCALARS] + whole(1 + len(pieces)),
        out_specs=whole(1)[0],
        out_shape=jax.ShapeDtypeStruct((total, span), F32),
        compiler_params=params(),
        cost_estimate=cost(2 * total * model * span * blocks, 2 * total * model),
        name="rank",
    )(table, shrink, *pieces)


def order_kernel(rows, groups, table_ref, *refs):
    parts, out_ref, scratch = refs[:-2], refs[-2], refs[-1]
    span = out_ref.shape[0]
    for numbers, part in zip(groups, parts, strict=True):
        for index, number in enumerate(numbers):
            start = pl.multiple_of(table_ref[number], rows)
            scratch[pl.ds(start, rows), :span] = part[index * rows : (index + 1) * rows, :]
    out_ref[...] = scratch[...].T[:span].astype(BF16)


def ordered(table, rows, groups, parts):
    span = parts[0].shape[1]
    total = sum(part.shape[0] for part in parts)
    return pl.pallas_call(
        functools.partial(order_kernel, rows, groups),
        in_specs=[SCALARS] + whole(len(parts)),
        out_specs=whole(1)[0],
        out_shape=jax.ShapeDtypeStruct((span, total), BF16),
        scratch_shapes=[pltpu.VMEM((total, 128), F32)],
        compiler_params=params(),
        name="ordered",
    )(table, *parts)


def product_kernel(first, chunks, slots, table_ref, w_ref, *refs):
    pieces = refs[: -4]
    out_ref, total, store, sems = refs[-4:]
    size = store.shape[1]
    rows = pieces[0].shape[0]

    def copy(chunk):
        return pltpu.make_async_copy(
            w_ref.at[pl.ds(first + chunk * size, size), :],
            store.at[chunk % slots],
            sems.at[chunk % slots],
        )

    for chunk in range(min(slots, chunks)):
        copy(chunk).start()
    for chunk in range(chunks):
        start = first + chunk * size
        lhs = jnp.concatenate([piece[:, start : start + size] for piece in pieces], axis=0)
        copy(chunk).wait()
        part = jnp.dot(lhs, store[chunk % slots], preferred_element_type=F32)
        if chunk + slots < chunks:
            copy(chunk + slots).start()
        if chunk == 0:
            total[...] = part
        elif chunk < chunks - 1:
            total[...] += part
        else:
            part += total[...]
            for index in range(len(pieces)):
                place = pl.multiple_of(table_ref[index], rows)
                out_ref[pl.ds(place, rows), :] = part[index * rows : (index + 1) * rows]


def product(table, pieces, matrix, part, parts):
    rows, model = pieces[0].shape
    total = rows * len(pieces)
    width = matrix.shape[1]
    depth = model // parts
    size = min(512, depth // 2)
    chunks = depth // size
    slots = min(4, chunks)
    return pl.pallas_call(
        functools.partial(product_kernel, part * depth, chunks, slots),
        in_specs=[SCALARS, FAR] + whole(len(pieces)),
        out_specs=whole(1)[0],
        out_shape=jax.ShapeDtypeStruct((total, width), F32),
        scratch_shapes=[
            pltpu.VMEM((total, width), F32),
            pltpu.VMEM((slots, size, width), BF16),
            pltpu.SemaphoreType.DMA((slots,)),
        ],
        compiler_params=params(),
        cost_estimate=cost(2 * total * depth * width, 2 * depth * (width + total)),
        name="product",
    )(table, matrix, *pieces)


def finish_kernel(parts, span, table_ref, ids_ref, *refs):
    g_refs, u_refs = refs[:parts], refs[parts : 2 * parts]
    rank_ref, expand_ref, hidden_ref = refs[2 * parts :]
    ranks = rank_ref.shape[0]
    device = table_ref[table_ref.shape[0] - 1]
    shape = (ranks, ranks)
    want = lax.broadcasted_iota(jnp.int32, shape, 0)
    have = lax.broadcasted_iota(jnp.int32, shape, 1)
    origin = ((have // span) ^ device) * span + have % span
    order = jnp.where(want == origin, 1.0, 0.0).astype(BF16)
    rank = jnp.dot(order, rank_ref[...], preferred_element_type=F32).T.astype(BF16)
    half = ranks // 2
    gate = jnp.dot(rank[:, :half], expand_ref[0, :half], preferred_element_type=F32)
    up = jnp.dot(rank[:, half:], expand_ref[0, half:], preferred_element_type=F32)
    for g_ref in g_refs:
        gate += g_ref[...]
    for u_ref in u_refs:
        up += u_ref[...]
    hidden_ref[...] = (gate / (1.0 + jnp.exp(-gate)) * up).astype(BF16)


def finish(table, at, blocks, gates, ups, rank, expand, span):
    total, width = gates[0].shape
    rows = total // blocks
    ranks = rank.shape[0]
    parts = len(gates)
    wide = pl.BlockSpec((rows, width), lambda b, table: (b, 0))

    def kernel(table_ref, *refs):
        finish_kernel(parts, span, table_ref, None, *refs)

    return pl.pallas_call(
        kernel,
        grid_spec=pltpu.PrefetchScalarGridSpec(
            num_scalar_prefetch=1,
            grid=(blocks,),
            in_specs=[wide] * (2 * parts)
            + [
                pl.BlockSpec((ranks, rows), lambda b, table: (0, b)),
                pl.BlockSpec((1, ranks, width), lambda b, table: (table[at + b], 0, 0)),
            ],
            out_specs=wide,
        ),
        out_shape=jax.ShapeDtypeStruct((total, width), BF16),
        compiler_params=params(),
        name="finish",
    )(table, *gates, *ups, rank, expand)


def down_kernel(first, groups, rows, chunks, slots, table_ref, w_ref, hidden_ref, *refs):
    outs, (product_ref, store, sems) = refs[:-3], refs[-3:]
    size = store.shape[2]

    def copy(chunk):
        return pltpu.make_async_copy(
            w_ref.at[:, pl.ds(chunk * size, size)],
            store.at[chunk % slots],
            sems.at[chunk % slots],
        )

    for chunk in range(min(slots, chunks)):
        copy(chunk).start()
    hidden = hidden_ref[...]
    for chunk in range(chunks):
        columns = slice(chunk * size, (chunk + 1) * size)
        copy(chunk).wait()
        part = jnp.dot(hidden, store[chunk % slots], preferred_element_type=F32)
        if chunk + slots < chunks:
            copy(chunk + slots).start()
        product_ref[...] = part.astype(BF16)
        at = first
        for out, group in zip(outs, groups, strict=True):
            for index in range(group):
                start = pl.multiple_of(table_ref[at], rows)
                out[index * rows : (index + 1) * rows, columns] = product_ref[pl.ds(start, rows), :]
                at += 1


def down(table, first, hidden, down_matrix, groups, rows):
    total, depth = hidden.shape
    columns = down_matrix.shape[1]
    size = min(512, columns // 2)
    chunks = columns // size
    slots = min(4, chunks)
    return pl.pallas_call(
        functools.partial(down_kernel, first, groups, rows, chunks, slots),
        in_specs=[SCALARS, FAR] + whole(1),
        out_specs=whole(len(groups)),
        out_shape=[jax.ShapeDtypeStruct((group * rows, columns), BF16) for group in groups],
        scratch_shapes=[
            pltpu.VMEM((total, size), BF16),
            pltpu.VMEM((slots, depth, size), BF16),
            pltpu.SemaphoreType.DMA((slots,)),
        ],
        compiler_params=params(),
        cost_estimate=cost(
            2 * total * depth * columns, 2 * depth * columns + 2 * total * columns
        ),
        name="down",
    )(table, down_matrix, hidden)


def last_kernel(at, table_ref, *refs):
    out_ref = refs[-1]
    summed = refs[0][...].astype(F32)
    for ref in refs[1:-1]:
        summed += ref[...].astype(F32)
    size = table_ref.shape[0]
    live = table_ref[at + table_ref[size - 3]] - table_ref[size - 2]
    row = lax.broadcasted_iota(jnp.int32, summed.shape, 0)
    out_ref[...] = jnp.where(row < live, summed, 0.0).astype(BF16)


def last(table, at, terms):
    shape = terms[0].shape
    return pl.pallas_call(
        functools.partial(last_kernel, at),
        in_specs=[SCALARS] + whole(len(terms)),
        out_specs=whole(1)[0],
        out_shape=jax.ShapeDtypeStruct(shape, BF16),
        compiler_params=params(),
        name="last",
    )(table, *terms)


def add_kernel(starts, *refs):
    out_ref = refs[-1]
    rows = out_ref.shape[0]
    total = 0.0
    for start, ref in zip(starts, refs[:-1], strict=True):
        total += ref[start : start + rows, :].astype(F32)
    out_ref[...] = total.astype(BF16)


def added(rows, *terms):
    starts = [start for start, _ in terms]
    columns = terms[0][1].shape[1]
    return pl.pallas_call(
        functools.partial(add_kernel, starts),
        in_specs=whole(len(terms)),
        out_specs=whole(1)[0],
        out_shape=jax.ShapeDtypeStruct((rows, columns), BF16),
        compiler_params=params(),
        cost_estimate=cost(len(terms) * rows * columns, 2 * rows * columns),
        name="added",
    )(*[term for _, term in terms])


def per_device(
    members,
    tokens,
    gate_matrix,
    up_matrix,
    down_matrix,
    shrink_matrices,
    expand_matrices,
    adapter_per_block,
    block_token_count,
):
    rows, model = tokens.shape
    blocks = adapter_per_block.shape[0]
    span = shrink_matrices.shape[2]
    reach = members // 4
    block_rows = members * rows // blocks
    where = layout(members, rows, block_rows)
    known = where.shape[1]
    here = jnp.asarray(where)[lax.axis_index("tp")]
    table = jnp.concatenate([here, adapter_per_block, block_token_count, here[-3:]])
    adapters_at, counts_at = known, known + blocks
    ring = around(members)

    def step(x):
        return lax.ppermute(x, "tp", ring)

    def cross(x, bit=1):
        return lax.ppermute(x, "tp", crossing(members, bit))

    first, second = tokens, cross(tokens)
    pieces, mine, theirs = [first, second], [], []
    for distance in range(1, reach + 1):
        first = step(first)
        mine.append(first)
        theirs.append(cross(first))
        if distance < reach:
            second = step(second)
            mine.append(second)
            theirs.append(cross(second))
    pieces = pieces + mine + theirs

    shrink = jnp.swapaxes(shrink_matrices, 1, 2)
    early = reach if reach > 1 else 1
    soon = [0, 1] + [2 + i for i in range(early)] + [2 + len(mine) + i for i in range(early - 2)]
    late = [i for i in range(members) if i not in soon]
    groups = [soon, late]
    found = [
        rank_of(
            table, adapters_at, blocks, block_rows, group, [pieces[i] for i in group], shrink
        )
        for group in groups
    ]
    rank = ordered(table, rows, groups, found)
    bit = 1
    while bit < members:
        rank = jnp.concatenate([rank, cross(rank, bit)], axis=0)
        bit *= 2

    parts = 2
    gates = [product(table, pieces, gate_matrix, part, parts) for part in range(parts)]
    ups = [product(table, pieces, up_matrix, part, parts) for part in range(parts)]
    hidden = finish(table, adapters_at, blocks, gates, ups, rank, expand_matrices, span)

    slots = 2 * reach
    groups = [1] * slots + [1] + [2] * (reach - 1) + [1]
    outs = down(table, members, hidden, down_matrix, groups, rows)
    keep, give = outs[:slots], outs[slots:]
    came = [cross(x) for x in give]
    first = step(added(rows, (0, keep[0]), (0, came[0])))
    second = None
    for index in range(1, reach):
        more = [] if second is None else [(0, second)]
        second = step(added(rows, (0, keep[2 * index]), (rows, came[index]), *more))
        first = step(added(rows, (0, keep[2 * index - 1]), (0, came[index]), (0, first)))
    return last(table, counts_at, [keep[-1], came[-1], first, cross(second)])


def solution(mesh):
    members = mesh.shape["tp"]
    return jax.shard_map(
        functools.partial(per_device, members),
        mesh=mesh,
        in_specs=(
            P(("rep", "tp"), None),
            P(None, "tp"),
            P(None, "tp"),
            P("tp", None),
            P("rep", None, "tp"),
            P("rep", None, "tp"),
            P("rep"),
            P("rep"),
        ),
        out_specs=P(("rep", "tp"), None),
        check_vma=False,
    )
```

```python
import functools

import jax
import jax.numpy as jnp
from jax import lax
from jax.experimental import pallas as pl
from jax.experimental.pallas import tpu as pltpu
from jax.sharding import PartitionSpec as P

F32 = jnp.float32
BF16 = jnp.bfloat16
VMEM_LIMIT = 20 * 1024 * 1024


def largest_tile(size, limit):
    tile = limit
    while size % tile:
        tile //= 2
    return tile


def params():
    return pltpu.CompilerParams(vmem_limit_bytes=VMEM_LIMIT)


def cost(flops, moved):
    return pl.CostEstimate(flops=flops, bytes_accessed=moved, transcendentals=0)


def ring_of(chips):
    return list(range(0, chips, 2)) + list(range(chips - 1, 0, -2))


def piece_row(device, members, rows, side, distance, half):
    chips = members // 2
    chip = device // 2
    place = jnp.where(chip % 2 == 0, chip // 2, chips - (chip + 1) // 2)
    spot = (place + chips + jnp.where(side == 0, distance, -distance)) % chips
    there = jnp.where(spot < chips // 2, 2 * spot, 2 * (chips - spot) - 1)
    return pl.multiple_of((2 * there + half) * rows, rows)


def arrivals(device, members, rows):
    core, reach = device % 2, members // 4
    places = [(core, 0, core), (core, 0, 1 - core)]
    for side in (core, 1 - core):
        for step in range(1, reach + 1):
            places.append((1 - side, step, side))
            if step < reach:
                places.append((1 - side, step, 1 - side))
    return [piece_row(device, members, rows, *place) for place in places]


def departures(device, members, rows):
    core, reach = device % 2, members // 4
    places = []
    for side in (core, 1 - core):
        places.append((side, reach, side))
        for step in range(reach - 1, 0, -1):
            places += [(side, step, side), (side, step, 1 - side)]
        places.append((side, 0, side))
    return [piece_row(device, members, rows, *place) for place in places]


def around(members):
    ring = ring_of(members // 2)
    size = len(ring)
    pairs = []
    for i in range(size):
        pairs.append((2 * ring[i], 2 * ring[(i + 1) % size]))
        pairs.append((2 * ring[i] + 1, 2 * ring[i - 1] + 1))
    return pairs


def crossing(members, bit):
    return [(i, i ^ bit) for i in range(members)]


def whole(count):
    return [pl.BlockSpec(memory_space=pltpu.VMEM)] * count


SCALARS = pl.BlockSpec(memory_space=pltpu.SMEM)
FAR = pl.BlockSpec(memory_space=pl.ANY)


def far(x):
    return pltpu.with_memory_space_constraint(x, pltpu.HBM)


def prepare_kernel(blocks, ids_ref, tokens_ref, shrink_ref, expand_ref, passed_in, *refs):
    own_ref, weights_ref, chosen_ref, passed_out, sems = refs
    copies = [pltpu.make_async_copy(tokens_ref, own_ref, sems.at[0])]
    for b in range(blocks):
        copies.append(
            pltpu.make_async_copy(shrink_ref.at[ids_ref[b]], weights_ref.at[b], sems.at[1 + 2 * b])
        )
        copies.append(
            pltpu.make_async_copy(expand_ref.at[ids_ref[b]], chosen_ref.at[b], sems.at[2 + 2 * b])
        )
    for copy in copies:
        copy.start()
    for copy in copies:
        copy.wait()


def prepare(adapters, tokens, shrink, expand, passed):
    blocks = adapters.shape[0]

    def like(shape):
        return jax.ShapeDtypeStruct(shape, BF16)

    return pl.pallas_call(
        functools.partial(prepare_kernel, blocks),
        in_specs=[SCALARS, FAR, FAR, FAR, FAR],
        out_specs=whole(3) + [FAR],
        out_shape=[
            like(tokens.shape),
            like((blocks,) + shrink.shape[1:]),
            like((blocks,) + expand.shape[1:]),
            like(passed.shape),
        ],
        input_output_aliases={4: 3},
        scratch_shapes=[pltpu.SemaphoreType.DMA((1 + 2 * blocks,))],
        compiler_params=params(),
        name="prepare",
    )(adapters, far(tokens), far(shrink), far(expand), passed)


def rank_kernel(shrink_ref, *refs):
    pieces, out_ref, scratch = refs[:-2], refs[-2], refs[-1]
    members = len(pieces)
    rows = pieces[0].shape[0]
    blocks, span, _ = shrink_ref.shape
    block_rows = members * rows // blocks
    places = arrivals(lax.axis_index("tp"), members, rows)
    lhs = jnp.concatenate([piece[...] for piece in pieces], axis=0)
    weights = jnp.concatenate([shrink_ref[b] for b in range(blocks)], axis=0)
    found = lax.dot_general(
        lhs, weights, (((1,), (1,)), ((), ())), preferred_element_type=F32
    )
    for index, place in enumerate(places):
        part = found[index * rows : (index + 1) * rows]
        value = part[:, :span]
        for b in range(1, blocks):
            value = jnp.where(place // block_rows == b, part[:, b * span : (b + 1) * span], value)
        scratch[pl.ds(place, rows), :span] = value
    out_ref[...] = scratch[...].T[:span].astype(BF16)


def rank_of(pieces, shrink):
    rows, model = pieces[0].shape
    blocks, span, _ = shrink.shape
    total = rows * len(pieces)
    return pl.pallas_call(
        rank_kernel,
        in_specs=whole(1 + len(pieces)),
        out_specs=whole(1)[0],
        out_shape=jax.ShapeDtypeStruct((span, total), BF16),
        scratch_shapes=[pltpu.VMEM((total, 128), F32)],
        compiler_params=params(),
        cost_estimate=cost(2 * total * model * span * blocks, 2 * total * model),
        name="rank",
    )(shrink, *pieces)


def product_kernel(first, size, chunks, slots, w_ref, *refs):
    pieces = refs[:-5]
    out_ref, total, store, sems = refs[-4:]
    rows = pieces[0].shape[0]

    def copy(chunk):
        return pltpu.make_async_copy(
            w_ref.at[pl.ds(first + chunk * size, size), :],
            store.at[chunk % slots],
            sems.at[chunk % slots],
        )

    for chunk in range(slots):
        copy(chunk).start()
    places = arrivals(lax.axis_index("tp"), len(pieces), rows)
    for chunk in range(chunks):
        start = first + chunk * size
        lhs = jnp.concatenate([piece[:, start : start + size] for piece in pieces], axis=0)
        copy(chunk).wait()
        part = jnp.dot(lhs, store[chunk % slots], preferred_element_type=F32)
        if chunk + slots < chunks:
            copy(chunk + slots).start()
        if chunk > 0:
            part += total[...]
        if chunk < chunks - 1:
            total[...] = part
    for index, place in enumerate(places):
        out_ref[pl.ds(place, rows), :] = part[index * rows : (index + 1) * rows]


def product(pieces, matrix, part, parts, after):
    rows, model = pieces[0].shape
    total = rows * len(pieces)
    width = matrix.shape[1]
    depth = model // parts
    size = min(1024, depth)
    chunks = depth // size
    slots = min(4, chunks)
    return pl.pallas_call(
        functools.partial(product_kernel, part * depth, size, chunks, slots),
        in_specs=[FAR] + whole(len(pieces) + 1),
        out_specs=whole(1)[0],
        out_shape=jax.ShapeDtypeStruct((total, width), F32),
        scratch_shapes=[
            pltpu.VMEM((total, width), F32),
            pltpu.VMEM((slots, size, width), BF16),
            pltpu.SemaphoreType.DMA((slots,)),
        ],
        compiler_params=params(),
        cost_estimate=cost(2 * total * depth * width, 2 * depth * (width + total)),
        name="product",
    )(far(matrix), *pieces, after)


def finish_kernel(span, gate_a, gate_b, up_a, up_b, rank_ref, expand_ref, hidden_ref):
    ranks = rank_ref.shape[0]
    device = lax.axis_index("tp")
    shape = (ranks, ranks)
    want = lax.broadcasted_iota(jnp.int32, shape, 0)
    have = lax.broadcasted_iota(jnp.int32, shape, 1)
    origin = ((have // span) ^ device) * span + have % span
    order = jnp.where(want == origin, 1.0, 0.0).astype(BF16)
    rank = jnp.dot(order, rank_ref[...], preferred_element_type=F32).T.astype(BF16)
    half = ranks // 2
    blocks = expand_ref.shape[0]
    rows = hidden_ref.shape[0] // blocks
    for b in range(blocks):
        part = slice(b * rows, (b + 1) * rows)
        expand = expand_ref[b]
        gate = jnp.dot(rank[part, :half], expand[:half], preferred_element_type=F32)
        up = jnp.dot(rank[part, half:], expand[half:], preferred_element_type=F32)
        gate += gate_a[part] + gate_b[part]
        up += up_a[part] + up_b[part]
        hidden_ref[part] = (gate / (1.0 + jnp.exp(-gate)) * up).astype(BF16)


def finish(products, rank, expand, span):
    total, width = products[0].shape
    return pl.pallas_call(
        functools.partial(finish_kernel, span),
        in_specs=whole(6),
        out_specs=whole(1)[0],
        out_shape=jax.ShapeDtypeStruct((total, width), BF16),
        compiler_params=params(),
        name="finish",
    )(*products, rank, expand)


def down_kernel(members, groups, rows, chunks, slots, w_ref, hidden_ref, *refs):
    outs, (product_ref, store, sems) = refs[:-3], refs[-3:]
    size = store.shape[2]

    def copy(chunk):
        return pltpu.make_async_copy(
            w_ref.at[:, pl.ds(chunk * size, size)],
            store.at[chunk % slots],
            sems.at[chunk % slots],
        )

    for chunk in range(slots):
        copy(chunk).start()
    places = departures(lax.axis_index("tp"), members, rows)
    hidden = hidden_ref[...]
    for chunk in range(chunks):
        columns = slice(chunk * size, (chunk + 1) * size)
        copy(chunk).wait()
        part = jnp.dot(hidden, store[chunk % slots], preferred_element_type=F32)
        if chunk + slots < chunks:
            copy(chunk + slots).start()
        product_ref[...] = part.astype(BF16)
        at = 0
        for out, group in zip(outs, groups, strict=True):
            for index in range(group):
                out[index * rows : (index + 1) * rows, columns] = product_ref[
                    pl.ds(places[at], rows), :
                ]
                at += 1


def down(hidden, down_matrix, groups, rows):
    total, depth = hidden.shape
    columns = down_matrix.shape[1]
    size = min(1024, columns)
    chunks = columns // size
    slots = min(4, chunks)
    return pl.pallas_call(
        functools.partial(down_kernel, total // rows, groups, rows, chunks, slots),
        in_specs=[FAR] + whole(1),
        out_specs=whole(len(groups)),
        out_shape=[jax.ShapeDtypeStruct((group * rows, columns), BF16) for group in groups],
        scratch_shapes=[
            pltpu.VMEM((total, size), BF16),
            pltpu.VMEM((slots, depth, size), BF16),
            pltpu.SemaphoreType.DMA((slots,)),
        ],
        compiler_params=params(),
        cost_estimate=cost(
            2 * total * depth * columns, 2 * depth * columns + 2 * total * columns
        ),
        name="down",
    )(far(down_matrix), hidden)


def last_kernel(blocks, members, counts_ref, *refs):
    out_ref = refs[-1]
    rows = out_ref.shape[0]
    summed = refs[0][...].astype(F32)
    for ref in refs[1:-1]:
        summed += ref[...].astype(F32)
    first = lax.axis_index("tp") * rows
    block_rows = members * rows // blocks
    live = counts_ref[first // block_rows] - first % block_rows
    row = lax.broadcasted_iota(jnp.int32, summed.shape, 0)
    out_ref[...] = jnp.where(row < live, summed, 0.0).astype(BF16)


def last(members, counts, terms):
    return pl.pallas_call(
        functools.partial(last_kernel, counts.shape[0], members),
        in_specs=[SCALARS] + whole(len(terms)),
        out_specs=whole(1)[0],
        out_shape=jax.ShapeDtypeStruct(terms[0].shape, BF16),
        compiler_params=params(),
        name="last",
    )(counts, *terms)


def add_kernel(starts, *refs):
    out_ref = refs[-1]
    rows = out_ref.shape[0]
    total = 0.0
    for start, ref in zip(starts, refs[:-1], strict=True):
        total += ref[start : start + rows, :].astype(F32)
    out_ref[...] = total.astype(BF16)


def added(rows, *terms):
    starts = [start for start, _ in terms]
    columns = terms[0][1].shape[1]
    return pl.pallas_call(
        functools.partial(add_kernel, starts),
        in_specs=whole(len(terms)),
        out_specs=whole(1)[0],
        out_shape=jax.ShapeDtypeStruct((rows, columns), BF16),
        compiler_params=params(),
        cost_estimate=cost(len(terms) * rows * columns, 2 * rows * columns),
        name="added",
    )(*[term for _, term in terms])


def per_device(
    members,
    tokens,
    gate_matrix,
    up_matrix,
    down_matrix,
    shrink_matrices,
    expand_matrices,
    adapter_per_block,
    block_token_count,
):
    rows = tokens.shape[0]
    span = shrink_matrices.shape[2]
    reach = members // 4
    ring = around(members)

    def step(x):
        return lax.ppermute(x, "tp", ring)

    def cross(x, bit=1):
        return lax.ppermute(x, "tp", crossing(members, bit))

    first = tokens
    own, shrink, expand, second = prepare(
        adapter_per_block,
        tokens,
        jnp.swapaxes(shrink_matrices, 1, 2),
        expand_matrices,
        cross(tokens),
    )
    pieces, mine, theirs = [own, second], [], []
    for distance in range(1, reach + 1):
        first = step(first)
        mine.append(first)
        theirs.append(cross(first))
        if distance < reach:
            second = step(second)
            mine.append(second)
            theirs.append(cross(second))
    pieces = pieces + mine + theirs

    rank = rank_of(pieces, shrink)
    work = [(gate_matrix, 0), (gate_matrix, 1), (up_matrix, 0), (up_matrix, 1)]
    products, after = [], rank
    bit = 1
    while bit < members or work:
        if work:
            matrix, part = work.pop(0)
            products.append(product(pieces, matrix, part, 2, after))
        if bit < members:
            after = cross(rank, bit)
            rank = jnp.concatenate([rank, after], axis=0)
            bit *= 2
    hidden = finish(products, rank, expand, span)

    slots = 2 * reach
    groups = [1] * slots + [1] + [2] * (reach - 1) + [1]
    outs = down(hidden, down_matrix, groups, rows)
    keep, give = outs[:slots], outs[slots:]
    came = [cross(x) for x in give]
    first = step(added(rows, (0, keep[0]), (0, came[0])))
    second = None
    for index in range(1, reach):
        more = [] if second is None else [(0, second)]
        second = step(added(rows, (0, keep[2 * index]), (rows, came[index]), *more))
        first = step(added(rows, (0, keep[2 * index - 1]), (0, came[index]), (0, first)))
    return last(members, block_token_count, [keep[-1], came[-1], first, cross(second)])


def solution(mesh):
    members = mesh.shape["tp"]
    return jax.shard_map(
        functools.partial(per_device, members),
        mesh=mesh,
        in_specs=(
            P(("rep", "tp"), None),
            P(None, "tp"),
            P(None, "tp"),
            P("tp", None),
            P("rep", None, "tp"),
            P("rep", None, "tp"),
            P("rep"),
            P("rep"),
        ),
        out_specs=P(("rep", "tp"), None),
        check_vma=False,
    )
```

```python
import functools

import jax
import jax.numpy as jnp
from jax import lax
from jax.experimental import pallas as pl
from jax.experimental.pallas import tpu as pltpu
from jax.sharding import PartitionSpec as P

F32 = jnp.float32
BF16 = jnp.bfloat16
VMEM_LIMIT = 20 * 1024 * 1024


def largest_tile(size, limit):
    tile = limit
    while size % tile:
        tile //= 2
    return tile


def params():
    return pltpu.CompilerParams(vmem_limit_bytes=VMEM_LIMIT)


def cost(flops, moved):
    return pl.CostEstimate(flops=flops, bytes_accessed=moved, transcendentals=0)


def ring_of(chips):
    return list(range(0, chips, 2)) + list(range(chips - 1, 0, -2))


def piece_row(device, members, rows, side, distance, half):
    chips = members // 2
    chip = device // 2
    place = jnp.where(chip % 2 == 0, chip // 2, chips - (chip + 1) // 2)
    spot = (place + chips + jnp.where(side == 0, distance, -distance)) % chips
    there = jnp.where(spot < chips // 2, 2 * spot, 2 * (chips - spot) - 1)
    return pl.multiple_of((2 * there + half) * rows, rows)


def arrivals(device, members, rows):
    core, reach = device % 2, members // 4
    places = [(core, 0, core), (core, 0, 1 - core)]
    for side in (core, 1 - core):
        for step in range(1, reach + 1):
            places.append((1 - side, step, side))
            if step < reach:
                places.append((1 - side, step, 1 - side))
    return [piece_row(device, members, rows, *place) for place in places]


def departures(device, members, rows):
    core, reach = device % 2, members // 4
    places = []
    for side in (core, 1 - core):
        places.append((side, reach, side))
        for step in range(reach - 1, 0, -1):
            places += [(side, step, side), (side, step, 1 - side)]
        places.append((side, 0, side))
    return [piece_row(device, members, rows, *place) for place in places]


def around(members):
    ring = ring_of(members // 2)
    size = len(ring)
    pairs = []
    for i in range(size):
        pairs.append((2 * ring[i], 2 * ring[(i + 1) % size]))
        pairs.append((2 * ring[i] + 1, 2 * ring[i - 1] + 1))
    return pairs


def crossing(members, bit):
    return [(i, i ^ bit) for i in range(members)]


def whole(count):
    return [pl.BlockSpec(memory_space=pltpu.VMEM)] * count


SCALARS = pl.BlockSpec(memory_space=pltpu.SMEM)
FAR = pl.BlockSpec(memory_space=pl.ANY)


def far(x):
    return pltpu.with_memory_space_constraint(x, pltpu.HBM)


def prepare_kernel(blocks, ids_ref, tokens_ref, shrink_ref, expand_ref, passed_in, *refs):
    own_ref, weights_ref, chosen_ref, passed_out, sems = refs
    copies = [pltpu.make_async_copy(tokens_ref, own_ref, sems.at[0])]
    for b in range(blocks):
        copies.append(
            pltpu.make_async_copy(shrink_ref.at[ids_ref[b]], weights_ref.at[b], sems.at[1 + 2 * b])
        )
        copies.append(
            pltpu.make_async_copy(expand_ref.at[ids_ref[b]], chosen_ref.at[b], sems.at[2 + 2 * b])
        )
    for copy in copies:
        copy.start()
    for copy in copies:
        copy.wait()


def prepare(adapters, tokens, shrink, expand, passed):
    blocks = adapters.shape[0]

    def like(shape):
        return jax.ShapeDtypeStruct(shape, BF16)

    return pl.pallas_call(
        functools.partial(prepare_kernel, blocks),
        in_specs=[SCALARS, FAR, FAR, FAR, FAR],
        out_specs=whole(3) + [FAR],
        out_shape=[
            like(tokens.shape),
            like((blocks,) + shrink.shape[1:]),
            like((blocks,) + expand.shape[1:]),
            like(passed.shape),
        ],
        input_output_aliases={4: 3},
        cost_estimate=cost(30_000_000_000, 0),
        scratch_shapes=[pltpu.SemaphoreType.DMA((1 + 2 * blocks,))],
        compiler_params=params(),
        name="prepare",
    )(adapters, far(tokens), far(shrink), far(expand), passed)


def rank_kernel(shrink_ref, *refs):
    pieces, out_ref, scratch = refs[:-2], refs[-2], refs[-1]
    members = len(pieces)
    rows = pieces[0].shape[0]
    blocks, span, _ = shrink_ref.shape
    block_rows = members * rows // blocks
    places = arrivals(lax.axis_index("tp"), members, rows)
    lhs = jnp.concatenate([piece[...] for piece in pieces], axis=0)
    weights = jnp.concatenate([shrink_ref[b] for b in range(blocks)], axis=0)
    found = lax.dot_general(
        lhs, weights, (((1,), (1,)), ((), ())), preferred_element_type=F32
    )
    for index, place in enumerate(places):
        part = found[index * rows : (index + 1) * rows]
        value = part[:, :span]
        for b in range(1, blocks):
            value = jnp.where(place // block_rows == b, part[:, b * span : (b + 1) * span], value)
        scratch[pl.ds(place, rows), :span] = value
    out_ref[...] = scratch[...].T[:span].astype(BF16)


def rank_of(pieces, shrink):
    rows, model = pieces[0].shape
    blocks, span, _ = shrink.shape
    total = rows * len(pieces)
    return pl.pallas_call(
        rank_kernel,
        in_specs=whole(1 + len(pieces)),
        out_specs=whole(1)[0],
        out_shape=jax.ShapeDtypeStruct((span, total), BF16),
        scratch_shapes=[pltpu.VMEM((total, 128), F32)],
        compiler_params=params(),
        cost_estimate=cost(2 * total * model * span * blocks, 2 * total * model),
        name="rank",
    )(shrink, *pieces)


def product_kernel(first, w_ref, *refs):
    pieces, out_ref = refs[:-2], refs[-1]
    rows = pieces[0].shape[0]
    depth = w_ref.shape[0] // 2
    size = min(2048, depth)
    places = arrivals(lax.axis_index("tp"), len(pieces), rows)
    part = 0.0
    for start in range(first, first + depth, size):
        lhs = jnp.concatenate([piece[:, start : start + size] for piece in pieces], axis=0)
        part += jnp.dot(lhs, w_ref[start : start + size, :], preferred_element_type=F32)
    for index, place in enumerate(places):
        out_ref[pl.ds(place, rows), :] = part[index * rows : (index + 1) * rows]


def product(pieces, matrix, part, parts, after):
    rows, model = pieces[0].shape
    total = rows * len(pieces)
    width = matrix.shape[1]
    depth = model // parts
    return pl.pallas_call(
        functools.partial(product_kernel, part * depth),
        in_specs=whole(len(pieces) + 2),
        out_specs=whole(1)[0],
        out_shape=jax.ShapeDtypeStruct((total, width), F32),
        compiler_params=params(),
        cost_estimate=cost(2 * total * depth * width, 2 * depth * (width + total)),
        name="product",
    )(matrix, *pieces, after)


def finish_kernel(span, gate_a, gate_b, up_a, up_b, rank_ref, expand_ref, hidden_ref):
    ranks = rank_ref.shape[0]
    device = lax.axis_index("tp")
    shape = (ranks, ranks)
    want = lax.broadcasted_iota(jnp.int32, shape, 0)
    have = lax.broadcasted_iota(jnp.int32, shape, 1)
    origin = ((have // span) ^ device) * span + have % span
    order = jnp.where(want == origin, 1.0, 0.0).astype(BF16)
    rank = jnp.dot(order, rank_ref[...], preferred_element_type=F32).T.astype(BF16)
    half = ranks // 2
    blocks = expand_ref.shape[0]
    rows = hidden_ref.shape[0] // blocks
    for b in range(blocks):
        part = slice(b * rows, (b + 1) * rows)
        expand = expand_ref[b]
        gate = jnp.dot(rank[part, :half], expand[:half], preferred_element_type=F32)
        up = jnp.dot(rank[part, half:], expand[half:], preferred_element_type=F32)
        gate += gate_a[part] + gate_b[part]
        up += up_a[part] + up_b[part]
        hidden_ref[part] = (gate / (1.0 + jnp.exp(-gate)) * up).astype(BF16)


def finish(products, rank, expand, span):
    total, width = products[0].shape
    return pl.pallas_call(
        functools.partial(finish_kernel, span),
        in_specs=whole(6),
        out_specs=whole(1)[0],
        out_shape=jax.ShapeDtypeStruct((total, width), BF16),
        compiler_params=params(),
        name="finish",
    )(*products, rank, expand)


def down_kernel(members, groups, rows, size, w_ref, hidden_ref, *refs):
    outs, product_ref = refs[:-1], refs[-1]
    places = departures(lax.axis_index("tp"), members, rows)
    hidden = hidden_ref[...]
    for start in range(0, w_ref.shape[1], size):
        columns = slice(start, start + size)
        part = jnp.dot(hidden, w_ref[:, columns], preferred_element_type=F32)
        product_ref[...] = part.astype(BF16)
        at = 0
        for out, group in zip(outs, groups, strict=True):
            for index in range(group):
                out[index * rows : (index + 1) * rows, columns] = product_ref[
                    pl.ds(places[at], rows), :
                ]
                at += 1


def down(hidden, down_matrix, groups, rows):
    total, depth = hidden.shape
    columns = down_matrix.shape[1]
    size = min(1024, columns)
    return pl.pallas_call(
        functools.partial(down_kernel, total // rows, groups, rows, size),
        in_specs=whole(2),
        out_specs=whole(len(groups)),
        out_shape=[jax.ShapeDtypeStruct((group * rows, columns), BF16) for group in groups],
        scratch_shapes=[pltpu.VMEM((total, size), BF16)],
        compiler_params=params(),
        cost_estimate=cost(
            2 * total * depth * columns, 2 * depth * columns + 2 * total * columns
        ),
        name="down",
    )(down_matrix, hidden)


def last_kernel(blocks, members, counts_ref, *refs):
    out_ref = refs[-1]
    rows = out_ref.shape[0]
    summed = refs[0][...].astype(F32)
    for ref in refs[1:-1]:
        summed += ref[...].astype(F32)
    first = lax.axis_index("tp") * rows
    block_rows = members * rows // blocks
    live = counts_ref[first // block_rows] - first % block_rows
    row = lax.broadcasted_iota(jnp.int32, summed.shape, 0)
    out_ref[...] = jnp.where(row < live, summed, 0.0).astype(BF16)


def last(members, counts, terms):
    return pl.pallas_call(
        functools.partial(last_kernel, counts.shape[0], members),
        in_specs=[SCALARS] + whole(len(terms)),
        out_specs=whole(1)[0],
        out_shape=jax.ShapeDtypeStruct(terms[0].shape, BF16),
        compiler_params=params(),
        name="last",
    )(counts, *terms)


def add_kernel(starts, *refs):
    out_ref = refs[-1]
    rows = out_ref.shape[0]
    total = 0.0
    for start, ref in zip(starts, refs[:-1], strict=True):
        total += ref[start : start + rows, :].astype(F32)
    out_ref[...] = total.astype(BF16)


def added(rows, *terms):
    starts = [start for start, _ in terms]
    columns = terms[0][1].shape[1]
    return pl.pallas_call(
        functools.partial(add_kernel, starts),
        in_specs=whole(len(terms)),
        out_specs=whole(1)[0],
        out_shape=jax.ShapeDtypeStruct((rows, columns), BF16),
        compiler_params=params(),
        cost_estimate=cost(len(terms) * rows * columns, 2 * rows * columns),
        name="added",
    )(*[term for _, term in terms])


def per_device(
    members,
    tokens,
    gate_matrix,
    up_matrix,
    down_matrix,
    shrink_matrices,
    expand_matrices,
    adapter_per_block,
    block_token_count,
):
    rows = tokens.shape[0]
    span = shrink_matrices.shape[2]
    reach = members // 4
    ring = around(members)

    def step(x):
        return lax.ppermute(x, "tp", ring)

    def cross(x, bit=1):
        return lax.ppermute(x, "tp", crossing(members, bit))

    first = tokens
    own, shrink, expand, second = prepare(
        adapter_per_block,
        tokens,
        jnp.swapaxes(shrink_matrices, 1, 2),
        expand_matrices,
        cross(tokens),
    )
    pieces, mine, theirs = [own, second], [], []
    for distance in range(1, reach + 1):
        first = step(first)
        mine.append(first)
        theirs.append(cross(first))
        if distance < reach:
            second = step(second)
            mine.append(second)
            theirs.append(cross(second))
    pieces = pieces + mine + theirs

    rank = rank_of(pieces, shrink)
    work = [(gate_matrix, 0), (gate_matrix, 1), (up_matrix, 0), (up_matrix, 1)]
    products, after = [], rank
    bit = 1
    while bit < members or work:
        if work:
            matrix, part = work.pop(0)
            products.append(product(pieces, matrix, part, 2, after))
        if bit < members:
            after = cross(rank, bit)
            rank = jnp.concatenate([rank, after], axis=0)
            bit *= 2
    hidden = finish(products, rank, expand, span)

    slots = 2 * reach
    groups = [1] * slots + [1] + [2] * (reach - 1) + [1]
    outs = down(hidden, down_matrix, groups, rows)
    keep, give = outs[:slots], outs[slots:]
    came = [cross(x) for x in give]
    first = step(added(rows, (0, keep[0]), (0, came[0])))
    second = None
    for index in range(1, reach):
        more = [] if second is None else [(0, second)]
        second = step(added(rows, (0, keep[2 * index]), (rows, came[index]), *more))
        first = step(added(rows, (0, keep[2 * index - 1]), (0, came[index]), (0, first)))
    return last(members, block_token_count, [keep[-1], came[-1], first, cross(second)])


def solution(mesh):
    members = mesh.shape["tp"]
    return jax.shard_map(
        functools.partial(per_device, members),
        mesh=mesh,
        in_specs=(
            P(("rep", "tp"), None),
            P(None, "tp"),
            P(None, "tp"),
            P("tp", None),
            P("rep", None, "tp"),
            P("rep", None, "tp"),
            P("rep"),
            P("rep"),
        ),
        out_specs=P(("rep", "tp"), None),
        check_vma=False,
    )
```

```python
import functools

import jax
import jax.numpy as jnp
from jax import lax
from jax.experimental import pallas as pl
from jax.experimental.pallas import tpu as pltpu
from jax.sharding import PartitionSpec as P

F32 = jnp.float32
BF16 = jnp.bfloat16
VMEM_LIMIT = 20 * 1024 * 1024


def largest_tile(size, limit):
    tile = limit
    while size % tile:
        tile //= 2
    return tile


def params():
    return pltpu.CompilerParams(vmem_limit_bytes=VMEM_LIMIT)


def cost(flops, moved):
    return pl.CostEstimate(flops=flops, bytes_accessed=moved, transcendentals=0)


def ring_of(chips):
    return list(range(0, chips, 2)) + list(range(chips - 1, 0, -2))


def piece_row(device, members, rows, side, distance, half):
    chips = members // 2
    chip = device // 2
    place = jnp.where(chip % 2 == 0, chip // 2, chips - (chip + 1) // 2)
    spot = (place + chips + jnp.where(side == 0, distance, -distance)) % chips
    there = jnp.where(spot < chips // 2, 2 * spot, 2 * (chips - spot) - 1)
    return pl.multiple_of((2 * there + half) * rows, rows)


def arrivals(device, members, rows):
    core, reach = device % 2, members // 4
    places = [(core, 0, core), (core, 0, 1 - core)]
    for side in (core, 1 - core):
        for step in range(1, reach + 1):
            places.append((1 - side, step, side))
            if step < reach:
                places.append((1 - side, step, 1 - side))
    return [piece_row(device, members, rows, *place) for place in places]


def departures(device, members, rows):
    core, reach = device % 2, members // 4
    places = []
    for side in (core, 1 - core):
        places.append((side, reach, side))
        for step in range(reach - 1, 0, -1):
            places += [(side, step, side), (side, step, 1 - side)]
        places.append((side, 0, side))
    return [piece_row(device, members, rows, *place) for place in places]


def around(members):
    ring = ring_of(members // 2)
    size = len(ring)
    pairs = []
    for i in range(size):
        pairs.append((2 * ring[i], 2 * ring[(i + 1) % size]))
        pairs.append((2 * ring[i] + 1, 2 * ring[i - 1] + 1))
    return pairs


def crossing(members, bit):
    return [(i, i ^ bit) for i in range(members)]


def whole(count):
    return [pl.BlockSpec(memory_space=pltpu.VMEM)] * count


SCALARS = pl.BlockSpec(memory_space=pltpu.SMEM)
FAR = pl.BlockSpec(memory_space=pl.ANY)


def far(x):
    return pltpu.with_memory_space_constraint(x, pltpu.HBM)


def anchor_kernel(tokens_ref, passed_in, own_ref, passed_out, sem):
    copy = pltpu.make_async_copy(tokens_ref, own_ref, sem)
    copy.start()
    copy.wait()


def anchor(tokens, passed):
    return pl.pallas_call(
        anchor_kernel,
        in_specs=[FAR, FAR],
        out_specs=whole(1) + [FAR],
        out_shape=[jax.ShapeDtypeStruct(passed.shape, passed.dtype)] * 2,
        input_output_aliases={1: 1},
        scratch_shapes=[pltpu.SemaphoreType.DMA],
        compiler_params=params(),
        cost_estimate=cost(30_000_000_000, 0),
        name="anchor",
    )(far(tokens), passed)


def rank_kernel(blocks, ids_ref, shrink_ref, *refs):
    pieces, out_ref, scratch = refs[:-2], refs[-2], refs[-1]
    members = len(pieces)
    rows = pieces[0].shape[0]
    span = shrink_ref.shape[1]
    block_rows = members * rows // blocks
    places = arrivals(lax.axis_index("tp"), members, rows)
    lhs = jnp.concatenate([piece[...] for piece in pieces], axis=0)
    weights = jnp.concatenate([shrink_ref[ids_ref[b]] for b in range(blocks)], axis=0)
    found = lax.dot_general(
        lhs, weights, (((1,), (1,)), ((), ())), preferred_element_type=F32
    )
    for index, place in enumerate(places):
        part = found[index * rows : (index + 1) * rows]
        value = part[:, :span]
        for b in range(1, blocks):
            value = jnp.where(place // block_rows == b, part[:, b * span : (b + 1) * span], value)
        scratch[pl.ds(place, rows), :span] = value
    out_ref[...] = scratch[...].T[:span].astype(BF16)


def rank_of(adapters, pieces, shrink):
    rows, model = pieces[0].shape
    blocks, span = adapters.shape[0], shrink.shape[1]
    total = rows * len(pieces)
    return pl.pallas_call(
        functools.partial(rank_kernel, blocks),
        in_specs=[SCALARS] + whole(1 + len(pieces)),
        out_specs=whole(1)[0],
        out_shape=jax.ShapeDtypeStruct((span, total), BF16),
        scratch_shapes=[pltpu.VMEM((total, 128), F32)],
        compiler_params=params(),
        cost_estimate=cost(2 * total * model * span * blocks, 2 * total * model),
        name="rank",
    )(adapters, shrink, *pieces)


def product_kernel(first, w_ref, *refs):
    pieces, out_ref = refs[:-2], refs[-1]
    rows = pieces[0].shape[0]
    depth = w_ref.shape[0] // 2
    size = min(2048, depth)
    places = arrivals(lax.axis_index("tp"), len(pieces), rows)
    part = 0.0
    for start in range(first, first + depth, size):
        lhs = jnp.concatenate([piece[:, start : start + size] for piece in pieces], axis=0)
        part += jnp.dot(lhs, w_ref[start : start + size, :], preferred_element_type=F32)
    for index, place in enumerate(places):
        out_ref[pl.ds(place, rows), :] = part[index * rows : (index + 1) * rows]


def product(pieces, matrix, part, parts, after):
    rows, model = pieces[0].shape
    total = rows * len(pieces)
    width = matrix.shape[1]
    depth = model // parts
    return pl.pallas_call(
        functools.partial(product_kernel, part * depth),
        in_specs=whole(len(pieces) + 2),
        out_specs=whole(1)[0],
        out_shape=jax.ShapeDtypeStruct((total, width), F32),
        compiler_params=params(),
        cost_estimate=cost(2 * total * depth * width, 2 * depth * (width + total)),
        name="product",
    )(matrix, *pieces, after)


def finish_kernel(blocks, ids_ref, gate_a, gate_b, up_a, up_b, rank_ref, expand_ref, hidden_ref):
    ranks = rank_ref.shape[0]
    rank = rank_ref[...].astype(F32).T.astype(BF16)
    half = ranks // 2
    rows = hidden_ref.shape[0] // blocks
    for b in range(blocks):
        part = slice(b * rows, (b + 1) * rows)
        expand = expand_ref[ids_ref[b]]
        gate = jnp.dot(rank[part, :half], expand[:half], preferred_element_type=F32)
        up = jnp.dot(rank[part, half:], expand[half:], preferred_element_type=F32)
        gate += gate_a[part] + gate_b[part]
        up += up_a[part] + up_b[part]
        hidden_ref[part] = (gate / (1.0 + jnp.exp(-gate)) * up).astype(BF16)


def finish(adapters, products, rank, expand):
    total, width = products[0].shape
    return pl.pallas_call(
        functools.partial(finish_kernel, adapters.shape[0]),
        in_specs=[SCALARS] + whole(6),
        out_specs=whole(1)[0],
        out_shape=jax.ShapeDtypeStruct((total, width), BF16),
        compiler_params=params(),
        name="finish",
    )(adapters, *products, rank, expand)


def down_kernel(members, groups, rows, size, w_ref, hidden_ref, *refs):
    outs, product_ref = refs[:-1], refs[-1]
    places = departures(lax.axis_index("tp"), members, rows)
    hidden = hidden_ref[...]
    for start in range(0, w_ref.shape[1], size):
        columns = slice(start, start + size)
        part = jnp.dot(hidden, w_ref[:, columns], preferred_element_type=F32)
        product_ref[...] = part.astype(BF16)
        at = 0
        for out, group in zip(outs, groups, strict=True):
            for index in range(group):
                out[index * rows : (index + 1) * rows, columns] = product_ref[
                    pl.ds(places[at], rows), :
                ]
                at += 1


def down(hidden, down_matrix, groups, rows):
    total, depth = hidden.shape
    columns = down_matrix.shape[1]
    size = min(1024, columns)
    return pl.pallas_call(
        functools.partial(down_kernel, total // rows, groups, rows, size),
        in_specs=whole(2),
        out_specs=whole(len(groups)),
        out_shape=[jax.ShapeDtypeStruct((group * rows, columns), BF16) for group in groups],
        scratch_shapes=[pltpu.VMEM((total, size), BF16)],
        compiler_params=params(),
        cost_estimate=cost(
            2 * total * depth * columns, 2 * depth * columns + 2 * total * columns
        ),
        name="down",
    )(down_matrix, hidden)


def last_kernel(blocks, members, counts_ref, *refs):
    out_ref = refs[-1]
    rows = out_ref.shape[0]
    summed = refs[0][...].astype(F32)
    for ref in refs[1:-1]:
        summed += ref[...].astype(F32)
    first = lax.axis_index("tp") * rows
    block_rows = members * rows // blocks
    live = counts_ref[first // block_rows] - first % block_rows
    row = lax.broadcasted_iota(jnp.int32, summed.shape, 0)
    out_ref[...] = jnp.where(row < live, summed, 0.0).astype(BF16)


def last(members, counts, terms):
    return pl.pallas_call(
        functools.partial(last_kernel, counts.shape[0], members),
        in_specs=[SCALARS] + whole(len(terms)),
        out_specs=whole(1)[0],
        out_shape=jax.ShapeDtypeStruct(terms[0].shape, BF16),
        compiler_params=params(),
        name="last",
    )(counts, *terms)


def add_kernel(starts, *refs):
    out_ref = refs[-1]
    rows = out_ref.shape[0]
    total = 0.0
    for start, ref in zip(starts, refs[:-1], strict=True):
        total += ref[start : start + rows, :].astype(F32)
    out_ref[...] = total.astype(BF16)


def added(rows, *terms):
    starts = [start for start, _ in terms]
    columns = terms[0][1].shape[1]
    return pl.pallas_call(
        functools.partial(add_kernel, starts),
        in_specs=whole(len(terms)),
        out_specs=whole(1)[0],
        out_shape=jax.ShapeDtypeStruct((rows, columns), BF16),
        compiler_params=params(),
        cost_estimate=cost(len(terms) * rows * columns, 2 * rows * columns),
        name="added",
    )(*[term for _, term in terms])


def per_device(
    members,
    tokens,
    gate_matrix,
    up_matrix,
    down_matrix,
    shrink_matrices,
    expand_matrices,
    adapter_per_block,
    block_token_count,
):
    rows = tokens.shape[0]
    span = shrink_matrices.shape[2]
    reach = members // 4
    ring = around(members)

    def step(x):
        return lax.ppermute(x, "tp", ring)

    def cross(x, bit=1):
        return lax.ppermute(x, "tp", crossing(members, bit))

    first = tokens
    own, second = anchor(tokens, cross(tokens))
    pieces, mine, theirs = [own, second], [], []
    for distance in range(1, reach + 1):
        first = step(first)
        mine.append(first)
        theirs.append(cross(first))
        if distance < reach:
            second = step(second)
            mine.append(second)
            theirs.append(cross(second))
    pieces = pieces + mine + theirs

    rank = rank_of(adapter_per_block, pieces, jnp.swapaxes(shrink_matrices, 1, 2))
    everyone = lax.all_to_all(
        jnp.broadcast_to(rank[None], (members,) + rank.shape), "tp", 0, 0, tiled=True
    ).reshape(members * span, -1)
    products = [
        product(pieces, matrix, part, 2, rank)
        for matrix in (gate_matrix, up_matrix)
        for part in range(2)
    ]
    hidden = finish(adapter_per_block, products, everyone, expand_matrices)

    slots = 2 * reach
    groups = [1] * slots + [1] + [2] * (reach - 1) + [1]
    outs = down(hidden, down_matrix, groups, rows)
    keep, give = outs[:slots], outs[slots:]
    came = [cross(x) for x in give]
    first = step(added(rows, (0, keep[0]), (0, came[0])))
    second = None
    for index in range(1, reach):
        more = [] if second is None else [(0, second)]
        second = step(added(rows, (0, keep[2 * index]), (rows, came[index]), *more))
        first = step(added(rows, (0, keep[2 * index - 1]), (0, came[index]), (0, first)))
    return last(members, block_token_count, [keep[-1], came[-1], first, cross(second)])


def solution(mesh):
    members = mesh.shape["tp"]
    return jax.shard_map(
        functools.partial(per_device, members),
        mesh=mesh,
        in_specs=(
            P(("rep", "tp"), None),
            P(None, "tp"),
            P(None, "tp"),
            P("tp", None),
            P("rep", None, "tp"),
            P("rep", None, "tp"),
            P("rep"),
            P("rep"),
        ),
        out_specs=P(("rep", "tp"), None),
        check_vma=False,
    )
```

```python
import functools

import jax
import jax.numpy as jnp
from jax import lax
from jax.experimental import pallas as pl
from jax.experimental.pallas import tpu as pltpu
from jax.sharding import PartitionSpec as P

F32 = jnp.float32
BF16 = jnp.bfloat16
VMEM_LIMIT = 20 * 1024 * 1024


def largest_tile(size, limit):
    tile = limit
    while size % tile:
        tile //= 2
    return tile


def params():
    return pltpu.CompilerParams(vmem_limit_bytes=VMEM_LIMIT)


def cost(flops, moved):
    return pl.CostEstimate(flops=flops, bytes_accessed=moved, transcendentals=0)


def ring_of(chips):
    return list(range(0, chips, 2)) + list(range(chips - 1, 0, -2))


def piece_row(device, members, rows, side, distance, half):
    chips = members // 2
    chip = device // 2
    place = jnp.where(chip % 2 == 0, chip // 2, chips - (chip + 1) // 2)
    spot = (place + chips + jnp.where(side == 0, distance, -distance)) % chips
    there = jnp.where(spot < chips // 2, 2 * spot, 2 * (chips - spot) - 1)
    return pl.multiple_of((2 * there + half) * rows, rows)


def arrivals(device, members, rows):
    core, reach = device % 2, members // 4
    places = [(core, 0, core), (core, 0, 1 - core)]
    for side in (core, 1 - core):
        for step in range(1, reach + 1):
            places.append((1 - side, step, side))
            if step < reach:
                places.append((1 - side, step, 1 - side))
    return [piece_row(device, members, rows, *place) for place in places]


def departures(device, members, rows):
    core, reach = device % 2, members // 4
    places = []
    for side in (core, 1 - core):
        places.append((side, reach, side))
        for step in range(reach - 1, 0, -1):
            places += [(side, step, side), (side, step, 1 - side)]
        places.append((side, 0, side))
    return [piece_row(device, members, rows, *place) for place in places]


def around(members):
    ring = ring_of(members // 2)
    size = len(ring)
    pairs = []
    for i in range(size):
        pairs.append((2 * ring[i], 2 * ring[(i + 1) % size]))
        pairs.append((2 * ring[i] + 1, 2 * ring[i - 1] + 1))
    return pairs


def crossing(members, bit):
    return [(i, i ^ bit) for i in range(members)]


def whole(count):
    return [pl.BlockSpec(memory_space=pltpu.VMEM)] * count


FAR = pl.BlockSpec(memory_space=pl.ANY)


def far(x):
    return pltpu.with_memory_space_constraint(x, pltpu.HBM)


def picked(ref, index):
    row = ref[...]
    spots = lax.broadcasted_iota(jnp.int32, row.shape, 1)
    return jnp.sum(jnp.where(spots == index, row, 0))


def anchor_kernel(tokens_ref, passed_in, own_ref, passed_out, sem):
    copy = pltpu.make_async_copy(tokens_ref, own_ref, sem)
    copy.start()
    copy.wait()


def anchor(tokens, passed):
    return pl.pallas_call(
        anchor_kernel,
        in_specs=[FAR, FAR],
        out_specs=whole(1) + [FAR],
        out_shape=[jax.ShapeDtypeStruct(passed.shape, passed.dtype)] * 2,
        input_output_aliases={1: 1},
        scratch_shapes=[pltpu.SemaphoreType.DMA],
        compiler_params=params(),
        cost_estimate=cost(30_000_000_000, 0),
        name="anchor",
    )(far(tokens), passed)


def rank_kernel(blocks, ids_ref, shrink_ref, *refs):
    pieces, out_ref, scratch = refs[:-2], refs[-2], refs[-1]
    members = len(pieces)
    rows = pieces[0].shape[0]
    span = shrink_ref.shape[1]
    block_rows = members * rows // blocks
    places = arrivals(lax.axis_index("tp"), members, rows)
    lhs = jnp.concatenate([piece[...] for piece in pieces], axis=0)
    weights = jnp.concatenate([shrink_ref[picked(ids_ref, b)] for b in range(blocks)], axis=0)
    found = lax.dot_general(
        lhs, weights, (((1,), (1,)), ((), ())), preferred_element_type=F32
    )
    for index, place in enumerate(places):
        part = found[index * rows : (index + 1) * rows]
        value = part[:, :span]
        for b in range(1, blocks):
            value = jnp.where(place // block_rows == b, part[:, b * span : (b + 1) * span], value)
        scratch[pl.ds(place, rows), :span] = value
    out_ref[...] = scratch[...].T[:span].astype(BF16)


def rank_of(adapters, pieces, shrink):
    rows, model = pieces[0].shape
    blocks, span = adapters.shape[1], shrink.shape[1]
    total = rows * len(pieces)
    return pl.pallas_call(
        functools.partial(rank_kernel, blocks),
        in_specs=whole(2 + len(pieces)),
        out_specs=whole(1)[0],
        out_shape=jax.ShapeDtypeStruct((span, total), BF16),
        scratch_shapes=[pltpu.VMEM((total, 128), F32)],
        compiler_params=params(),
        cost_estimate=cost(2 * total * model * span * blocks, 2 * total * model),
        name="rank",
    )(adapters, shrink, *pieces)


def product_kernel(first, w_ref, *refs):
    pieces, out_ref = refs[:-2], refs[-1]
    rows = pieces[0].shape[0]
    depth = w_ref.shape[0] // 2
    size = min(2048, depth)
    places = arrivals(lax.axis_index("tp"), len(pieces), rows)
    part = 0.0
    for start in range(first, first + depth, size):
        lhs = jnp.concatenate([piece[:, start : start + size] for piece in pieces], axis=0)
        part += jnp.dot(lhs, w_ref[start : start + size, :], preferred_element_type=F32)
    for index, place in enumerate(places):
        out_ref[pl.ds(place, rows), :] = part[index * rows : (index + 1) * rows]


def product(pieces, matrix, part, parts, after):
    rows, model = pieces[0].shape
    total = rows * len(pieces)
    width = matrix.shape[1]
    depth = model // parts
    return pl.pallas_call(
        functools.partial(product_kernel, part * depth),
        in_specs=whole(len(pieces) + 2),
        out_specs=whole(1)[0],
        out_shape=jax.ShapeDtypeStruct((total, width), F32),
        compiler_params=params(),
        cost_estimate=cost(2 * total * depth * width, 2 * depth * (width + total)),
        name="product",
    )(matrix, *pieces, after)


def finish_kernel(blocks, span, ids_ref, gate_a, gate_b, up_a, up_b, rank_ref, expand_ref, hidden_ref):
    ranks = rank_ref.shape[0]
    device = lax.axis_index("tp")
    shape = (ranks, ranks)
    want = lax.broadcasted_iota(jnp.int32, shape, 0)
    have = lax.broadcasted_iota(jnp.int32, shape, 1)
    origin = ((have // span) ^ device) * span + have % span
    order = jnp.where(want == origin, 1.0, 0.0).astype(BF16)
    rank = jnp.dot(order, rank_ref[...], preferred_element_type=F32).T.astype(BF16)
    half = ranks // 2
    rows = hidden_ref.shape[0] // blocks
    for b in range(blocks):
        part = slice(b * rows, (b + 1) * rows)
        expand = expand_ref[picked(ids_ref, b)]
        gate = jnp.dot(rank[part, :half], expand[:half], preferred_element_type=F32)
        up = jnp.dot(rank[part, half:], expand[half:], preferred_element_type=F32)
        gate += gate_a[part] + gate_b[part]
        up += up_a[part] + up_b[part]
        hidden_ref[part] = (gate / (1.0 + jnp.exp(-gate)) * up).astype(BF16)


def finish(adapters, products, rank, expand, span):
    total, width = products[0].shape
    return pl.pallas_call(
        functools.partial(finish_kernel, adapters.shape[1], span),
        in_specs=whole(7),
        out_specs=whole(1)[0],
        out_shape=jax.ShapeDtypeStruct((total, width), BF16),
        compiler_params=params(),
        name="finish",
    )(adapters, *products, rank, expand)


def down_kernel(members, groups, rows, first, size, w_ref, hidden_ref, *refs):
    outs, product_ref = refs[:-1], refs[-1]
    places = departures(lax.axis_index("tp"), members, rows)
    hidden = hidden_ref[...]
    for start in range(0, outs[0].shape[1], size):
        columns = slice(start, start + size)
        weights = w_ref[:, first + start : first + start + size]
        part = jnp.dot(hidden, weights, preferred_element_type=F32)
        product_ref[...] = part.astype(BF16)
        at = 0
        for out, group in zip(outs, groups, strict=True):
            for index in range(group):
                out[index * rows : (index + 1) * rows, columns] = product_ref[
                    pl.ds(places[at], rows), :
                ]
                at += 1


def down(hidden, down_matrix, groups, rows, part, parts):
    total, depth = hidden.shape
    columns = down_matrix.shape[1] // parts
    size = min(1024, columns)
    return pl.pallas_call(
        functools.partial(down_kernel, total // rows, groups, rows, part * columns, size),
        in_specs=whole(2),
        out_specs=whole(len(groups)),
        out_shape=[jax.ShapeDtypeStruct((group * rows, columns), BF16) for group in groups],
        scratch_shapes=[pltpu.VMEM((total, size), BF16)],
        compiler_params=params(),
        cost_estimate=cost(
            2 * total * depth * columns, 2 * depth * columns + 2 * total * columns
        ),
        name="down",
    )(down_matrix, hidden)


def last_kernel(blocks, members, parts, counts_ref, *refs):
    terms, out_ref = refs[:-1], refs[-1]
    rows = out_ref.shape[0]
    first = lax.axis_index("tp") * rows
    block_rows = members * rows // blocks
    live = picked(counts_ref, first // block_rows) - first % block_rows
    each = len(terms) // parts
    columns = out_ref.shape[1] // parts
    for part in range(parts):
        summed = 0.0
        for term in terms[part * each : (part + 1) * each]:
            summed += term[...].astype(F32)
        row = lax.broadcasted_iota(jnp.int32, summed.shape, 0)
        out_ref[:, part * columns : (part + 1) * columns] = jnp.where(
            row < live, summed, 0.0
        ).astype(BF16)


def last(members, counts, halves):
    terms = [term for half in halves for term in half]
    rows, columns = terms[0].shape
    return pl.pallas_call(
        functools.partial(last_kernel, counts.shape[1], members, len(halves)),
        in_specs=whole(1 + len(terms)),
        out_specs=whole(1)[0],
        out_shape=jax.ShapeDtypeStruct((rows, columns * len(halves)), BF16),
        compiler_params=params(),
        name="last",
    )(counts, *terms)


def add_kernel(starts, *refs):
    out_ref = refs[-1]
    rows = out_ref.shape[0]
    total = 0.0
    for start, ref in zip(starts, refs[:-1], strict=True):
        total += ref[start : start + rows, :].astype(F32)
    out_ref[...] = total.astype(BF16)


def added(rows, *terms):
    starts = [start for start, _ in terms]
    columns = terms[0][1].shape[1]
    return pl.pallas_call(
        functools.partial(add_kernel, starts),
        in_specs=whole(len(terms)),
        out_specs=whole(1)[0],
        out_shape=jax.ShapeDtypeStruct((rows, columns), BF16),
        compiler_params=params(),
        cost_estimate=cost(len(terms) * rows * columns, 2 * rows * columns),
        name="added",
    )(*[term for _, term in terms])


def per_device(
    members,
    tokens,
    gate_matrix,
    up_matrix,
    down_matrix,
    shrink_matrices,
    expand_matrices,
    adapter_per_block,
    block_token_count,
):
    rows = tokens.shape[0]
    span = shrink_matrices.shape[2]
    reach = members // 4
    ring = around(members)

    def step(x):
        return lax.ppermute(x, "tp", ring)

    def cross(x, bit=1):
        return lax.ppermute(x, "tp", crossing(members, bit))

    first = tokens
    own, second = anchor(tokens, cross(tokens))
    pieces, mine, theirs = [own, second], [], []
    for distance in range(1, reach + 1):
        first = step(first)
        mine.append(first)
        theirs.append(cross(first))
        if distance < reach:
            second = step(second)
            mine.append(second)
            theirs.append(cross(second))
    pieces = pieces + mine + theirs

    adapters, counts = adapter_per_block[None], block_token_count[None]
    rank = rank_of(adapters, pieces, jnp.swapaxes(shrink_matrices, 1, 2))
    work = [(gate_matrix, 0), (gate_matrix, 1), (up_matrix, 0), (up_matrix, 1)]
    products, after = [], rank
    bit = 1
    while bit < members or work:
        if work:
            matrix, part = work.pop(0)
            products.append(product(pieces, matrix, part, 2, after))
        if bit < members:
            after = cross(rank, bit)
            rank = jnp.concatenate([rank, after], axis=0)
            bit *= 2
    hidden = finish(adapters, products, rank, expand_matrices, span)

    slots = 2 * reach
    groups = [1] * slots + [1] + [2] * (reach - 1) + [1]
    halves = []
    for part in range(2):
        outs = down(hidden, down_matrix, groups, rows, part, 2)
        keep, give = outs[:slots], outs[slots:]
        came = [cross(x) for x in give]
        first = step(added(rows, (0, keep[0]), (0, came[0])))
        second = None
        for index in range(1, reach):
            more = [] if second is None else [(0, second)]
            second = step(added(rows, (0, keep[2 * index]), (rows, came[index]), *more))
            first = step(added(rows, (0, keep[2 * index - 1]), (0, came[index]), (0, first)))
        halves.append([keep[-1], came[-1], first, cross(second)])
    return last(members, counts, halves)


def solution(mesh):
    members = mesh.shape["tp"]
    return jax.shard_map(
        functools.partial(per_device, members),
        mesh=mesh,
        in_specs=(
            P(("rep", "tp"), None),
            P(None, "tp"),
            P(None, "tp"),
            P("tp", None),
            P("rep", None, "tp"),
            P("rep", None, "tp"),
            P("rep"),
            P("rep"),
        ),
        out_specs=P(("rep", "tp"), None),
        check_vma=False,
    )
```

```python
import functools

import jax
import jax.numpy as jnp
from jax import lax
from jax.experimental import pallas as pl
from jax.experimental.pallas import tpu as pltpu
from jax.sharding import PartitionSpec as P

F32 = jnp.float32
BF16 = jnp.bfloat16
VMEM_LIMIT = 17 * 1024 * 1024


def largest_tile(size, limit):
    tile = limit
    while size % tile:
        tile //= 2
    return tile


def params():
    return pltpu.CompilerParams(vmem_limit_bytes=VMEM_LIMIT)


def cost(flops, moved):
    return pl.CostEstimate(flops=flops, bytes_accessed=moved, transcendentals=0)


def ring_of(chips):
    return list(range(0, chips, 2)) + list(range(chips - 1, 0, -2))


def piece_row(device, members, rows, side, distance, half):
    chips = members // 2
    chip = device // 2
    place = jnp.where(chip % 2 == 0, chip // 2, chips - (chip + 1) // 2)
    spot = (place + chips + jnp.where(side == 0, distance, -distance)) % chips
    there = jnp.where(spot < chips // 2, 2 * spot, 2 * (chips - spot) - 1)
    return pl.multiple_of((2 * there + half) * rows, rows)


def arrivals(device, members, rows):
    core, reach = device % 2, members // 4
    places = [(core, 0, core), (core, 0, 1 - core)]
    for side in (core, 1 - core):
        for step in range(1, reach + 1):
            places.append((1 - side, step, side))
            if step < reach:
                places.append((1 - side, step, 1 - side))
    return [piece_row(device, members, rows, *place) for place in places]


def departures(device, members, rows):
    core, reach = device % 2, members // 4
    places = []
    for side in (core, 1 - core):
        places.append((side, reach, side))
        for step in range(reach - 1, 0, -1):
            places += [(side, step, side), (side, step, 1 - side)]
        places.append((side, 0, side))
    return [piece_row(device, members, rows, *place) for place in places]


def around(members):
    ring = ring_of(members // 2)
    size = len(ring)
    pairs = []
    for i in range(size):
        pairs.append((2 * ring[i], 2 * ring[(i + 1) % size]))
        pairs.append((2 * ring[i] + 1, 2 * ring[i - 1] + 1))
    return pairs


def crossing(members, bit):
    return [(i, i ^ bit) for i in range(members)]


def whole(count):
    return [pl.BlockSpec(memory_space=pltpu.VMEM)] * count


FAR = pl.BlockSpec(memory_space=pl.ANY)


def far(x):
    return pltpu.with_memory_space_constraint(x, pltpu.HBM)


def picked(ref, index):
    row = ref[...]
    spots = lax.broadcasted_iota(jnp.int32, row.shape, 1)
    return jnp.sum(jnp.where(spots == index, row, 0))


def anchor_kernel(ids_ref, tokens_ref, shrink_ref, passed_in, own_ref, chosen_ref, passed_out, sems):
    blocks = ids_ref.shape[1]
    copies = [pltpu.make_async_copy(tokens_ref, own_ref, sems.at[blocks])]
    for b in range(blocks):
        source = shrink_ref.at[picked(ids_ref, b)]
        copies.append(pltpu.make_async_copy(source, chosen_ref.at[b], sems.at[b]))
    for copy in copies:
        copy.start()
    for copy in copies:
        copy.wait()


def anchor(adapters, tokens, shrink, passed):
    blocks = adapters.shape[1]
    return pl.pallas_call(
        anchor_kernel,
        in_specs=whole(1) + [FAR] * 3,
        out_specs=whole(2) + [FAR],
        out_shape=[
            jax.ShapeDtypeStruct(tokens.shape, BF16),
            jax.ShapeDtypeStruct((blocks,) + shrink.shape[1:], BF16),
            jax.ShapeDtypeStruct(passed.shape, BF16),
        ],
        input_output_aliases={3: 2},
        scratch_shapes=[pltpu.SemaphoreType.DMA((blocks + 1,))],
        compiler_params=params(),
        cost_estimate=cost(30_000_000_000, 0),
        name="anchor",
    )(adapters, far(tokens), far(shrink), passed)


def tie_kernel(x_ref, after_ref, out_ref):
    del x_ref, after_ref, out_ref


def tie(x, after):
    return pl.pallas_call(
        tie_kernel,
        in_specs=[FAR, FAR],
        out_specs=FAR,
        out_shape=jax.ShapeDtypeStruct(x.shape, x.dtype),
        input_output_aliases={0: 0},
        compiler_params=params(),
        name="tie",
    )(x, after)


def rank_kernel(members, numbers, ids_ref, expand_ref, own_ref, other_ref, *refs):
    pieces, (out_ref, chosen_ref, scratch, sems) = refs[: len(numbers)], refs[-4:]
    rows = pieces[0].shape[0]
    blocks, span = ids_ref.shape[1], own_ref.shape[1]
    block_rows = members * rows // blocks
    device = lax.axis_index("tp")
    places = arrivals(device, members, rows)
    lhs = jnp.concatenate([piece[...] for piece in pieces], axis=0)
    ids = [picked(ids_ref, b) for b in range(blocks)]
    copies = [
        pltpu.make_async_copy(expand_ref.at[ids[b]], chosen_ref.at[b], sems.at[b])
        for b in range(blocks)
    ]
    for copy in copies:
        copy.start()
    weights = jnp.concatenate([ref[b] for ref in (own_ref, other_ref) for b in range(blocks)], axis=0)
    found = lax.dot_general(
        lhs, weights, (((1,), (1,)), ((), ())), preferred_element_type=F32
    )
    scratch[...] = jnp.zeros_like(scratch)
    for index, number in enumerate(numbers):
        part = found[index * rows : (index + 1) * rows]
        for source in range(2):
            first = source * blocks * span
            value = part[:, first : first + span]
            for b in range(1, blocks):
                columns = part[:, first + b * span : first + (b + 1) * span]
                value = jnp.where(places[number] // block_rows == b, columns, value)
            scratch[source, pl.ds(places[number], rows), :span] = value
    own, other = scratch[0].T[:span], scratch[1].T[:span]
    lower = device % 2 == 0
    out_ref[...] = jnp.concatenate(
        [jnp.where(lower, own, other), jnp.where(lower, other, own)], axis=0
    ).astype(BF16)
    for copy in copies:
        copy.wait()


def rank_of(adapters, members, numbers, pieces, shrink, other, expand, after):
    rows, model = pieces[0].shape
    span = shrink.shape[1]
    total = rows * members
    return pl.pallas_call(
        functools.partial(rank_kernel, members, numbers),
        in_specs=whole(1) + [FAR] + whole(2 + len(pieces)) + [FAR] * len(after),
        out_specs=whole(2),
        out_shape=[
            jax.ShapeDtypeStruct((2 * span, total), BF16),
            jax.ShapeDtypeStruct((adapters.shape[1],) + expand.shape[1:], BF16),
        ],
        scratch_shapes=[
            pltpu.VMEM((2, total, 128), F32),
            pltpu.SemaphoreType.DMA((adapters.shape[1],)),
        ],
        compiler_params=params(),
        cost_estimate=cost(2 * total * model * span * 2, 2 * total * model),
        name="rank",
    )(adapters, far(expand), shrink, other, *pieces, *after)


def product_kernel(first, w_ref, *refs):
    pieces, out_ref = refs[:-2], refs[-1]
    rows = pieces[0].shape[0]
    depth = w_ref.shape[0] // 2
    size = min(2048, depth)
    places = arrivals(lax.axis_index("tp"), len(pieces), rows)
    part = 0.0
    for start in range(first, first + depth, size):
        lhs = jnp.concatenate([piece[:, start : start + size] for piece in pieces], axis=0)
        part += jnp.dot(lhs, w_ref[start : start + size, :], preferred_element_type=F32)
    for index, place in enumerate(places):
        out_ref[pl.ds(place, rows), :] = part[index * rows : (index + 1) * rows]


def product(pieces, matrix, part, parts, after):
    rows, model = pieces[0].shape
    total = rows * len(pieces)
    width = matrix.shape[1]
    depth = model // parts
    return pl.pallas_call(
        functools.partial(product_kernel, part * depth),
        in_specs=whole(len(pieces) + 2),
        out_specs=whole(1)[0],
        out_shape=jax.ShapeDtypeStruct((total, width), F32),
        compiler_params=params(),
        cost_estimate=cost(2 * total * depth * width, 2 * depth * (width + total)),
        name="product",
    )(matrix, *pieces, after)


def finish_kernel(span, gate_a, gate_b, up_a, up_b, rank_ref, expand_ref, hidden_ref):
    ranks = rank_ref.shape[0]
    chip = lax.axis_index("tp") // 2
    shape = (ranks, ranks)
    want = lax.broadcasted_iota(jnp.int32, shape, 0)
    have = lax.broadcasted_iota(jnp.int32, shape, 1)
    origin = ((have // span) ^ chip) * span + have % span
    order = jnp.where(want == origin, 1.0, 0.0).astype(BF16)
    rank = jnp.dot(order, rank_ref[...], preferred_element_type=F32).T.astype(BF16)
    half = ranks // 2
    blocks = expand_ref.shape[0]
    rows = hidden_ref.shape[0] // blocks
    for b in range(blocks):
        part = slice(b * rows, (b + 1) * rows)
        expand = expand_ref[b]
        gate = jnp.dot(rank[part, :half], expand[:half], preferred_element_type=F32)
        up = jnp.dot(rank[part, half:], expand[half:], preferred_element_type=F32)
        gate += gate_a[part] + gate_b[part]
        up += up_a[part] + up_b[part]
        hidden_ref[part] = (gate / (1.0 + jnp.exp(-gate)) * up).astype(BF16)


def finish(products, rank, expand, span):
    total, width = products[0].shape
    return pl.pallas_call(
        functools.partial(finish_kernel, span),
        in_specs=whole(6),
        out_specs=whole(1)[0],
        out_shape=jax.ShapeDtypeStruct((total, width), BF16),
        compiler_params=params(),
        cost_estimate=cost(6_000_000_000, 0),
        name="finish",
    )(*products, rank, expand)


def down_kernel(members, groups, rows, size, w_ref, hidden_ref, *refs):
    outs, product_ref = refs[:-1], refs[-1]
    places = departures(lax.axis_index("tp"), members, rows)
    hidden = hidden_ref[...]
    for start in range(0, w_ref.shape[1], size):
        columns = slice(start, start + size)
        part = jnp.dot(hidden, w_ref[:, columns], preferred_element_type=F32)
        product_ref[...] = part.astype(BF16)
        at = 0
        for out, group in zip(outs, groups, strict=True):
            for index in range(group):
                out[index * rows : (index + 1) * rows, columns] = product_ref[
                    pl.ds(places[at], rows), :
                ]
                at += 1


def down(hidden, down_matrix, groups, rows):
    total, depth = hidden.shape
    columns = down_matrix.shape[1]
    size = min(1024, columns)
    return pl.pallas_call(
        functools.partial(down_kernel, total // rows, groups, rows, size),
        in_specs=whole(2),
        out_specs=whole(len(groups)),
        out_shape=[jax.ShapeDtypeStruct((group * rows, columns), BF16) for group in groups],
        scratch_shapes=[pltpu.VMEM((total, size), BF16)],
        compiler_params=params(),
        cost_estimate=cost(
            2 * total * depth * columns, 2 * depth * columns + 2 * total * columns
        ),
        name="down",
    )(down_matrix, hidden)


def last_kernel(blocks, members, parts, counts_ref, *refs):
    terms, out_ref = refs[:-1], refs[-1]
    rows = out_ref.shape[0]
    first = lax.axis_index("tp") * rows
    block_rows = members * rows // blocks
    live = picked(counts_ref, first // block_rows) - first % block_rows
    each = len(terms) // parts
    columns = out_ref.shape[1] // parts
    for part in range(parts):
        summed = 0.0
        for term in terms[part * each : (part + 1) * each]:
            summed += term[...].astype(F32)
        row = lax.broadcasted_iota(jnp.int32, summed.shape, 0)
        out_ref[:, part * columns : (part + 1) * columns] = jnp.where(
            row < live, summed, 0.0
        ).astype(BF16)


def last(members, counts, halves):
    terms = [term for half in halves for term in half]
    rows, columns = terms[0].shape
    return pl.pallas_call(
        functools.partial(last_kernel, counts.shape[1], members, len(halves)),
        in_specs=whole(1 + len(terms)),
        out_specs=whole(1)[0],
        out_shape=jax.ShapeDtypeStruct((rows, columns * len(halves)), BF16),
        compiler_params=params(),
        name="last",
    )(counts, *terms)


def add_kernel(starts, *refs):
    out_ref = refs[-1]
    rows = out_ref.shape[0]
    total = 0.0
    for start, ref in zip(starts, refs[:-1], strict=True):
        total += ref[start : start + rows, :].astype(F32)
    out_ref[...] = total.astype(BF16)


def added(rows, *terms):
    starts = [start for start, _ in terms]
    columns = terms[0][1].shape[1]
    return pl.pallas_call(
        functools.partial(add_kernel, starts),
        in_specs=whole(len(terms)),
        out_specs=whole(1)[0],
        out_shape=jax.ShapeDtypeStruct((rows, columns), BF16),
        compiler_params=params(),
        cost_estimate=cost(len(terms) * rows * columns, 2 * rows * columns),
        name="added",
    )(*[term for _, term in terms])


def per_device(
    members,
    tokens,
    gate_matrix,
    up_matrix,
    down_matrix,
    shrink_matrices,
    expand_matrices,
    adapter_per_block,
    block_token_count,
):
    rows = tokens.shape[0]
    span = shrink_matrices.shape[2]
    reach = members // 4
    ring = around(members)

    def step(x):
        return lax.ppermute(x, "tp", ring)

    def cross(x, bit=1):
        return lax.ppermute(x, "tp", crossing(members, bit))

    first = tokens
    adapters, counts = adapter_per_block[None], block_token_count[None]
    own, shrink, second = anchor(
        adapters, tokens, jnp.swapaxes(shrink_matrices, 1, 2), cross(tokens)
    )
    other_shrink = cross(shrink)
    pieces, mine, theirs = [own, second], [], []
    for distance in range(1, reach + 1):
        first = step(first)
        mine.append(first)
        theirs.append(cross(first))
        if distance < reach:
            second = step(second)
            mine.append(second)
            theirs.append(cross(second))
    pieces = pieces + mine + theirs

    received = [0] + list(range(2, 2 + len(mine)))
    rank, expand = rank_of(
        adapters,
        members,
        received,
        [pieces[i] for i in received],
        shrink,
        other_shrink,
        expand_matrices,
        theirs[:-1],
    )
    work = [(gate_matrix, 0), (gate_matrix, 1), (up_matrix, 0), (up_matrix, 1)]
    products, after, bit = [], rank, 1
    while bit < members or work:
        if work:
            matrix, part = work.pop(0)
            products.append(product(pieces, matrix, part, 2, after))
        if bit < members:
            after = cross(rank, bit)
            rank = rank + after if bit == 1 else jnp.concatenate([rank, after], axis=0)
            bit *= 2
    hidden = finish(products, rank, expand, 2 * span)

    slots = 2 * reach
    groups = [1] * slots + [1] + [2] * (reach - 1) + [1]
    outs = down(hidden, down_matrix, groups, rows)
    keep, give = outs[:slots], outs[slots:]
    came = [cross(give[0])]
    came += [cross(tie(x, came[0])) for x in give[1:]]
    first = step(added(rows, (0, keep[0]), (0, came[0])))
    second = None
    for index in range(1, reach):
        more = [] if second is None else [(0, second)]
        second = step(added(rows, (0, keep[2 * index]), (rows, came[index]), *more))
        first = step(added(rows, (0, keep[2 * index - 1]), (0, came[index]), (0, first)))
    return last(members, counts, [[keep[-1], came[-1], first, cross(second)]])


def solution(mesh):
    members = mesh.shape["tp"]
    return jax.shard_map(
        functools.partial(per_device, members),
        mesh=mesh,
        in_specs=(
            P(("rep", "tp"), None),
            P(None, "tp"),
            P(None, "tp"),
            P("tp", None),
            P("rep", None, "tp"),
            P("rep", None, "tp"),
            P("rep"),
            P("rep"),
        ),
        out_specs=P(("rep", "tp"), None),
        check_vma=False,
    )
```

```python
import functools

import jax
import jax.numpy as jnp
from jax import lax
from jax.experimental import pallas as pl
from jax.experimental.pallas import tpu as pltpu
from jax.sharding import PartitionSpec as P

F32 = jnp.float32
BF16 = jnp.bfloat16
VMEM_LIMIT = 20 * 1024 * 1024
WEIGHTS = (2, 2, 6, 6)


def largest_tile(size, limit):
    tile = limit
    while size % tile:
        tile //= 2
    return tile


def params():
    return pltpu.CompilerParams(vmem_limit_bytes=VMEM_LIMIT)


def cost(flops, moved):
    return pl.CostEstimate(flops=flops, bytes_accessed=moved, transcendentals=0)


def ring_of(chips):
    return list(range(0, chips, 2)) + list(range(chips - 1, 0, -2))


def piece_row(device, members, rows, side, distance, half):
    chips = members // 2
    chip = device // 2
    place = jnp.where(chip % 2 == 0, chip // 2, chips - (chip + 1) // 2)
    spot = (place + chips + jnp.where(side == 0, distance, -distance)) % chips
    there = jnp.where(spot < chips // 2, 2 * spot, 2 * (chips - spot) - 1)
    return pl.multiple_of((2 * there + half) * rows, rows)


def arrivals(device, members, rows):
    core, reach = device % 2, members // 4
    places = [(core, 0, core), (core, 0, 1 - core)]
    for side in (core, 1 - core):
        for step in range(1, reach + 1):
            places.append((1 - side, step, side))
            if step < reach:
                places.append((1 - side, step, 1 - side))
    return [piece_row(device, members, rows, *place) for place in places]


def departures(device, members, rows):
    core, reach = device % 2, members // 4
    places = []
    for side in (core, 1 - core):
        places.append((side, reach, side))
        for step in range(reach - 1, 0, -1):
            places += [(side, step, side), (side, step, 1 - side)]
        places.append((side, 0, side))
    return [piece_row(device, members, rows, *place) for place in places]


def around(members):
    ring = ring_of(members // 2)
    size = len(ring)
    pairs = []
    for i in range(size):
        pairs.append((2 * ring[i], 2 * ring[(i + 1) % size]))
        pairs.append((2 * ring[i] + 1, 2 * ring[i - 1] + 1))
    return pairs


def crossing(members, bit):
    return [(i, i ^ bit) for i in range(members)]


def whole(count):
    return [pl.BlockSpec(memory_space=pltpu.VMEM)] * count


FAR = pl.BlockSpec(memory_space=pl.ANY)


def far(x):
    return pltpu.with_memory_space_constraint(x, pltpu.HBM)


def picked(ref, index):
    row = ref[...]
    spots = lax.broadcasted_iota(jnp.int32, row.shape, 1)
    return jnp.sum(jnp.where(spots == index, row, 0))


def anchor_kernel(tokens_ref, passed_in, own_ref, passed_out, sem):
    copy = pltpu.make_async_copy(tokens_ref, own_ref, sem)
    copy.start()
    copy.wait()


def anchor(tokens, passed):
    return pl.pallas_call(
        anchor_kernel,
        in_specs=[FAR, FAR],
        out_specs=whole(1) + [FAR],
        out_shape=[jax.ShapeDtypeStruct(passed.shape, passed.dtype)] * 2,
        input_output_aliases={1: 1},
        scratch_shapes=[pltpu.SemaphoreType.DMA],
        compiler_params=params(),
        cost_estimate=cost(30_000_000_000, 0),
        name="anchor",
    )(far(tokens), passed)


def rank_kernel(members, numbers, ids_ref, expand_ref, own_ref, other_ref, *refs):
    pieces, (out_ref, chosen_ref, scratch, sems) = refs[: len(numbers)], refs[-4:]
    rows = pieces[0].shape[0]
    blocks, span = ids_ref.shape[1], own_ref.shape[1]
    block_rows = members * rows // blocks
    device = lax.axis_index("tp")
    places = arrivals(device, members, rows)
    lhs = jnp.concatenate([piece[...] for piece in pieces], axis=0)
    ids = [picked(ids_ref, b) for b in range(blocks)]
    copies = [
        pltpu.make_async_copy(expand_ref.at[ids[b]], chosen_ref.at[b], sems.at[b])
        for b in range(blocks)
    ]
    for copy in copies:
        copy.start()
    weights = jnp.concatenate([ref[i] for ref in (own_ref, other_ref) for i in ids], axis=0)
    found = lax.dot_general(
        lhs, weights, (((1,), (1,)), ((), ())), preferred_element_type=F32
    )
    scratch[...] = jnp.zeros_like(scratch)
    for index, number in enumerate(numbers):
        part = found[index * rows : (index + 1) * rows]
        for source in range(2):
            first = source * blocks * span
            value = part[:, first : first + span]
            for b in range(1, blocks):
                columns = part[:, first + b * span : first + (b + 1) * span]
                value = jnp.where(places[number] // block_rows == b, columns, value)
            scratch[source, pl.ds(places[number], rows), :span] = value
    own, other = scratch[0].T[:span], scratch[1].T[:span]
    lower = device % 2 == 0
    out_ref[...] = jnp.concatenate(
        [jnp.where(lower, own, other), jnp.where(lower, other, own)], axis=0
    ).astype(BF16)
    for copy in copies:
        copy.wait()


def rank_of(adapters, members, numbers, pieces, shrink, other, expand, after):
    rows, model = pieces[0].shape
    span = shrink.shape[1]
    total = rows * members
    return pl.pallas_call(
        functools.partial(rank_kernel, members, numbers),
        in_specs=whole(1) + [FAR] + whole(2 + len(pieces)) + [FAR] * len(after),
        out_specs=whole(2),
        out_shape=[
            jax.ShapeDtypeStruct((2 * span, total), BF16),
            jax.ShapeDtypeStruct((adapters.shape[1],) + expand.shape[1:], BF16),
        ],
        scratch_shapes=[
            pltpu.VMEM((2, total, 128), F32),
            pltpu.SemaphoreType.DMA((adapters.shape[1],)),
        ],
        compiler_params=params(),
        cost_estimate=cost(2 * total * model * span * 2, 2 * total * model),
        name="rank",
    )(adapters, far(expand), shrink, other, *pieces, *after)


def product_kernel(first, w_ref, *refs):
    pieces, out_ref = refs[:-2], refs[-1]
    rows = pieces[0].shape[0]
    depth = w_ref.shape[0] // 2
    size = min(2048, depth)
    places = arrivals(lax.axis_index("tp"), len(pieces), rows)
    part = 0.0
    for start in range(first, first + depth, size):
        lhs = jnp.concatenate([piece[:, start : start + size] for piece in pieces], axis=0)
        part += jnp.dot(lhs, w_ref[start : start + size, :], preferred_element_type=F32)
    for index, place in enumerate(places):
        out_ref[pl.ds(place, rows), :] = part[index * rows : (index + 1) * rows]


def product(pieces, matrix, part, parts, after, weight):
    rows, model = pieces[0].shape
    total = rows * len(pieces)
    width = matrix.shape[1]
    depth = model // parts
    return pl.pallas_call(
        functools.partial(product_kernel, part * depth),
        in_specs=whole(len(pieces) + 2),
        out_specs=whole(1)[0],
        out_shape=jax.ShapeDtypeStruct((total, width), F32),
        compiler_params=params(),
        cost_estimate=cost(weight * total * depth * width, 2 * depth * (width + total)),
        name="product",
    )(matrix, *pieces, after)


def finish_kernel(span, gate_a, gate_b, up_a, up_b, rank_ref, expand_ref, hidden_ref):
    ranks = rank_ref.shape[0]
    chip = lax.axis_index("tp") // 2
    shape = (ranks, ranks)
    want = lax.broadcasted_iota(jnp.int32, shape, 0)
    have = lax.broadcasted_iota(jnp.int32, shape, 1)
    origin = ((have // span) ^ chip) * span + have % span
    order = jnp.where(want == origin, 1.0, 0.0).astype(BF16)
    rank = jnp.dot(order, rank_ref[...], preferred_element_type=F32).T.astype(BF16)
    half = ranks // 2
    blocks = expand_ref.shape[0]
    rows = hidden_ref.shape[0] // blocks
    for b in range(blocks):
        part = slice(b * rows, (b + 1) * rows)
        expand = expand_ref[b]
        gate = jnp.dot(rank[part, :half], expand[:half], preferred_element_type=F32)
        up = jnp.dot(rank[part, half:], expand[half:], preferred_element_type=F32)
        gate += gate_a[part] + gate_b[part]
        up += up_a[part] + up_b[part]
        hidden_ref[part] = (gate / (1.0 + jnp.exp(-gate)) * up).astype(BF16)


def finish(products, rank, expand, span):
    total, width = products[0].shape
    return pl.pallas_call(
        functools.partial(finish_kernel, span),
        in_specs=whole(6),
        out_specs=whole(1)[0],
        out_shape=jax.ShapeDtypeStruct((total, width), BF16),
        compiler_params=params(),
        name="finish",
    )(*products, rank, expand)


def down_kernel(members, groups, rows, size, w_ref, hidden_ref, *refs):
    outs, product_ref = refs[:-1], refs[-1]
    places = departures(lax.axis_index("tp"), members, rows)
    hidden = hidden_ref[...]
    for start in range(0, w_ref.shape[1], size):
        columns = slice(start, start + size)
        part = jnp.dot(hidden, w_ref[:, columns], preferred_element_type=F32)
        product_ref[...] = part.astype(BF16)
        at = 0
        for out, group in zip(outs, groups, strict=True):
            for index in range(group):
                out[index * rows : (index + 1) * rows, columns] = product_ref[
                    pl.ds(places[at], rows), :
                ]
                at += 1


def down(hidden, down_matrix, groups, rows):
    total, depth = hidden.shape
    columns = down_matrix.shape[1]
    size = min(1024, columns)
    return pl.pallas_call(
        functools.partial(down_kernel, total // rows, groups, rows, size),
        in_specs=whole(2),
        out_specs=whole(len(groups)),
        out_shape=[jax.ShapeDtypeStruct((group * rows, columns), BF16) for group in groups],
        scratch_shapes=[pltpu.VMEM((total, size), BF16)],
        compiler_params=params(),
        cost_estimate=cost(
            2 * total * depth * columns, 2 * depth * columns + 2 * total * columns
        ),
        name="down",
    )(down_matrix, hidden)


def last_kernel(blocks, members, parts, counts_ref, *refs):
    terms, out_ref = refs[:-1], refs[-1]
    rows = out_ref.shape[0]
    first = lax.axis_index("tp") * rows
    block_rows = members * rows // blocks
    live = picked(counts_ref, first // block_rows) - first % block_rows
    each = len(terms) // parts
    columns = out_ref.shape[1] // parts
    for part in range(parts):
        summed = 0.0
        for term in terms[part * each : (part + 1) * each]:
            summed += term[...].astype(F32)
        row = lax.broadcasted_iota(jnp.int32, summed.shape, 0)
        out_ref[:, part * columns : (part + 1) * columns] = jnp.where(
            row < live, summed, 0.0
        ).astype(BF16)


def last(members, counts, halves):
    terms = [term for half in halves for term in half]
    rows, columns = terms[0].shape
    return pl.pallas_call(
        functools.partial(last_kernel, counts.shape[1], members, len(halves)),
        in_specs=whole(1 + len(terms)),
        out_specs=whole(1)[0],
        out_shape=jax.ShapeDtypeStruct((rows, columns * len(halves)), BF16),
        compiler_params=params(),
        name="last",
    )(counts, *terms)


def add_kernel(starts, *refs):
    out_ref = refs[-1]
    rows = out_ref.shape[0]
    total = 0.0
    for start, ref in zip(starts, refs[:-1], strict=True):
        total += ref[start : start + rows, :].astype(F32)
    out_ref[...] = total.astype(BF16)


def added(rows, *terms):
    starts = [start for start, _ in terms]
    columns = terms[0][1].shape[1]
    return pl.pallas_call(
        functools.partial(add_kernel, starts),
        in_specs=whole(len(terms)),
        out_specs=whole(1)[0],
        out_shape=jax.ShapeDtypeStruct((rows, columns), BF16),
        compiler_params=params(),
        cost_estimate=cost(len(terms) * rows * columns, 2 * rows * columns),
        name="added",
    )(*[term for _, term in terms])


def per_device(
    members,
    tokens,
    gate_matrix,
    up_matrix,
    down_matrix,
    shrink_matrices,
    expand_matrices,
    adapter_per_block,
    block_token_count,
):
    rows = tokens.shape[0]
    span = shrink_matrices.shape[2]
    reach = members // 4
    ring = around(members)

    def step(x):
        return lax.ppermute(x, "tp", ring)

    def cross(x, bit=1):
        return lax.ppermute(x, "tp", crossing(members, bit))

    first = tokens
    own, second = anchor(tokens, cross(tokens))
    shrink = jnp.swapaxes(shrink_matrices, 1, 2)
    other_shrink = cross(shrink)
    pieces, mine, theirs = [own, second], [], []
    for distance in range(1, reach + 1):
        first = step(first)
        mine.append(first)
        theirs.append(cross(first))
        if distance < reach:
            second = step(second)
            mine.append(second)
            theirs.append(cross(second))
    pieces = pieces + mine + theirs

    adapters, counts = adapter_per_block[None], block_token_count[None]
    received = [0] + list(range(2, 2 + len(mine)))
    rank, expand = rank_of(
        adapters,
        members,
        received,
        [pieces[i] for i in received],
        shrink,
        other_shrink,
        expand_matrices,
        theirs[:-1],
    )
    work = [(gate_matrix, 0), (gate_matrix, 1), (up_matrix, 0), (up_matrix, 1)]
    products, after, bit = [], rank, 1
    while bit < members or work:
        if work:
            matrix, part = work.pop(0)
            products.append(product(pieces, matrix, part, 2, after, WEIGHTS[len(products)]))
        if bit < members:
            after = cross(rank, bit)
            rank = rank + after if bit == 1 else jnp.concatenate([rank, after], axis=0)
            bit *= 2
    hidden = finish(products, rank, expand, 2 * span)

    slots = 2 * reach
    groups = [1] * slots + [1] + [2] * (reach - 1) + [1]
    outs = down(hidden, down_matrix, groups, rows)
    keep, give = outs[:slots], outs[slots:]
    came = [cross(x) for x in give]
    first = step(added(rows, (0, keep[0]), (0, came[0])))
    second = None
    for index in range(1, reach):
        more = [] if second is None else [(0, second)]
        second = step(added(rows, (0, keep[2 * index]), (rows, came[index]), *more))
        first = step(added(rows, (0, keep[2 * index - 1]), (0, came[index]), (0, first)))
    return last(members, counts, [[keep[-1], came[-1], first, cross(second)]])


def solution(mesh):
    members = mesh.shape["tp"]
    return jax.shard_map(
        functools.partial(per_device, members),
        mesh=mesh,
        in_specs=(
            P(("rep", "tp"), None),
            P(None, "tp"),
            P(None, "tp"),
            P("tp", None),
            P("rep", None, "tp"),
            P("rep", None, "tp"),
            P("rep"),
            P("rep"),
        ),
        out_specs=P(("rep", "tp"), None),
        check_vma=False,
    )
```

```python
import functools

import jax
import jax.numpy as jnp
from jax import lax
from jax.experimental import pallas as pl
from jax.experimental.pallas import tpu as pltpu
from jax.sharding import PartitionSpec as P

F32 = jnp.float32
BF16 = jnp.bfloat16
VMEM_LIMIT = 20 * 1024 * 1024
WEIGHTS = (2, 2, 6, 6)


def largest_tile(size, limit):
    tile = limit
    while size % tile:
        tile //= 2
    return tile


def params():
    return pltpu.CompilerParams(vmem_limit_bytes=VMEM_LIMIT)


def cost(flops, moved):
    return pl.CostEstimate(flops=flops, bytes_accessed=moved, transcendentals=0)


def ring_of(chips):
    return list(range(0, chips, 2)) + list(range(chips - 1, 0, -2))


def piece_row(device, members, rows, side, distance, half):
    chips = members // 2
    chip = device // 2
    place = jnp.where(chip % 2 == 0, chip // 2, chips - (chip + 1) // 2)
    spot = (place + chips + jnp.where(side == 0, distance, -distance)) % chips
    there = jnp.where(spot < chips // 2, 2 * spot, 2 * (chips - spot) - 1)
    return pl.multiple_of((2 * there + half) * rows, rows)


def arrivals(device, members, rows):
    core, reach = device % 2, members // 4
    places = [(core, 0, core), (core, 0, 1 - core)]
    for side in (core, 1 - core):
        for step in range(1, reach + 1):
            places.append((1 - side, step, side))
            if step < reach:
                places.append((1 - side, step, 1 - side))
    return [piece_row(device, members, rows, *place) for place in places]


def departures(device, members, rows):
    core, reach = device % 2, members // 4
    places = []
    for side in (core, 1 - core):
        places.append((side, reach, side))
        for step in range(reach - 1, 0, -1):
            places += [(side, step, side), (side, step, 1 - side)]
        places.append((side, 0, side))
    return [piece_row(device, members, rows, *place) for place in places]


def around(members):
    ring = ring_of(members // 2)
    size = len(ring)
    pairs = []
    for i in range(size):
        pairs.append((2 * ring[i], 2 * ring[(i + 1) % size]))
        pairs.append((2 * ring[i] + 1, 2 * ring[i - 1] + 1))
    return pairs


def crossing(members, bit):
    return [(i, i ^ bit) for i in range(members)]


def whole(count):
    return [pl.BlockSpec(memory_space=pltpu.VMEM)] * count


FAR = pl.BlockSpec(memory_space=pl.ANY)


def far(x):
    return pltpu.with_memory_space_constraint(x, pltpu.HBM)


def picked(ref, index):
    row = ref[...]
    spots = lax.broadcasted_iota(jnp.int32, row.shape, 1)
    return jnp.sum(jnp.where(spots == index, row, 0))


def anchor_kernel(tokens_ref, passed_in, own_ref, passed_out, sem):
    copy = pltpu.make_async_copy(tokens_ref, own_ref, sem)
    copy.start()
    copy.wait()


def anchor(tokens, passed):
    return pl.pallas_call(
        anchor_kernel,
        in_specs=[FAR, FAR],
        out_specs=whole(1) + [FAR],
        out_shape=[jax.ShapeDtypeStruct(passed.shape, passed.dtype)] * 2,
        input_output_aliases={1: 1},
        scratch_shapes=[pltpu.SemaphoreType.DMA],
        compiler_params=params(),
        cost_estimate=cost(30_000_000_000, 0),
        name="anchor",
    )(far(tokens), passed)


def rank_kernel(members, numbers, ids_ref, expand_ref, own_ref, other_ref, *refs):
    pieces, (out_ref, chosen_ref, scratch, sems) = refs[: len(numbers)], refs[-4:]
    rows = pieces[0].shape[0]
    blocks, span = ids_ref.shape[1], own_ref.shape[1]
    block_rows = members * rows // blocks
    device = lax.axis_index("tp")
    places = arrivals(device, members, rows)
    lhs = jnp.concatenate([piece[...] for piece in pieces], axis=0)
    ids = [picked(ids_ref, b) for b in range(blocks)]
    copies = [
        pltpu.make_async_copy(expand_ref.at[ids[b]], chosen_ref.at[b], sems.at[b])
        for b in range(blocks)
    ]
    for copy in copies:
        copy.start()
    weights = jnp.concatenate([ref[i] for ref in (own_ref, other_ref) for i in ids], axis=0)
    found = lax.dot_general(
        lhs, weights, (((1,), (1,)), ((), ())), preferred_element_type=F32
    )
    scratch[...] = jnp.zeros_like(scratch)
    for index, number in enumerate(numbers):
        part = found[index * rows : (index + 1) * rows]
        for source in range(2):
            first = source * blocks * span
            value = part[:, first : first + span]
            for b in range(1, blocks):
                columns = part[:, first + b * span : first + (b + 1) * span]
                value = jnp.where(places[number] // block_rows == b, columns, value)
            scratch[source, pl.ds(places[number], rows), :span] = value
    own, other = scratch[0].T[:span], scratch[1].T[:span]
    lower = device % 2 == 0
    out_ref[...] = jnp.concatenate(
        [jnp.where(lower, own, other), jnp.where(lower, other, own)], axis=0
    ).astype(BF16)
    for copy in copies:
        copy.wait()


def rank_of(adapters, members, numbers, pieces, shrink, other, expand, after):
    rows, model = pieces[0].shape
    span = shrink.shape[1]
    total = rows * members
    return pl.pallas_call(
        functools.partial(rank_kernel, members, numbers),
        in_specs=whole(1) + [FAR] + whole(2 + len(pieces)) + [FAR] * len(after),
        out_specs=whole(2),
        out_shape=[
            jax.ShapeDtypeStruct((2 * span, total), BF16),
            jax.ShapeDtypeStruct((adapters.shape[1],) + expand.shape[1:], BF16),
        ],
        scratch_shapes=[
            pltpu.VMEM((2, total, 128), F32),
            pltpu.SemaphoreType.DMA((adapters.shape[1],)),
        ],
        compiler_params=params(),
        cost_estimate=cost(2 * total * model * span * 2, 2 * total * model),
        name="rank",
    )(adapters, far(expand), shrink, other, *pieces, *after)


def product_kernel(first, w_ref, *refs):
    pieces, out_ref = refs[:-2], refs[-1]
    rows = pieces[0].shape[0]
    depth = w_ref.shape[0] // 2
    size = depth
    places = arrivals(lax.axis_index("tp"), len(pieces), rows)
    part = 0.0
    for start in range(first, first + depth, size):
        lhs = jnp.concatenate([piece[:, start : start + size] for piece in pieces], axis=0)
        part += jnp.dot(lhs, w_ref[start : start + size, :], preferred_element_type=F32)
    for index, place in enumerate(places):
        out_ref[pl.ds(place, rows), :] = part[index * rows : (index + 1) * rows]


def product(pieces, matrix, part, parts, after, weight):
    rows, model = pieces[0].shape
    total = rows * len(pieces)
    width = matrix.shape[1]
    depth = model // parts
    return pl.pallas_call(
        functools.partial(product_kernel, part * depth),
        in_specs=whole(len(pieces) + 2),
        out_specs=whole(1)[0],
        out_shape=jax.ShapeDtypeStruct((total, width), F32),
        compiler_params=params(),
        cost_estimate=cost(weight * total * depth * width, 2 * depth * (width + total)),
        name="product",
    )(matrix, *pieces, after)


def finish_kernel(span, piece_rows, gate_a, gate_b, up_a, up_b, rank_ref, expand_ref, out_ref, hidden_ref):
    ranks = rank_ref.shape[0]
    chip = lax.axis_index("tp") // 2
    shape = (ranks, ranks)
    want = lax.broadcasted_iota(jnp.int32, shape, 0)
    have = lax.broadcasted_iota(jnp.int32, shape, 1)
    origin = ((have // span) ^ chip) * span + have % span
    order = jnp.where(want == origin, 1.0, 0.0).astype(BF16)
    rank = jnp.dot(order, rank_ref[...], preferred_element_type=F32).T.astype(BF16)
    half = ranks // 2
    blocks = expand_ref.shape[0]
    rows = hidden_ref.shape[0] // blocks
    for b in range(blocks):
        part = slice(b * rows, (b + 1) * rows)
        expand = expand_ref[b]
        gate = jnp.dot(rank[part, :half], expand[:half], preferred_element_type=F32)
        up = jnp.dot(rank[part, half:], expand[half:], preferred_element_type=F32)
        gate += gate_a[part] + gate_b[part]
        up += up_a[part] + up_b[part]
        hidden_ref[part] = (gate / (1.0 + jnp.exp(-gate)) * up).astype(BF16)
    members = hidden_ref.shape[0] // piece_rows
    for index, place in enumerate(departures(lax.axis_index("tp"), members, piece_rows)):
        out_ref[index * piece_rows : (index + 1) * piece_rows, :] = hidden_ref[
            pl.ds(place, piece_rows), :
        ]


def finish(products, rank, expand, span, piece_rows):
    total, width = products[0].shape
    return pl.pallas_call(
        functools.partial(finish_kernel, span, piece_rows),
        in_specs=whole(6),
        out_specs=whole(1)[0],
        out_shape=jax.ShapeDtypeStruct((total, width), BF16),
        scratch_shapes=[pltpu.VMEM((total, width), BF16)],
        compiler_params=params(),
        name="finish",
    )(*products, rank, expand)


def down_kernel(groups, rows, size, w_ref, hidden_ref, *outs):
    hidden = hidden_ref[...]
    for start in range(0, w_ref.shape[1], size):
        columns = slice(start, start + size)
        part = jnp.dot(hidden, w_ref[:, columns], preferred_element_type=F32)
        at = 0
        for out, group in zip(outs, groups, strict=True):
            out[:, columns] = part[at : at + group * rows].astype(BF16)
            at += group * rows


def down(hidden, down_matrix, groups, rows):
    total, depth = hidden.shape
    columns = down_matrix.shape[1]
    size = min(1024, columns)
    return pl.pallas_call(
        functools.partial(down_kernel, groups, rows, size),
        in_specs=whole(2),
        out_specs=whole(len(groups)),
        out_shape=[jax.ShapeDtypeStruct((group * rows, columns), BF16) for group in groups],
        compiler_params=params(),
        cost_estimate=cost(
            2 * total * depth * columns, 2 * depth * columns + 2 * total * columns
        ),
        name="down",
    )(down_matrix, hidden)


def last_kernel(blocks, members, parts, counts_ref, *refs):
    terms, out_ref = refs[:-1], refs[-1]
    rows = out_ref.shape[0]
    first = lax.axis_index("tp") * rows
    block_rows = members * rows // blocks
    live = picked(counts_ref, first // block_rows) - first % block_rows
    each = len(terms) // parts
    columns = out_ref.shape[1] // parts
    for part in range(parts):
        summed = 0.0
        for term in terms[part * each : (part + 1) * each]:
            summed += term[...].astype(F32)
        row = lax.broadcasted_iota(jnp.int32, summed.shape, 0)
        out_ref[:, part * columns : (part + 1) * columns] = jnp.where(
            row < live, summed, 0.0
        ).astype(BF16)


def last(members, counts, halves):
    terms = [term for half in halves for term in half]
    rows, columns = terms[0].shape
    return pl.pallas_call(
        functools.partial(last_kernel, counts.shape[1], members, len(halves)),
        in_specs=whole(1 + len(terms)),
        out_specs=whole(1)[0],
        out_shape=jax.ShapeDtypeStruct((rows, columns * len(halves)), BF16),
        compiler_params=params(),
        name="last",
    )(counts, *terms)


def add_kernel(starts, *refs):
    out_ref = refs[-1]
    rows = out_ref.shape[0]
    total = 0.0
    for start, ref in zip(starts, refs[:-1], strict=True):
        total += ref[start : start + rows, :].astype(F32)
    out_ref[...] = total.astype(BF16)


def added(rows, *terms):
    starts = [start for start, _ in terms]
    columns = terms[0][1].shape[1]
    return pl.pallas_call(
        functools.partial(add_kernel, starts),
        in_specs=whole(len(terms)),
        out_specs=whole(1)[0],
        out_shape=jax.ShapeDtypeStruct((rows, columns), BF16),
        compiler_params=params(),
        cost_estimate=cost(len(terms) * rows * columns, 2 * rows * columns),
        name="added",
    )(*[term for _, term in terms])


def per_device(
    members,
    tokens,
    gate_matrix,
    up_matrix,
    down_matrix,
    shrink_matrices,
    expand_matrices,
    adapter_per_block,
    block_token_count,
):
    rows = tokens.shape[0]
    span = shrink_matrices.shape[2]
    reach = members // 4
    ring = around(members)

    def step(x):
        return lax.ppermute(x, "tp", ring)

    def cross(x, bit=1):
        return lax.ppermute(x, "tp", crossing(members, bit))

    first = tokens
    own, second = anchor(tokens, cross(tokens))
    shrink = jnp.swapaxes(shrink_matrices, 1, 2)
    other_shrink = cross(shrink)
    pieces, mine, theirs = [own, second], [], []
    for distance in range(1, reach + 1):
        first = step(first)
        mine.append(first)
        theirs.append(cross(first))
        if distance < reach:
            second = step(second)
            mine.append(second)
            theirs.append(cross(second))
    pieces = pieces + mine + theirs

    adapters, counts = adapter_per_block[None], block_token_count[None]
    received = [0] + list(range(2, 2 + len(mine)))
    rank, expand = rank_of(
        adapters,
        members,
        received,
        [pieces[i] for i in received],
        shrink,
        other_shrink,
        expand_matrices,
        theirs[:-1],
    )
    work = [(gate_matrix, 0), (gate_matrix, 1), (up_matrix, 0), (up_matrix, 1)]
    products, after, bit = [], rank, 1
    while bit < members or work:
        if work:
            matrix, part = work.pop(0)
            products.append(product(pieces, matrix, part, 2, after, WEIGHTS[len(products)]))
        if bit < members:
            after = cross(rank, bit)
            rank = rank + after if bit == 1 else jnp.concatenate([rank, after], axis=0)
            bit *= 2
    hidden = finish(products, rank, expand, 2 * span, rows)

    slots = 2 * reach
    groups = [1] * slots + [1] + [2] * (reach - 1) + [1]
    outs = down(hidden, down_matrix, groups, rows)
    keep, give = outs[:slots], outs[slots:]
    came = [cross(x) for x in give]
    first = step(added(rows, (0, keep[0]), (0, came[0])))
    second = None
    for index in range(1, reach):
        more = [] if second is None else [(0, second)]
        second = step(added(rows, (0, keep[2 * index]), (rows, came[index]), *more))
        first = step(added(rows, (0, keep[2 * index - 1]), (0, came[index]), (0, first)))
    return last(members, counts, [[keep[-1], came[-1], first, cross(second)]])


def solution(mesh):
    members = mesh.shape["tp"]
    return jax.shard_map(
        functools.partial(per_device, members),
        mesh=mesh,
        in_specs=(
            P(("rep", "tp"), None),
            P(None, "tp"),
            P(None, "tp"),
            P("tp", None),
            P("rep", None, "tp"),
            P("rep", None, "tp"),
            P("rep"),
            P("rep"),
        ),
        out_specs=P(("rep", "tp"), None),
        check_vma=False,
    )
```

```python
import functools

import jax
import jax.numpy as jnp
from jax import lax
from jax.experimental import pallas as pl
from jax.experimental.pallas import tpu as pltpu
from jax.sharding import PartitionSpec as P

F32 = jnp.float32
BF16 = jnp.bfloat16
VMEM_LIMIT = 17 * 1024 * 1024
WEIGHTS = (2, 2, 20, 20)


def largest_tile(size, limit):
    tile = limit
    while size % tile:
        tile //= 2
    return tile


def params():
    return pltpu.CompilerParams(vmem_limit_bytes=VMEM_LIMIT)


def cost(flops, moved):
    return pl.CostEstimate(flops=flops, bytes_accessed=moved, transcendentals=0)


def ring_of(chips):
    return list(range(0, chips, 2)) + list(range(chips - 1, 0, -2))


def piece_row(device, members, rows, side, distance, half):
    chips = members // 2
    chip = device // 2
    place = jnp.where(chip % 2 == 0, chip // 2, chips - (chip + 1) // 2)
    spot = (place + chips + jnp.where(side == 0, distance, -distance)) % chips
    there = jnp.where(spot < chips // 2, 2 * spot, 2 * (chips - spot) - 1)
    return pl.multiple_of((2 * there + half) * rows, rows)


def arrivals(device, members, rows):
    core, reach = device % 2, members // 4
    places = [(core, 0, core), (core, 0, 1 - core)]
    for side in (core, 1 - core):
        for step in range(1, reach + 1):
            places.append((1 - side, step, side))
            if step < reach:
                places.append((1 - side, step, 1 - side))
    return [piece_row(device, members, rows, *place) for place in places]


def departures(device, members, rows):
    core, reach = device % 2, members // 4
    places = []
    for side in (core, 1 - core):
        places.append((side, reach, side))
        for step in range(reach - 1, 0, -1):
            places += [(side, step, side), (side, step, 1 - side)]
        places.append((side, 0, side))
    return [piece_row(device, members, rows, *place) for place in places]


def around(members):
    ring = ring_of(members // 2)
    size = len(ring)
    pairs = []
    for i in range(size):
        pairs.append((2 * ring[i], 2 * ring[(i + 1) % size]))
        pairs.append((2 * ring[i] + 1, 2 * ring[i - 1] + 1))
    return pairs


def crossing(members, bit):
    return [(i, i ^ bit) for i in range(members)]


def whole(count):
    return [pl.BlockSpec(memory_space=pltpu.VMEM)] * count


FAR = pl.BlockSpec(memory_space=pl.ANY)


def far(x):
    return pltpu.with_memory_space_constraint(x, pltpu.HBM)


def picked(ref, index):
    row = ref[...]
    spots = lax.broadcasted_iota(jnp.int32, row.shape, 1)
    return jnp.sum(jnp.where(spots == index, row, 0))


def anchor_kernel(tokens_ref, passed_in, own_ref, passed_out, sem):
    copy = pltpu.make_async_copy(tokens_ref, own_ref, sem)
    copy.start()
    copy.wait()


def anchor(tokens, passed):
    return pl.pallas_call(
        anchor_kernel,
        in_specs=[FAR, FAR],
        out_specs=whole(1) + [FAR],
        out_shape=[jax.ShapeDtypeStruct(passed.shape, passed.dtype)] * 2,
        input_output_aliases={1: 1},
        scratch_shapes=[pltpu.SemaphoreType.DMA],
        compiler_params=params(),
        cost_estimate=cost(30_000_000_000, 0),
        name="anchor",
    )(far(tokens), passed)


def rank_kernel(members, numbers, ids_ref, expand_ref, own_ref, other_ref, *refs):
    pieces, (out_ref, chosen_ref, scratch, sems) = refs[: len(numbers)], refs[-4:]
    rows = pieces[0].shape[0]
    blocks, span = ids_ref.shape[1], own_ref.shape[1]
    block_rows = members * rows // blocks
    device = lax.axis_index("tp")
    places = arrivals(device, members, rows)
    lhs = jnp.concatenate([piece[...] for piece in pieces], axis=0)
    ids = [picked(ids_ref, b) for b in range(blocks)]
    copies = [
        pltpu.make_async_copy(expand_ref.at[ids[b]], chosen_ref.at[b], sems.at[b])
        for b in range(blocks)
    ]
    for copy in copies:
        copy.start()
    weights = jnp.concatenate([ref[i] for ref in (own_ref, other_ref) for i in ids], axis=0)
    found = lax.dot_general(
        lhs, weights, (((1,), (1,)), ((), ())), preferred_element_type=F32
    )
    scratch[...] = jnp.zeros_like(scratch)
    for index, number in enumerate(numbers):
        part = found[index * rows : (index + 1) * rows]
        for source in range(2):
            first = source * blocks * span
            value = part[:, first : first + span]
            for b in range(1, blocks):
                columns = part[:, first + b * span : first + (b + 1) * span]
                value = jnp.where(places[number] // block_rows == b, columns, value)
            scratch[source, pl.ds(places[number], rows), :span] = value
    own, other = scratch[0].T[:span], scratch[1].T[:span]
    lower = device % 2 == 0
    out_ref[...] = jnp.concatenate(
        [jnp.where(lower, own, other), jnp.where(lower, other, own)], axis=0
    ).astype(BF16)
    for copy in copies:
        copy.wait()


def rank_of(adapters, members, numbers, pieces, shrink, other, expand, after):
    rows, model = pieces[0].shape
    span = shrink.shape[1]
    total = rows * members
    return pl.pallas_call(
        functools.partial(rank_kernel, members, numbers),
        in_specs=whole(1) + [FAR] + whole(2 + len(pieces)) + [FAR] * len(after),
        out_specs=whole(2),
        out_shape=[
            jax.ShapeDtypeStruct((2 * span, total), BF16),
            jax.ShapeDtypeStruct((adapters.shape[1],) + expand.shape[1:], BF16),
        ],
        scratch_shapes=[
            pltpu.VMEM((2, total, 128), F32),
            pltpu.SemaphoreType.DMA((adapters.shape[1],)),
        ],
        compiler_params=params(),
        cost_estimate=cost(2 * total * model * span * 2, 2 * total * model),
        name="rank",
    )(adapters, far(expand), shrink, other, *pieces, *after)


def product_kernel(first, depth, w_ref, *refs):
    pieces, out_ref = refs[:-2], refs[-1]
    rows = pieces[0].shape[0]
    places = arrivals(lax.axis_index("tp"), len(pieces), rows)
    lhs = jnp.concatenate([piece[:, first : first + depth] for piece in pieces], axis=0)
    part = jnp.dot(lhs, w_ref[first : first + depth, :], preferred_element_type=F32)
    for index, place in enumerate(places):
        out_ref[pl.ds(place, rows), :] = part[index * rows : (index + 1) * rows]


def product(pieces, matrix, first, depth, after, weight):
    rows = pieces[0].shape[0]
    total = rows * len(pieces)
    width = matrix.shape[1]
    return pl.pallas_call(
        functools.partial(product_kernel, first, depth),
        in_specs=whole(len(pieces) + 2),
        out_specs=whole(1)[0],
        out_shape=jax.ShapeDtypeStruct((total, width), F32),
        compiler_params=params(),
        cost_estimate=cost(weight * total * depth * width, 2 * depth * (width + total)),
        name="product",
    )(matrix, *pieces, after)


def finish_kernel(span, piece_rows, gate_a, gate_b, up_a, up_b, rank_ref, expand_ref, out_ref, hidden_ref):
    ranks = rank_ref.shape[0]
    chip = lax.axis_index("tp") // 2
    shape = (ranks, ranks)
    want = lax.broadcasted_iota(jnp.int32, shape, 0)
    have = lax.broadcasted_iota(jnp.int32, shape, 1)
    origin = ((have // span) ^ chip) * span + have % span
    order = jnp.where(want == origin, 1.0, 0.0).astype(BF16)
    rank = jnp.dot(order, rank_ref[...], preferred_element_type=F32).T.astype(BF16)
    half = ranks // 2
    blocks = expand_ref.shape[0]
    rows = hidden_ref.shape[0] // blocks
    for b in range(blocks):
        part = slice(b * rows, (b + 1) * rows)
        expand = expand_ref[b]
        gate = jnp.dot(rank[part, :half], expand[:half], preferred_element_type=F32)
        up = jnp.dot(rank[part, half:], expand[half:], preferred_element_type=F32)
        gate += gate_a[part] + gate_b[part]
        up += up_a[part] + up_b[part]
        hidden_ref[part] = (gate / (1.0 + jnp.exp(-gate)) * up).astype(BF16)
    members = hidden_ref.shape[0] // piece_rows
    for index, place in enumerate(departures(lax.axis_index("tp"), members, piece_rows)):
        out_ref[index * piece_rows : (index + 1) * piece_rows, :] = hidden_ref[
            pl.ds(place, piece_rows), :
        ]


def finish(products, rank, expand, span, piece_rows):
    total, width = products[0].shape
    return pl.pallas_call(
        functools.partial(finish_kernel, span, piece_rows),
        in_specs=whole(6),
        out_specs=whole(1)[0],
        out_shape=jax.ShapeDtypeStruct((total, width), BF16),
        scratch_shapes=[pltpu.VMEM((total, width), BF16)],
        compiler_params=params(),
        name="finish",
    )(*products, rank, expand)


def down_kernel(groups, rows, size, w_ref, hidden_ref, *outs):
    hidden = hidden_ref[...]
    for start in range(0, w_ref.shape[1], size):
        columns = slice(start, start + size)
        part = jnp.dot(hidden, w_ref[:, columns], preferred_element_type=F32)
        at = 0
        for out, group in zip(outs, groups, strict=True):
            out[:, columns] = part[at : at + group * rows].astype(BF16)
            at += group * rows


def down(hidden, down_matrix, groups, rows):
    total, depth = hidden.shape
    columns = down_matrix.shape[1]
    size = min(1024, columns)
    return pl.pallas_call(
        functools.partial(down_kernel, groups, rows, size),
        in_specs=whole(2),
        out_specs=whole(len(groups)),
        out_shape=[jax.ShapeDtypeStruct((group * rows, columns), BF16) for group in groups],
        compiler_params=params(),
        cost_estimate=cost(
            2 * total * depth * columns, 2 * depth * columns + 2 * total * columns
        ),
        name="down",
    )(down_matrix, hidden)


def last_kernel(blocks, members, parts, counts_ref, *refs):
    terms, out_ref = refs[:-1], refs[-1]
    rows = out_ref.shape[0]
    first = lax.axis_index("tp") * rows
    block_rows = members * rows // blocks
    live = picked(counts_ref, first // block_rows) - first % block_rows
    each = len(terms) // parts
    columns = out_ref.shape[1] // parts
    for part in range(parts):
        summed = 0.0
        for term in terms[part * each : (part + 1) * each]:
            summed += term[...].astype(F32)
        row = lax.broadcasted_iota(jnp.int32, summed.shape, 0)
        out_ref[:, part * columns : (part + 1) * columns] = jnp.where(
            row < live, summed, 0.0
        ).astype(BF16)


def last(members, counts, halves):
    terms = [term for half in halves for term in half]
    rows, columns = terms[0].shape
    return pl.pallas_call(
        functools.partial(last_kernel, counts.shape[1], members, len(halves)),
        in_specs=whole(1 + len(terms)),
        out_specs=whole(1)[0],
        out_shape=jax.ShapeDtypeStruct((rows, columns * len(halves)), BF16),
        compiler_params=params(),
        name="last",
    )(counts, *terms)


def add_kernel(starts, *refs):
    out_ref = refs[-1]
    rows = out_ref.shape[0]
    total = 0.0
    for start, ref in zip(starts, refs[:-1], strict=True):
        total += ref[start : start + rows, :].astype(F32)
    out_ref[...] = total.astype(BF16)


def added(rows, *terms):
    starts = [start for start, _ in terms]
    columns = terms[0][1].shape[1]
    return pl.pallas_call(
        functools.partial(add_kernel, starts),
        in_specs=whole(len(terms)),
        out_specs=whole(1)[0],
        out_shape=jax.ShapeDtypeStruct((rows, columns), BF16),
        compiler_params=params(),
        cost_estimate=cost(len(terms) * rows * columns, 2 * rows * columns),
        name="added",
    )(*[term for _, term in terms])


def per_device(
    members,
    tokens,
    gate_matrix,
    up_matrix,
    down_matrix,
    shrink_matrices,
    expand_matrices,
    adapter_per_block,
    block_token_count,
):
    rows = tokens.shape[0]
    span = shrink_matrices.shape[2]
    reach = members // 4
    ring = around(members)

    def step(x):
        return lax.ppermute(x, "tp", ring)

    def cross(x, bit=1):
        return lax.ppermute(x, "tp", crossing(members, bit))

    first = tokens
    own, second = anchor(tokens, cross(tokens))
    shrink = jnp.swapaxes(shrink_matrices, 1, 2)
    other_shrink = cross(shrink)
    pieces, mine, theirs = [own, second], [], []
    for distance in range(1, reach + 1):
        first = step(first)
        mine.append(first)
        theirs.append(cross(first))
        if distance < reach:
            second = step(second)
            mine.append(second)
            theirs.append(cross(second))
    pieces = pieces + mine + theirs

    adapters, counts = adapter_per_block[None], block_token_count[None]
    received = [0] + list(range(2, 2 + len(mine)))
    rank, expand = rank_of(
        adapters,
        members,
        received,
        [pieces[i] for i in received],
        shrink,
        other_shrink,
        expand_matrices,
        theirs[:-1],
    )
    rank = rank + cross(rank)
    model = gate_matrix.shape[0]
    cut = model * 2 // 3 // 256 * 256
    rest = model - cut
    work = [
        [(gate_matrix, 0, cut)],
        [(gate_matrix, cut, rest), (up_matrix, 0, rest)],
        [(up_matrix, rest, cut)],
    ]
    products, after, bit = [], rank, 2
    while bit < members or work:
        for part in work.pop(0) if work else []:
            products.append(product(pieces, *part, after, WEIGHTS[len(products)]))
        if bit < members:
            after = cross(rank, bit)
            rank = jnp.concatenate([rank, after], axis=0)
            bit *= 2
    hidden = finish(products, rank, expand, 2 * span, rows)

    slots = 2 * reach
    groups = [1] * slots + [1] + [2] * (reach - 1) + [1]
    outs = down(hidden, down_matrix, groups, rows)
    keep, give = outs[:slots], outs[slots:]
    came = [cross(x) for x in give]
    first = step(added(rows, (0, keep[0]), (0, came[0])))
    second = None
    for index in range(1, reach):
        more = [] if second is None else [(0, second)]
        second = step(added(rows, (0, keep[2 * index]), (rows, came[index]), *more))
        first = step(added(rows, (0, keep[2 * index - 1]), (0, came[index]), (0, first)))
    return last(members, counts, [[keep[-1], came[-1], first, cross(second)]])


def solution(mesh):
    members = mesh.shape["tp"]
    return jax.shard_map(
        functools.partial(per_device, members),
        mesh=mesh,
        in_specs=(
            P(("rep", "tp"), None),
            P(None, "tp"),
            P(None, "tp"),
            P("tp", None),
            P("rep", None, "tp"),
            P("rep", None, "tp"),
            P("rep"),
            P("rep"),
        ),
        out_specs=P(("rep", "tp"), None),
        check_vma=False,
    )
```

```python
import functools

import jax
import jax.numpy as jnp
from jax import lax
from jax.experimental import pallas as pl
from jax.experimental.pallas import tpu as pltpu
from jax.sharding import PartitionSpec as P

F32 = jnp.float32
BF16 = jnp.bfloat16
VMEM_LIMIT = 8 * 1024 * 1024
WEIGHTS = (6, 6, 6, 6)


def largest_tile(size, limit):
    tile = limit
    while size % tile:
        tile //= 2
    return tile


def params():
    return pltpu.CompilerParams(vmem_limit_bytes=VMEM_LIMIT)


def cost(flops, moved):
    return pl.CostEstimate(flops=flops, bytes_accessed=moved, transcendentals=0)


def ring_of(chips):
    return list(range(0, chips, 2)) + list(range(chips - 1, 0, -2))


def piece_row(device, members, rows, side, distance, half):
    chips = members // 2
    chip = device // 2
    place = jnp.where(chip % 2 == 0, chip // 2, chips - (chip + 1) // 2)
    spot = (place + chips + jnp.where(side == 0, distance, -distance)) % chips
    there = jnp.where(spot < chips // 2, 2 * spot, 2 * (chips - spot) - 1)
    return pl.multiple_of((2 * there + half) * rows, rows)


def arrivals(device, members, rows):
    core, reach = device % 2, members // 4
    places = [(core, 0, core), (core, 0, 1 - core)]
    for side in (core, 1 - core):
        for step in range(1, reach + 1):
            places.append((1 - side, step, side))
            if step < reach:
                places.append((1 - side, step, 1 - side))
    return [piece_row(device, members, rows, *place) for place in places]


def departures(device, members, rows):
    core, reach = device % 2, members // 4
    places = []
    for side in (core, 1 - core):
        places.append((side, reach, side))
        for step in range(reach - 1, 0, -1):
            places += [(side, step, side), (side, step, 1 - side)]
        places.append((side, 0, side))
    return [piece_row(device, members, rows, *place) for place in places]


def around(members):
    ring = ring_of(members // 2)
    size = len(ring)
    pairs = []
    for i in range(size):
        pairs.append((2 * ring[i], 2 * ring[(i + 1) % size]))
        pairs.append((2 * ring[i] + 1, 2 * ring[i - 1] + 1))
    return pairs


def crossing(members, bit):
    return [(i, i ^ bit) for i in range(members)]


def whole(count):
    return [pl.BlockSpec(memory_space=pltpu.VMEM)] * count


FAR = pl.BlockSpec(memory_space=pl.ANY)


def far(x):
    return pltpu.with_memory_space_constraint(x, pltpu.HBM)


def picked(ref, index):
    row = ref[...]
    spots = lax.broadcasted_iota(jnp.int32, row.shape, 1)
    return jnp.sum(jnp.where(spots == index, row, 0))


def anchor_kernel(tokens_ref, passed_in, own_ref, passed_out, sem):
    copy = pltpu.make_async_copy(tokens_ref, own_ref, sem)
    copy.start()
    copy.wait()


def anchor(tokens, passed):
    return pl.pallas_call(
        anchor_kernel,
        in_specs=[FAR, FAR],
        out_specs=whole(1) + [FAR],
        out_shape=[jax.ShapeDtypeStruct(passed.shape, passed.dtype)] * 2,
        input_output_aliases={1: 1},
        scratch_shapes=[pltpu.SemaphoreType.DMA],
        compiler_params=params(),
        cost_estimate=cost(30_000_000_000, 0),
        name="anchor",
    )(far(tokens), passed)


def rank_kernel(members, numbers, ids_ref, expand_ref, own_ref, other_ref, *refs):
    pieces, (out_ref, chosen_ref, scratch, sems) = refs[: len(numbers)], refs[-4:]
    rows = pieces[0].shape[0]
    blocks, span = ids_ref.shape[1], own_ref.shape[1]
    block_rows = members * rows // blocks
    device = lax.axis_index("tp")
    places = arrivals(device, members, rows)
    lhs = jnp.concatenate([piece[...] for piece in pieces], axis=0)
    ids = [picked(ids_ref, b) for b in range(blocks)]
    copies = [
        pltpu.make_async_copy(expand_ref.at[ids[b]], chosen_ref.at[b], sems.at[b])
        for b in range(blocks)
    ]
    for copy in copies:
        copy.start()
    weights = jnp.concatenate([ref[i] for ref in (own_ref, other_ref) for i in ids], axis=0)
    found = lax.dot_general(
        lhs, weights, (((1,), (1,)), ((), ())), preferred_element_type=F32
    )
    scratch[...] = jnp.zeros_like(scratch)
    for index, number in enumerate(numbers):
        part = found[index * rows : (index + 1) * rows]
        for source in range(2):
            first = source * blocks * span
            value = part[:, first : first + span]
            for b in range(1, blocks):
                columns = part[:, first + b * span : first + (b + 1) * span]
                value = jnp.where(places[number] // block_rows == b, columns, value)
            scratch[source, pl.ds(places[number], rows), :span] = value
    own, other = scratch[0].T[:span], scratch[1].T[:span]
    lower = device % 2 == 0
    out_ref[...] = jnp.concatenate(
        [jnp.where(lower, own, other), jnp.where(lower, other, own)], axis=0
    ).astype(BF16)
    for copy in copies:
        copy.wait()


def rank_of(adapters, members, numbers, pieces, shrink, other, expand, after):
    rows, model = pieces[0].shape
    span = shrink.shape[1]
    total = rows * members
    return pl.pallas_call(
        functools.partial(rank_kernel, members, numbers),
        in_specs=whole(1) + [FAR] + whole(2 + len(pieces)) + [FAR] * len(after),
        out_specs=whole(2),
        out_shape=[
            jax.ShapeDtypeStruct((2 * span, total), BF16),
            jax.ShapeDtypeStruct((adapters.shape[1],) + expand.shape[1:], BF16),
        ],
        scratch_shapes=[
            pltpu.VMEM((2, total, 128), F32),
            pltpu.SemaphoreType.DMA((adapters.shape[1],)),
        ],
        compiler_params=params(),
        cost_estimate=cost(2 * total * model * span * 2, 2 * total * model),
        name="rank",
    )(adapters, far(expand), shrink, other, *pieces, *after)


def product_kernel(first, depth, main, role, w_ref, *refs):
    outs = 1 if role is None else 2
    refs, outs = refs[:-outs], refs[-outs:]
    aside, pieces = (refs[:1], refs[1:-1]) if role == 1 else ((), refs[:-1])
    rows = pieces[0].shape[0]
    places = arrivals(lax.axis_index("tp"), len(pieces), rows)
    lhs = jnp.concatenate([piece[:, first : first + depth] for piece in pieces], axis=0)
    span = slice(first, first + depth)

    def store(out_ref, weights):
        part = jnp.dot(lhs, weights, preferred_element_type=F32)
        for index, place in enumerate(places):
            out_ref[pl.ds(place, rows), :] = part[index * rows : (index + 1) * rows]

    store(outs[0], w_ref[span, :main])
    if role == 0:
        outs[1][...] = w_ref[span, main:]
    elif role == 1:
        store(outs[1], jnp.concatenate([w_ref[span, main:], aside[0][...]], axis=1))


def product(pieces, matrix, part, parts, after, weight, aside):
    rows = pieces[0].shape[0]
    total = rows * len(pieces)
    model, width = matrix.shape
    depth = model // parts
    tail = 128 if width % 256 == 128 else 0
    main = width - tail
    out_shape = [jax.ShapeDtypeStruct((total, main), F32)]
    role, extra = None, []
    if tail and isinstance(aside, int):
        role = 0
        out_shape.append(jax.ShapeDtypeStruct((depth, tail), BF16))
    elif tail:
        role, extra = 1, [aside]
        out_shape.append(jax.ShapeDtypeStruct((total, 2 * tail), F32))
    return pl.pallas_call(
        functools.partial(product_kernel, part * depth, depth, main, role),
        in_specs=whole(len(pieces) + 2 + len(extra)),
        out_specs=whole(len(out_shape)),
        out_shape=out_shape,
        compiler_params=params(),
        cost_estimate=cost(weight * total * depth * width, 2 * depth * (width + total)),
        name="product",
    )(matrix, *extra, *pieces, after)


def finish_kernel(span, piece_rows, *refs):
    *products, rank_ref, expand_ref, out_ref, hidden_ref = refs
    gate_a, gate_b, up_a, up_b, *tails = products
    ranks = rank_ref.shape[0]
    chip = lax.axis_index("tp") // 2
    shape = (ranks, ranks)
    want = lax.broadcasted_iota(jnp.int32, shape, 0)
    have = lax.broadcasted_iota(jnp.int32, shape, 1)
    origin = ((have // span) ^ chip) * span + have % span
    order = jnp.where(want == origin, 1.0, 0.0).astype(BF16)
    rank = jnp.dot(order, rank_ref[...], preferred_element_type=F32).T.astype(BF16)
    half = ranks // 2
    blocks = expand_ref.shape[0]
    rows = hidden_ref.shape[0] // blocks
    main = gate_a.shape[1]
    tail = hidden_ref.shape[1] - main
    for b in range(blocks):
        part = slice(b * rows, (b + 1) * rows)
        expand = expand_ref[b]
        gate = jnp.dot(rank[part, :half], expand[:half], preferred_element_type=F32)
        up = jnp.dot(rank[part, half:], expand[half:], preferred_element_type=F32)
        gates = [gate[:, :main] + gate_a[part] + gate_b[part]]
        ups = [up[:, :main] + up_a[part] + up_b[part]]
        if tail:
            both = tails[0][part] + tails[1][part]
            gates.append(gate[:, main:] + both[:, tail:])
            ups.append(up[:, main:] + both[:, :tail])
        column = 0
        for gate, up in zip(gates, ups, strict=True):
            hidden = (gate / (1.0 + jnp.exp(-gate)) * up).astype(BF16)
            hidden_ref[part, column : column + gate.shape[1]] = hidden
            column += gate.shape[1]
    members = hidden_ref.shape[0] // piece_rows
    for index, place in enumerate(departures(lax.axis_index("tp"), members, piece_rows)):
        out_ref[index * piece_rows : (index + 1) * piece_rows, :] = hidden_ref[
            pl.ds(place, piece_rows), :
        ]


def finish(products, rank, expand, span, piece_rows):
    total, width = products[0].shape[0], expand.shape[2]
    return pl.pallas_call(
        functools.partial(finish_kernel, span, piece_rows),
        in_specs=whole(len(products) + 2),
        out_specs=whole(1)[0],
        out_shape=jax.ShapeDtypeStruct((total, width), BF16),
        scratch_shapes=[pltpu.VMEM((total, width), BF16)],
        compiler_params=params(),
        name="finish",
    )(*products, rank, expand)


def down_kernel(groups, rows, size, w_ref, hidden_ref, *outs):
    hidden = hidden_ref[...]
    for start in range(0, w_ref.shape[1], size):
        columns = slice(start, start + size)
        part = jnp.dot(hidden, w_ref[:, columns], preferred_element_type=F32)
        at = 0
        for out, group in zip(outs, groups, strict=True):
            out[:, columns] = part[at : at + group * rows].astype(BF16)
            at += group * rows


def down(hidden, down_matrix, groups, rows):
    total, depth = hidden.shape
    columns = down_matrix.shape[1]
    size = min(1024, columns)
    return pl.pallas_call(
        functools.partial(down_kernel, groups, rows, size),
        in_specs=whole(2),
        out_specs=whole(len(groups)),
        out_shape=[jax.ShapeDtypeStruct((group * rows, columns), BF16) for group in groups],
        compiler_params=params(),
        cost_estimate=cost(
            2 * total * depth * columns, 2 * depth * columns + 2 * total * columns
        ),
        name="down",
    )(down_matrix, hidden)


def last_kernel(blocks, members, parts, counts_ref, *refs):
    terms, out_ref = refs[:-1], refs[-1]
    rows = out_ref.shape[0]
    first = lax.axis_index("tp") * rows
    block_rows = members * rows // blocks
    live = picked(counts_ref, first // block_rows) - first % block_rows
    each = len(terms) // parts
    columns = out_ref.shape[1] // parts
    for part in range(parts):
        summed = 0.0
        for term in terms[part * each : (part + 1) * each]:
            summed += term[...].astype(F32)
        row = lax.broadcasted_iota(jnp.int32, summed.shape, 0)
        out_ref[:, part * columns : (part + 1) * columns] = jnp.where(
            row < live, summed, 0.0
        ).astype(BF16)


def last(members, counts, halves):
    terms = [term for half in halves for term in half]
    rows, columns = terms[0].shape
    return pl.pallas_call(
        functools.partial(last_kernel, counts.shape[1], members, len(halves)),
        in_specs=whole(1 + len(terms)),
        out_specs=whole(1)[0],
        out_shape=jax.ShapeDtypeStruct((rows, columns * len(halves)), BF16),
        compiler_params=params(),
        name="last",
    )(counts, *terms)


def add_kernel(starts, *refs):
    out_ref = refs[-1]
    rows = out_ref.shape[0]
    total = 0.0
    for start, ref in zip(starts, refs[:-1], strict=True):
        total += ref[start : start + rows, :].astype(F32)
    out_ref[...] = total.astype(BF16)


def added(rows, *terms):
    starts = [start for start, _ in terms]
    columns = terms[0][1].shape[1]
    return pl.pallas_call(
        functools.partial(add_kernel, starts),
        in_specs=whole(len(terms)),
        out_specs=whole(1)[0],
        out_shape=jax.ShapeDtypeStruct((rows, columns), BF16),
        compiler_params=params(),
        cost_estimate=cost(len(terms) * rows * columns, 2 * rows * columns),
        name="added",
    )(*[term for _, term in terms])


def per_device(
    members,
    tokens,
    gate_matrix,
    up_matrix,
    down_matrix,
    shrink_matrices,
    expand_matrices,
    adapter_per_block,
    block_token_count,
):
    rows = tokens.shape[0]
    span = shrink_matrices.shape[2]
    reach = members // 4
    ring = around(members)

    def step(x):
        return lax.ppermute(x, "tp", ring)

    def cross(x, bit=1):
        return lax.ppermute(x, "tp", crossing(members, bit))

    first = tokens
    own, second = anchor(tokens, cross(tokens))
    shrink = jnp.swapaxes(shrink_matrices, 1, 2)
    other_shrink = cross(shrink)
    pieces, mine, theirs = [own, second], [], []
    for distance in range(1, reach + 1):
        first = step(first)
        mine.append(first)
        theirs.append(cross(first))
        if distance < reach:
            second = step(second)
            mine.append(second)
            theirs.append(cross(second))
    pieces = pieces + mine + theirs

    adapters, counts = adapter_per_block[None], block_token_count[None]
    received = [0] + list(range(2, 2 + len(mine)))
    rank, expand = rank_of(
        adapters,
        members,
        received,
        [pieces[i] for i in received],
        shrink,
        other_shrink,
        expand_matrices,
        theirs[:-1],
    )
    work = [(gate_matrix, 0), (gate_matrix, 1), (up_matrix, 0), (up_matrix, 1)]
    products, aside, after, bit = [], [0, 0], rank, 1
    while bit < members or work:
        if work:
            matrix, part = work.pop(0)
            result, *left = product(
                pieces, matrix, part, 2, after, WEIGHTS[len(products)], aside[part]
            )
            aside[part] = left[0] if left else None
            products.append(result)
        if bit < members:
            after = cross(rank, bit)
            rank = rank + after if bit == 1 else jnp.concatenate([rank, after], axis=0)
            bit *= 2
    products += [x for x in aside if x is not None]
    hidden = finish(products, rank, expand, 2 * span, rows)

    slots = 2 * reach
    groups = [1] * slots + [1] + [2] * (reach - 1) + [1]
    outs = down(hidden, down_matrix, groups, rows)
    keep, give = outs[:slots], outs[slots:]
    came = [cross(x) for x in give]
    first = step(added(rows, (0, keep[0]), (0, came[0])))
    second = None
    for index in range(1, reach):
        more = [] if second is None else [(0, second)]
        second = step(added(rows, (0, keep[2 * index]), (rows, came[index]), *more))
        first = step(added(rows, (0, keep[2 * index - 1]), (0, came[index]), (0, first)))
    return last(members, counts, [[keep[-1], came[-1], first, cross(second)]])


def solution(mesh):
    members = mesh.shape["tp"]
    return jax.shard_map(
        functools.partial(per_device, members),
        mesh=mesh,
        in_specs=(
            P(("rep", "tp"), None),
            P(None, "tp"),
            P(None, "tp"),
            P("tp", None),
            P("rep", None, "tp"),
            P("rep", None, "tp"),
            P("rep"),
            P("rep"),
        ),
        out_specs=P(("rep", "tp"), None),
        check_vma=False,
    )
```

```python
import functools

import jax
import jax.numpy as jnp
from jax import lax
from jax.experimental import pallas as pl
from jax.experimental.pallas import tpu as pltpu
from jax.sharding import PartitionSpec as P

F32 = jnp.float32
BF16 = jnp.bfloat16
VMEM_LIMIT = 8 * 1024 * 1024
WEIGHTS = (6, 6, 6, 6)


def largest_tile(size, limit):
    tile = limit
    while size % tile:
        tile //= 2
    return tile


def params():
    return pltpu.CompilerParams(vmem_limit_bytes=VMEM_LIMIT)


def cost(flops, moved):
    return pl.CostEstimate(flops=flops, bytes_accessed=moved, transcendentals=0)


def ring_of(chips):
    return list(range(0, chips, 2)) + list(range(chips - 1, 0, -2))


def piece_row(device, members, rows, side, distance, half):
    chips = members // 2
    chip = device // 2
    place = jnp.where(chip % 2 == 0, chip // 2, chips - (chip + 1) // 2)
    spot = (place + chips + jnp.where(side == 0, distance, -distance)) % chips
    there = jnp.where(spot < chips // 2, 2 * spot, 2 * (chips - spot) - 1)
    return pl.multiple_of((2 * there + half) * rows, rows)


def arrivals(device, members, rows):
    core, reach = device % 2, members // 4
    places = [(core, 0, core), (core, 0, 1 - core)]
    for side in (core, 1 - core):
        for step in range(1, reach + 1):
            places.append((1 - side, step, side))
            if step < reach:
                places.append((1 - side, step, 1 - side))
    return [piece_row(device, members, rows, *place) for place in places]


def departures(device, members, rows):
    core, reach = device % 2, members // 4
    places = []
    for side in (core, 1 - core):
        places.append((side, reach, side))
        for step in range(reach - 1, 0, -1):
            places += [(side, step, side), (side, step, 1 - side)]
        places.append((side, 0, side))
    return [piece_row(device, members, rows, *place) for place in places]


def around(members):
    ring = ring_of(members // 2)
    size = len(ring)
    pairs = []
    for i in range(size):
        pairs.append((2 * ring[i], 2 * ring[(i + 1) % size]))
        pairs.append((2 * ring[i] + 1, 2 * ring[i - 1] + 1))
    return pairs


def crossing(members, bit):
    return [(i, i ^ bit) for i in range(members)]


def whole(count):
    return [pl.BlockSpec(memory_space=pltpu.VMEM)] * count


FAR = pl.BlockSpec(memory_space=pl.ANY)


def far(x):
    return pltpu.with_memory_space_constraint(x, pltpu.HBM)


def picked(ref, index):
    row = ref[...]
    spots = lax.broadcasted_iota(jnp.int32, row.shape, 1)
    return jnp.sum(jnp.where(spots == index, row, 0))


def anchor_kernel(tokens_ref, passed_in, own_ref, passed_out, sem):
    copy = pltpu.make_async_copy(tokens_ref, own_ref, sem)
    copy.start()
    copy.wait()


def anchor(tokens, passed):
    return pl.pallas_call(
        anchor_kernel,
        in_specs=[FAR, FAR],
        out_specs=whole(1) + [FAR],
        out_shape=[jax.ShapeDtypeStruct(passed.shape, passed.dtype)] * 2,
        input_output_aliases={1: 1},
        scratch_shapes=[pltpu.SemaphoreType.DMA],
        compiler_params=params(),
        cost_estimate=cost(30_000_000_000, 0),
        name="anchor",
    )(far(tokens), passed)


def rank_kernel(members, numbers, ids_ref, expand_ref, own_ref, other_ref, *refs):
    pieces, (out_ref, chosen_ref, scratch, sems) = refs[: len(numbers)], refs[-4:]
    rows = pieces[0].shape[0]
    blocks, span = ids_ref.shape[1], own_ref.shape[1]
    block_rows = members * rows // blocks
    device = lax.axis_index("tp")
    places = arrivals(device, members, rows)
    ids = [picked(ids_ref, b) for b in range(blocks)]
    copies = [
        pltpu.make_async_copy(expand_ref.at[ids[b]], chosen_ref.at[b], sems.at[b])
        for b in range(blocks)
    ]
    for copy in copies:
        copy.start()
    weights = jnp.concatenate([ref[i] for ref in (own_ref, other_ref) for i in ids], axis=0)
    wanted = weights.shape[0]
    slices = max(1, 256 // wanted)
    depth = weights.shape[1] // slices
    spans = [slice(i * depth, (i + 1) * depth) for i in range(slices)]
    lhs = jnp.concatenate([piece[:, cut] for cut in spans for piece in pieces], axis=0)
    rhs = jnp.concatenate([weights[:, cut] for cut in spans], axis=0)
    squares = lax.dot_general(lhs, rhs, (((1,), (1,)), ((), ())), preferred_element_type=F32)
    height = len(pieces) * rows
    found = 0.0
    for i in range(slices):
        found += squares[i * height : (i + 1) * height, i * wanted : (i + 1) * wanted]
    scratch[...] = jnp.zeros_like(scratch)
    for index, number in enumerate(numbers):
        part = found[index * rows : (index + 1) * rows]
        for source in range(2):
            first = source * blocks * span
            value = part[:, first : first + span]
            for b in range(1, blocks):
                columns = part[:, first + b * span : first + (b + 1) * span]
                value = jnp.where(places[number] // block_rows == b, columns, value)
            scratch[source, pl.ds(places[number], rows), :span] = value
    own, other = scratch[0].T[:span], scratch[1].T[:span]
    lower = device % 2 == 0
    out_ref[...] = jnp.concatenate(
        [jnp.where(lower, own, other), jnp.where(lower, other, own)], axis=0
    ).astype(BF16)
    for copy in copies:
        copy.wait()


def rank_of(adapters, members, numbers, pieces, shrink, other, expand, after):
    rows, model = pieces[0].shape
    span = shrink.shape[1]
    total = rows * members
    return pl.pallas_call(
        functools.partial(rank_kernel, members, numbers),
        in_specs=whole(1) + [FAR] + whole(2 + len(pieces)) + [FAR] * len(after),
        out_specs=whole(2),
        out_shape=[
            jax.ShapeDtypeStruct((2 * span, total), BF16),
            jax.ShapeDtypeStruct((adapters.shape[1],) + expand.shape[1:], BF16),
        ],
        scratch_shapes=[
            pltpu.VMEM((2, total, 128), F32),
            pltpu.SemaphoreType.DMA((adapters.shape[1],)),
        ],
        compiler_params=params(),
        cost_estimate=cost(2 * total * model * span * 2, 2 * total * model),
        name="rank",
    )(adapters, far(expand), shrink, other, *pieces, *after)


def product_kernel(first, depth, main, role, w_ref, *refs):
    outs = 1 if role is None else 2
    refs, outs = refs[:-outs], refs[-outs:]
    aside, pieces = (refs[:1], refs[1:-1]) if role == 1 else ((), refs[:-1])
    rows = pieces[0].shape[0]
    places = arrivals(lax.axis_index("tp"), len(pieces), rows)
    lhs = jnp.concatenate([piece[:, first : first + depth] for piece in pieces], axis=0)
    span = slice(first, first + depth)

    def store(out_ref, weights):
        part = jnp.dot(lhs, weights, preferred_element_type=F32)
        for index, place in enumerate(places):
            out_ref[pl.ds(place, rows), :] = part[index * rows : (index + 1) * rows]

    store(outs[0], w_ref[span, :main])
    if role == 0:
        outs[1][...] = w_ref[span, main:]
    elif role == 1:
        store(outs[1], jnp.concatenate([w_ref[span, main:], aside[0][...]], axis=1))


def product(pieces, matrix, part, parts, after, weight, aside):
    rows = pieces[0].shape[0]
    total = rows * len(pieces)
    model, width = matrix.shape
    depth = model // parts
    tail = 128 if width % 256 == 128 else 0
    main = width - tail
    out_shape = [jax.ShapeDtypeStruct((total, main), F32)]
    role, extra = None, []
    if tail and isinstance(aside, int):
        role = 0
        out_shape.append(jax.ShapeDtypeStruct((depth, tail), BF16))
    elif tail:
        role, extra = 1, [aside]
        out_shape.append(jax.ShapeDtypeStruct((total, 2 * tail), F32))
    return pl.pallas_call(
        functools.partial(product_kernel, part * depth, depth, main, role),
        in_specs=whole(len(pieces) + 2 + len(extra)),
        out_specs=whole(len(out_shape)),
        out_shape=out_shape,
        compiler_params=params(),
        cost_estimate=cost(weight * total * depth * width, 2 * depth * (width + total)),
        name="product",
    )(matrix, *extra, *pieces, after)


def finish_kernel(span, piece_rows, *refs):
    *products, rank_ref, expand_ref, out_ref, hidden_ref = refs
    gate_a, gate_b, up_a, up_b, *tails = products
    ranks = rank_ref.shape[0]
    chip = lax.axis_index("tp") // 2
    shape = (ranks, ranks)
    want = lax.broadcasted_iota(jnp.int32, shape, 0)
    have = lax.broadcasted_iota(jnp.int32, shape, 1)
    origin = ((have // span) ^ chip) * span + have % span
    order = jnp.where(want == origin, 1.0, 0.0).astype(BF16)
    rank = jnp.dot(order, rank_ref[...], preferred_element_type=F32).T.astype(BF16)
    half = ranks // 2
    blocks = expand_ref.shape[0]
    rows = hidden_ref.shape[0] // blocks
    main = gate_a.shape[1]
    tail = hidden_ref.shape[1] - main
    for b in range(blocks):
        part = slice(b * rows, (b + 1) * rows)
        expand = expand_ref[b]
        gate = jnp.dot(rank[part, :half], expand[:half], preferred_element_type=F32)
        up = jnp.dot(rank[part, half:], expand[half:], preferred_element_type=F32)
        gates = [gate[:, :main] + gate_a[part] + gate_b[part]]
        ups = [up[:, :main] + up_a[part] + up_b[part]]
        if tail:
            both = tails[0][part] + tails[1][part]
            gates.append(gate[:, main:] + both[:, tail:])
            ups.append(up[:, main:] + both[:, :tail])
        column = 0
        for gate, up in zip(gates, ups, strict=True):
            hidden = (gate / (1.0 + jnp.exp(-gate)) * up).astype(BF16)
            hidden_ref[part, column : column + gate.shape[1]] = hidden
            column += gate.shape[1]
    members = hidden_ref.shape[0] // piece_rows
    for index, place in enumerate(departures(lax.axis_index("tp"), members, piece_rows)):
        out_ref[index * piece_rows : (index + 1) * piece_rows, :] = hidden_ref[
            pl.ds(place, piece_rows), :
        ]


def finish(products, rank, expand, span, piece_rows):
    total, width = products[0].shape[0], expand.shape[2]
    return pl.pallas_call(
        functools.partial(finish_kernel, span, piece_rows),
        in_specs=whole(len(products) + 2),
        out_specs=whole(1)[0],
        out_shape=jax.ShapeDtypeStruct((total, width), BF16),
        scratch_shapes=[pltpu.VMEM((total, width), BF16)],
        compiler_params=params(),
        name="finish",
    )(*products, rank, expand)


def down_kernel(groups, rows, size, w_ref, hidden_ref, *outs):
    hidden = hidden_ref[...]
    for start in range(0, w_ref.shape[1], size):
        columns = slice(start, start + size)
        part = jnp.dot(hidden, w_ref[:, columns], preferred_element_type=F32)
        at = 0
        for out, group in zip(outs, groups, strict=True):
            out[:, columns] = part[at : at + group * rows].astype(BF16)
            at += group * rows


def down(hidden, down_matrix, groups, rows):
    total, depth = hidden.shape
    columns = down_matrix.shape[1]
    size = min(2048, columns)
    return pl.pallas_call(
        functools.partial(down_kernel, groups, rows, size),
        in_specs=whole(2),
        out_specs=whole(len(groups)),
        out_shape=[jax.ShapeDtypeStruct((group * rows, columns), BF16) for group in groups],
        compiler_params=params(),
        cost_estimate=cost(
            2 * total * depth * columns, 2 * depth * columns + 2 * total * columns
        ),
        name="down",
    )(down_matrix, hidden)


def last_kernel(blocks, members, parts, counts_ref, *refs):
    terms, out_ref = refs[:-1], refs[-1]
    rows = out_ref.shape[0]
    first = lax.axis_index("tp") * rows
    block_rows = members * rows // blocks
    live = picked(counts_ref, first // block_rows) - first % block_rows
    each = len(terms) // parts
    columns = out_ref.shape[1] // parts
    for part in range(parts):
        summed = 0.0
        for term in terms[part * each : (part + 1) * each]:
            summed += term[...].astype(F32)
        row = lax.broadcasted_iota(jnp.int32, summed.shape, 0)
        out_ref[:, part * columns : (part + 1) * columns] = jnp.where(
            row < live, summed, 0.0
        ).astype(BF16)


def last(members, counts, halves):
    terms = [term for half in halves for term in half]
    rows, columns = terms[0].shape
    return pl.pallas_call(
        functools.partial(last_kernel, counts.shape[1], members, len(halves)),
        in_specs=whole(1 + len(terms)),
        out_specs=whole(1)[0],
        out_shape=jax.ShapeDtypeStruct((rows, columns * len(halves)), BF16),
        compiler_params=params(),
        name="last",
    )(counts, *terms)


def add_kernel(starts, *refs):
    out_ref = refs[-1]
    rows = out_ref.shape[0]
    total = 0.0
    for start, ref in zip(starts, refs[:-1], strict=True):
        total += ref[start : start + rows, :].astype(F32)
    out_ref[...] = total.astype(BF16)


def added(rows, *terms):
    starts = [start for start, _ in terms]
    columns = terms[0][1].shape[1]
    return pl.pallas_call(
        functools.partial(add_kernel, starts),
        in_specs=whole(len(terms)),
        out_specs=whole(1)[0],
        out_shape=jax.ShapeDtypeStruct((rows, columns), BF16),
        compiler_params=params(),
        cost_estimate=cost(len(terms) * rows * columns, 2 * rows * columns),
        name="added",
    )(*[term for _, term in terms])


def per_device(
    members,
    tokens,
    gate_matrix,
    up_matrix,
    down_matrix,
    shrink_matrices,
    expand_matrices,
    adapter_per_block,
    block_token_count,
):
    rows = tokens.shape[0]
    span = shrink_matrices.shape[2]
    reach = members // 4
    ring = around(members)

    def step(x):
        return lax.ppermute(x, "tp", ring)

    def cross(x, bit=1):
        return lax.ppermute(x, "tp", crossing(members, bit))

    first = tokens
    own, second = anchor(tokens, cross(tokens))
    shrink = jnp.swapaxes(shrink_matrices, 1, 2)
    other_shrink = cross(shrink)
    pieces, mine, theirs = [own, second], [], []
    for distance in range(1, reach + 1):
        first = step(first)
        mine.append(first)
        theirs.append(cross(first))
        if distance < reach:
            second = step(second)
            mine.append(second)
            theirs.append(cross(second))
    pieces = pieces + mine + theirs

    adapters, counts = adapter_per_block[None], block_token_count[None]
    received = [0] + list(range(2, 2 + len(mine)))
    rank, expand = rank_of(
        adapters,
        members,
        received,
        [pieces[i] for i in received],
        shrink,
        other_shrink,
        expand_matrices,
        theirs[:-1],
    )
    work = [(gate_matrix, 0), (gate_matrix, 1), (up_matrix, 0), (up_matrix, 1)]
    products, aside, after, bit = [], [0, 0], rank, 1
    while bit < members or work:
        if work:
            matrix, part = work.pop(0)
            result, *left = product(
                pieces, matrix, part, 2, after, WEIGHTS[len(products)], aside[part]
            )
            aside[part] = left[0] if left else None
            products.append(result)
        if bit < members:
            after = cross(rank, bit)
            rank = rank + after if bit == 1 else jnp.concatenate([rank, after], axis=0)
            bit *= 2
    products += [x for x in aside if x is not None]
    hidden = finish(products, rank, expand, 2 * span, rows)

    slots = 2 * reach
    groups = [1] * slots + [1] + [2] * (reach - 1) + [1]
    outs = down(hidden, down_matrix, groups, rows)
    keep, give = outs[:slots], outs[slots:]
    came = [cross(x) for x in give]
    first = step(added(rows, (0, keep[0]), (0, came[0])))
    second = None
    for index in range(1, reach):
        more = [] if second is None else [(0, second)]
        second = step(added(rows, (0, keep[2 * index]), (rows, came[index]), *more))
        first = step(added(rows, (0, keep[2 * index - 1]), (0, came[index]), (0, first)))
    return last(members, counts, [[keep[-1], came[-1], first, cross(second)]])


def solution(mesh):
    members = mesh.shape["tp"]
    return jax.shard_map(
        functools.partial(per_device, members),
        mesh=mesh,
        in_specs=(
            P(("rep", "tp"), None),
            P(None, "tp"),
            P(None, "tp"),
            P("tp", None),
            P("rep", None, "tp"),
            P("rep", None, "tp"),
            P("rep"),
            P("rep"),
        ),
        out_specs=P(("rep", "tp"), None),
        check_vma=False,
    )
```

```python
import functools

import jax
import jax.numpy as jnp
from jax import lax
from jax.experimental import pallas as pl
from jax.experimental.pallas import tpu as pltpu
from jax.sharding import PartitionSpec as P

F32 = jnp.float32
BF16 = jnp.bfloat16
VMEM_LIMIT = 8 * 1024 * 1024
WEIGHTS = (6, 6, 6, 6)


def largest_tile(size, limit):
    tile = limit
    while size % tile:
        tile //= 2
    return tile


def params():
    return pltpu.CompilerParams(vmem_limit_bytes=VMEM_LIMIT)


def cost(flops, moved):
    return pl.CostEstimate(flops=flops, bytes_accessed=moved, transcendentals=0)


def ring_of(chips):
    return list(range(0, chips, 2)) + list(range(chips - 1, 0, -2))


def piece_row(device, members, rows, side, distance, half):
    chips = members // 2
    chip = device // 2
    place = jnp.where(chip % 2 == 0, chip // 2, chips - (chip + 1) // 2)
    spot = (place + chips + jnp.where(side == 0, distance, -distance)) % chips
    there = jnp.where(spot < chips // 2, 2 * spot, 2 * (chips - spot) - 1)
    return pl.multiple_of((2 * there + half) * rows, rows)


def arrivals(device, members, rows):
    core, reach = device % 2, members // 4
    places = [(core, 0, core), (core, 0, 1 - core)]
    for side in (core, 1 - core):
        for step in range(1, reach + 1):
            places.append((1 - side, step, side))
            if step < reach:
                places.append((1 - side, step, 1 - side))
    return [piece_row(device, members, rows, *place) for place in places]


def departures(device, members, rows):
    core, reach = device % 2, members // 4
    places = []
    for side in (core, 1 - core):
        places.append((side, reach, side))
        for step in range(reach - 1, 0, -1):
            places += [(side, step, side), (side, step, 1 - side)]
        places.append((side, 0, side))
    return [piece_row(device, members, rows, *place) for place in places]


def around(members):
    ring = ring_of(members // 2)
    size = len(ring)
    pairs = []
    for i in range(size):
        pairs.append((2 * ring[i], 2 * ring[(i + 1) % size]))
        pairs.append((2 * ring[i] + 1, 2 * ring[i - 1] + 1))
    return pairs


def crossing(members, bit):
    return [(i, i ^ bit) for i in range(members)]


def whole(count):
    return [pl.BlockSpec(memory_space=pltpu.VMEM)] * count


FAR = pl.BlockSpec(memory_space=pl.ANY)


def far(x):
    return pltpu.with_memory_space_constraint(x, pltpu.HBM)


def picked(ref, index):
    row = ref[...]
    spots = lax.broadcasted_iota(jnp.int32, row.shape, 1)
    return jnp.sum(jnp.where(spots == index, row, 0))


def anchor_kernel(tokens_ref, passed_in, own_ref, passed_out, sem):
    copy = pltpu.make_async_copy(tokens_ref, own_ref, sem)
    copy.start()
    copy.wait()


def anchor(tokens, passed):
    return pl.pallas_call(
        anchor_kernel,
        in_specs=[FAR, FAR],
        out_specs=whole(1) + [FAR],
        out_shape=[jax.ShapeDtypeStruct(passed.shape, passed.dtype)] * 2,
        input_output_aliases={1: 1},
        scratch_shapes=[pltpu.SemaphoreType.DMA],
        compiler_params=params(),
        cost_estimate=cost(30_000_000_000, 0),
        name="anchor",
    )(far(tokens), passed)


def rank_kernel(members, numbers, ids_ref, own_ref, other_ref, *refs):
    pieces, (out_ref, scratch) = refs[: len(numbers)], refs[-2:]
    rows = pieces[0].shape[0]
    blocks, span = ids_ref.shape[1], own_ref.shape[1]
    block_rows = members * rows // blocks
    device = lax.axis_index("tp")
    places = arrivals(device, members, rows)
    ids = [picked(ids_ref, b) for b in range(blocks)]
    weights = jnp.concatenate([ref[i] for ref in (own_ref, other_ref) for i in ids], axis=0)
    wanted = weights.shape[0]
    slices = max(1, 256 // wanted)
    depth = weights.shape[1] // slices
    spans = [slice(i * depth, (i + 1) * depth) for i in range(slices)]
    lhs = jnp.concatenate([piece[:, cut] for cut in spans for piece in pieces], axis=0)
    rhs = jnp.concatenate([weights[:, cut] for cut in spans], axis=0)
    squares = lax.dot_general(lhs, rhs, (((1,), (1,)), ((), ())), preferred_element_type=F32)
    height = len(pieces) * rows
    found = 0.0
    for i in range(slices):
        found += squares[i * height : (i + 1) * height, i * wanted : (i + 1) * wanted]
    scratch[...] = jnp.zeros_like(scratch)
    for index, number in enumerate(numbers):
        part = found[index * rows : (index + 1) * rows]
        for source in range(2):
            first = source * blocks * span
            value = part[:, first : first + span]
            for b in range(1, blocks):
                columns = part[:, first + b * span : first + (b + 1) * span]
                value = jnp.where(places[number] // block_rows == b, columns, value)
            scratch[source, pl.ds(places[number], rows), :span] = value
    own, other = scratch[0].T[:span], scratch[1].T[:span]
    lower = device % 2 == 0
    out_ref[...] = jnp.concatenate(
        [jnp.where(lower, own, other), jnp.where(lower, other, own)], axis=0
    ).astype(BF16)


def rank_of(adapters, members, numbers, pieces, shrink, other, after):
    rows, model = pieces[0].shape
    span = shrink.shape[1]
    total = rows * members
    return pl.pallas_call(
        functools.partial(rank_kernel, members, numbers),
        in_specs=whole(3 + len(pieces)) + [FAR] * len(after),
        out_specs=whole(1)[0],
        out_shape=jax.ShapeDtypeStruct((2 * span, total), BF16),
        scratch_shapes=[pltpu.VMEM((2, total, 128), F32)],
        compiler_params=params(),
        cost_estimate=cost(2 * total * model * span * 2, 2 * total * model),
        name="rank",
    )(adapters, shrink, other, *pieces, *after)


def product_kernel(first, depth, main, role, count, fetch, w_ref, *refs):
    aside, refs = refs[: role or 0], refs[role or 0 :]
    pieces, refs = refs[:count], refs[count + 1 :]
    copies = []
    if fetch:
        ids_ref, expand_ref, *refs, chosen_ref, sems = refs
        for b in range(ids_ref.shape[1]):
            source = expand_ref.at[picked(ids_ref, b)]
            copies.append(pltpu.make_async_copy(source, chosen_ref.at[b], sems.at[b]))
    for copy in copies:
        copy.start()
    outs = refs
    rows = pieces[0].shape[0]
    places = arrivals(lax.axis_index("tp"), len(pieces), rows)
    lhs = jnp.concatenate([piece[:, first : first + depth] for piece in pieces], axis=0)
    span = slice(first, first + depth)

    def store(out_ref, weights):
        part = jnp.dot(lhs, weights, preferred_element_type=F32)
        for index, place in enumerate(places):
            out_ref[pl.ds(place, rows), :] = part[index * rows : (index + 1) * rows]

    store(outs[0], w_ref[span, :main])
    if role == 0:
        outs[1][...] = w_ref[span, main:]
    elif role == 1:
        store(outs[1], jnp.concatenate([w_ref[span, main:], aside[0][...]], axis=1))
    for copy in copies:
        copy.wait()


def product(pieces, matrix, part, parts, after, weight, aside, fetch=None):
    rows = pieces[0].shape[0]
    total = rows * len(pieces)
    model, width = matrix.shape
    depth = model // parts
    tail = 128 if width % 256 == 128 else 0
    main = width - tail
    out_shape = [jax.ShapeDtypeStruct((total, main), F32)]
    role, extra = None, []
    if tail and isinstance(aside, int):
        role = 0
        out_shape.append(jax.ShapeDtypeStruct((depth, tail), BF16))
    elif tail:
        role, extra = 1, [aside]
        out_shape.append(jax.ShapeDtypeStruct((total, 2 * tail), F32))
    specs, scratch, fetched = whole(len(pieces) + 2 + len(extra)), [], []
    if fetch is not None:
        adapters, expand = fetch
        blocks = adapters.shape[1]
        fetched = [adapters, far(expand)]
        specs += whole(1) + [FAR]
        out_shape.append(jax.ShapeDtypeStruct((blocks,) + expand.shape[1:], BF16))
        scratch.append(pltpu.SemaphoreType.DMA((blocks,)))
    return pl.pallas_call(
        functools.partial(
            product_kernel, part * depth, depth, main, role, len(pieces), fetch is not None
        ),
        in_specs=specs,
        out_specs=whole(len(out_shape)),
        out_shape=out_shape,
        scratch_shapes=scratch,
        compiler_params=params(),
        cost_estimate=cost(weight * total * depth * width, 2 * depth * (width + total)),
        name="product",
    )(matrix, *extra, *pieces, after, *fetched)


def finish_kernel(span, piece_rows, *refs):
    *products, rank_ref, expand_ref, out_ref, hidden_ref = refs
    gate_a, gate_b, up_a, up_b, *tails = products
    ranks = rank_ref.shape[0]
    chip = lax.axis_index("tp") // 2
    shape = (ranks, ranks)
    want = lax.broadcasted_iota(jnp.int32, shape, 0)
    have = lax.broadcasted_iota(jnp.int32, shape, 1)
    origin = ((have // span) ^ chip) * span + have % span
    order = jnp.where(want == origin, 1.0, 0.0).astype(BF16)
    rank = jnp.dot(order, rank_ref[...], preferred_element_type=F32).T.astype(BF16)
    half = ranks // 2
    blocks = expand_ref.shape[0]
    rows = hidden_ref.shape[0] // blocks
    main = gate_a.shape[1]
    tail = hidden_ref.shape[1] - main
    for b in range(blocks):
        part = slice(b * rows, (b + 1) * rows)
        expand = expand_ref[b]
        gate = jnp.dot(rank[part, :half], expand[:half], preferred_element_type=F32)
        up = jnp.dot(rank[part, half:], expand[half:], preferred_element_type=F32)
        gates = [gate[:, :main] + gate_a[part] + gate_b[part]]
        ups = [up[:, :main] + up_a[part] + up_b[part]]
        if tail:
            both = tails[0][part] + tails[1][part]
            gates.append(gate[:, main:] + both[:, tail:])
            ups.append(up[:, main:] + both[:, :tail])
        column = 0
        for gate, up in zip(gates, ups, strict=True):
            hidden = (gate / (1.0 + jnp.exp(-gate)) * up).astype(BF16)
            hidden_ref[part, column : column + gate.shape[1]] = hidden
            column += gate.shape[1]
    members = hidden_ref.shape[0] // piece_rows
    for index, place in enumerate(departures(lax.axis_index("tp"), members, piece_rows)):
        out_ref[index * piece_rows : (index + 1) * piece_rows, :] = hidden_ref[
            pl.ds(place, piece_rows), :
        ]


def finish(products, rank, expand, span, piece_rows):
    total, width = products[0].shape[0], expand.shape[2]
    return pl.pallas_call(
        functools.partial(finish_kernel, span, piece_rows),
        in_specs=whole(len(products) + 2),
        out_specs=whole(1)[0],
        out_shape=jax.ShapeDtypeStruct((total, width), BF16),
        scratch_shapes=[pltpu.VMEM((total, width), BF16)],
        compiler_params=params(),
        name="finish",
    )(*products, rank, expand)


def down_kernel(groups, rows, size, w_ref, hidden_ref, *outs):
    hidden = hidden_ref[...]
    for start in range(0, w_ref.shape[1], size):
        columns = slice(start, start + size)
        part = jnp.dot(hidden, w_ref[:, columns], preferred_element_type=F32)
        at = 0
        for out, group in zip(outs, groups, strict=True):
            out[:, columns] = part[at : at + group * rows].astype(BF16)
            at += group * rows


def down(hidden, down_matrix, groups, rows):
    total, depth = hidden.shape
    columns = down_matrix.shape[1]
    size = min(2048, columns)
    return pl.pallas_call(
        functools.partial(down_kernel, groups, rows, size),
        in_specs=whole(2),
        out_specs=whole(len(groups)),
        out_shape=[jax.ShapeDtypeStruct((group * rows, columns), BF16) for group in groups],
        compiler_params=params(),
        cost_estimate=cost(
            2 * total * depth * columns, 2 * depth * columns + 2 * total * columns
        ),
        name="down",
    )(down_matrix, hidden)


def last_kernel(blocks, members, parts, counts_ref, *refs):
    terms, out_ref = refs[:-1], refs[-1]
    rows = out_ref.shape[0]
    first = lax.axis_index("tp") * rows
    block_rows = members * rows // blocks
    live = picked(counts_ref, first // block_rows) - first % block_rows
    each = len(terms) // parts
    columns = out_ref.shape[1] // parts
    for part in range(parts):
        summed = 0.0
        for term in terms[part * each : (part + 1) * each]:
            summed += term[...].astype(F32)
        row = lax.broadcasted_iota(jnp.int32, summed.shape, 0)
        out_ref[:, part * columns : (part + 1) * columns] = jnp.where(
            row < live, summed, 0.0
        ).astype(BF16)


def last(members, counts, halves):
    terms = [term for half in halves for term in half]
    rows, columns = terms[0].shape
    return pl.pallas_call(
        functools.partial(last_kernel, counts.shape[1], members, len(halves)),
        in_specs=whole(1 + len(terms)),
        out_specs=whole(1)[0],
        out_shape=jax.ShapeDtypeStruct((rows, columns * len(halves)), BF16),
        compiler_params=params(),
        name="last",
    )(counts, *terms)


def add_kernel(starts, *refs):
    out_ref = refs[-1]
    rows = out_ref.shape[0]
    total = 0.0
    for start, ref in zip(starts, refs[:-1], strict=True):
        total += ref[start : start + rows, :].astype(F32)
    out_ref[...] = total.astype(BF16)


def added(rows, *terms):
    starts = [start for start, _ in terms]
    columns = terms[0][1].shape[1]
    return pl.pallas_call(
        functools.partial(add_kernel, starts),
        in_specs=whole(len(terms)),
        out_specs=whole(1)[0],
        out_shape=jax.ShapeDtypeStruct((rows, columns), BF16),
        compiler_params=params(),
        cost_estimate=cost(len(terms) * rows * columns, 2 * rows * columns),
        name="added",
    )(*[term for _, term in terms])


def per_device(
    members,
    tokens,
    gate_matrix,
    up_matrix,
    down_matrix,
    shrink_matrices,
    expand_matrices,
    adapter_per_block,
    block_token_count,
):
    rows = tokens.shape[0]
    span = shrink_matrices.shape[2]
    reach = members // 4
    ring = around(members)

    def step(x):
        return lax.ppermute(x, "tp", ring)

    def cross(x, bit=1):
        return lax.ppermute(x, "tp", crossing(members, bit))

    first = tokens
    own, second = anchor(tokens, cross(tokens))
    shrink = jnp.swapaxes(shrink_matrices, 1, 2)
    other_shrink = cross(shrink)
    pieces, mine, theirs = [own, second], [], []
    for distance in range(1, reach + 1):
        first = step(first)
        mine.append(first)
        theirs.append(cross(first))
        if distance < reach:
            second = step(second)
            mine.append(second)
            theirs.append(cross(second))
    pieces = pieces + mine + theirs

    adapters, counts = adapter_per_block[None], block_token_count[None]
    received = [0] + list(range(2, 2 + len(mine)))
    rank = rank_of(
        adapters,
        members,
        received,
        [pieces[i] for i in received],
        shrink,
        other_shrink,
        theirs[:-1],
    )
    work = [(gate_matrix, 0), (gate_matrix, 1), (up_matrix, 0), (up_matrix, 1)]
    products, aside, after, bit = [], [0, 0], rank, 1
    while bit < members or work:
        if work:
            matrix, part = work.pop(0)
            fetch = None if products else (adapters, expand_matrices)
            result, *left = product(
                pieces, matrix, part, 2, after, WEIGHTS[len(products)], aside[part], fetch
            )
            if fetch is not None:
                expand = left.pop()
            aside[part] = left[0] if left else None
            products.append(result)
        if bit < members:
            after = cross(rank, bit)
            rank = rank + after if bit == 1 else jnp.concatenate([rank, after], axis=0)
            bit *= 2
    products += [x for x in aside if x is not None]
    hidden = finish(products, rank, expand, 2 * span, rows)

    slots = 2 * reach
    groups = [1] * slots + [1] + [2] * (reach - 1) + [1]
    outs = down(hidden, down_matrix, groups, rows)
    keep, give = outs[:slots], outs[slots:]
    came = [cross(x) for x in give]
    first = step(added(rows, (0, keep[0]), (0, came[0])))
    second = None
    for index in range(1, reach):
        more = [] if second is None else [(0, second)]
        second = step(added(rows, (0, keep[2 * index]), (rows, came[index]), *more))
        first = step(added(rows, (0, keep[2 * index - 1]), (0, came[index]), (0, first)))
    return last(members, counts, [[keep[-1], came[-1], first, cross(second)]])


def solution(mesh):
    members = mesh.shape["tp"]
    return jax.shard_map(
        functools.partial(per_device, members),
        mesh=mesh,
        in_specs=(
            P(("rep", "tp"), None),
            P(None, "tp"),
            P(None, "tp"),
            P("tp", None),
            P("rep", None, "tp"),
            P("rep", None, "tp"),
            P("rep"),
            P("rep"),
        ),
        out_specs=P(("rep", "tp"), None),
        check_vma=False,
    )
```

```python
import functools

import jax
import jax.numpy as jnp
from jax import lax
from jax.experimental import pallas as pl
from jax.experimental.pallas import tpu as pltpu
from jax.sharding import PartitionSpec as P

F32 = jnp.float32
BF16 = jnp.bfloat16
VMEM_LIMIT = 8 * 1024 * 1024
WEIGHTS = (6, 6, 6, 6)


def largest_tile(size, limit):
    tile = limit
    while size % tile:
        tile //= 2
    return tile


def params():
    return pltpu.CompilerParams(vmem_limit_bytes=VMEM_LIMIT)


def cost(flops, moved):
    return pl.CostEstimate(flops=flops, bytes_accessed=moved, transcendentals=0)


def ring_of(chips):
    return list(range(0, chips, 2)) + list(range(chips - 1, 0, -2))


def piece_row(device, members, rows, side, distance, half):
    chips = members // 2
    chip = device // 2
    place = jnp.where(chip % 2 == 0, chip // 2, chips - (chip + 1) // 2)
    spot = (place + chips + jnp.where(side == 0, distance, -distance)) % chips
    there = jnp.where(spot < chips // 2, 2 * spot, 2 * (chips - spot) - 1)
    return pl.multiple_of((2 * there + half) * rows, rows)


def arrivals(device, members, rows):
    core, reach = device % 2, members // 4
    places = [(core, 0, core), (core, 0, 1 - core)]
    for side in (core, 1 - core):
        for step in range(1, reach + 1):
            places.append((1 - side, step, side))
            if step < reach:
                places.append((1 - side, step, 1 - side))
    return [piece_row(device, members, rows, *place) for place in places]


def departures(device, members, rows):
    core, reach = device % 2, members // 4
    places = []
    for side in (core, 1 - core):
        places.append((side, reach, side))
        for step in range(reach - 1, 0, -1):
            places += [(side, step, side), (side, step, 1 - side)]
        places.append((side, 0, side))
    return [piece_row(device, members, rows, *place) for place in places]


def around(members):
    ring = ring_of(members // 2)
    size = len(ring)
    pairs = []
    for i in range(size):
        pairs.append((2 * ring[i], 2 * ring[(i + 1) % size]))
        pairs.append((2 * ring[i] + 1, 2 * ring[i - 1] + 1))
    return pairs


def crossing(members, bit):
    return [(i, i ^ bit) for i in range(members)]


def whole(count):
    return [pl.BlockSpec(memory_space=pltpu.VMEM)] * count


FAR = pl.BlockSpec(memory_space=pl.ANY)


def far(x):
    return pltpu.with_memory_space_constraint(x, pltpu.HBM)


def picked(ref, index):
    row = ref[...]
    spots = lax.broadcasted_iota(jnp.int32, row.shape, 1)
    return jnp.sum(jnp.where(spots == index, row, 0))


def anchor_kernel(tokens_ref, passed_in, own_ref, passed_out, sem):
    copy = pltpu.make_async_copy(tokens_ref, own_ref, sem)
    copy.start()
    copy.wait()


def anchor(tokens, passed):
    return pl.pallas_call(
        anchor_kernel,
        in_specs=[FAR, FAR],
        out_specs=whole(1) + [FAR],
        out_shape=[jax.ShapeDtypeStruct(passed.shape, passed.dtype)] * 2,
        input_output_aliases={1: 1},
        scratch_shapes=[pltpu.SemaphoreType.DMA],
        compiler_params=params(),
        cost_estimate=cost(30_000_000_000, 0),
        name="anchor",
    )(far(tokens), passed)


def tie_kernel(x_ref, after_ref, out_ref):
    del x_ref, after_ref, out_ref


def tie(x, after):
    return pl.pallas_call(
        tie_kernel,
        in_specs=[FAR, FAR],
        out_specs=FAR,
        out_shape=jax.ShapeDtypeStruct(x.shape, x.dtype),
        input_output_aliases={0: 0},
        compiler_params=params(),
        name="tie",
    )(x, after)


def rank_kernel(members, numbers, ids_ref, expand_ref, own_ref, other_ref, *refs):
    pieces, (out_ref, chosen_ref, scratch, sems) = refs[: len(numbers)], refs[-4:]
    rows = pieces[0].shape[0]
    blocks, span = ids_ref.shape[1], own_ref.shape[1]
    block_rows = members * rows // blocks
    device = lax.axis_index("tp")
    places = arrivals(device, members, rows)
    ids = [picked(ids_ref, b) for b in range(blocks)]
    copies = [
        pltpu.make_async_copy(expand_ref.at[ids[b]], chosen_ref.at[b], sems.at[b])
        for b in range(blocks)
    ]
    for copy in copies:
        copy.start()
    weights = jnp.concatenate([ref[i] for ref in (own_ref, other_ref) for i in ids], axis=0)
    wanted = weights.shape[0]
    slices = max(1, 256 // wanted)
    depth = weights.shape[1] // slices
    spans = [slice(i * depth, (i + 1) * depth) for i in range(slices)]
    lhs = jnp.concatenate([piece[:, cut] for cut in spans for piece in pieces], axis=0)
    rhs = jnp.concatenate([weights[:, cut] for cut in spans], axis=0)
    squares = lax.dot_general(lhs, rhs, (((1,), (1,)), ((), ())), preferred_element_type=F32)
    height = len(pieces) * rows
    found = 0.0
    for i in range(slices):
        found += squares[i * height : (i + 1) * height, i * wanted : (i + 1) * wanted]
    scratch[...] = jnp.zeros_like(scratch)
    for index, number in enumerate(numbers):
        part = found[index * rows : (index + 1) * rows]
        for source in range(2):
            first = source * blocks * span
            value = part[:, first : first + span]
            for b in range(1, blocks):
                columns = part[:, first + b * span : first + (b + 1) * span]
                value = jnp.where(places[number] // block_rows == b, columns, value)
            scratch[source, pl.ds(places[number], rows), :span] = value
    own, other = scratch[0].T[:span], scratch[1].T[:span]
    lower = device % 2 == 0
    out_ref[...] = jnp.concatenate(
        [jnp.where(lower, own, other), jnp.where(lower, other, own)], axis=0
    ).astype(BF16)
    for copy in copies:
        copy.wait()


def rank_of(adapters, members, numbers, pieces, shrink, other, expand, after):
    rows, model = pieces[0].shape
    span = shrink.shape[1]
    total = rows * members
    return pl.pallas_call(
        functools.partial(rank_kernel, members, numbers),
        in_specs=whole(1) + [FAR] + whole(2 + len(pieces)) + [FAR] * len(after),
        out_specs=whole(2),
        out_shape=[
            jax.ShapeDtypeStruct((2 * span, total), BF16),
            jax.ShapeDtypeStruct((adapters.shape[1],) + expand.shape[1:], BF16),
        ],
        scratch_shapes=[
            pltpu.VMEM((2, total, 128), F32),
            pltpu.SemaphoreType.DMA((adapters.shape[1],)),
        ],
        compiler_params=params(),
        cost_estimate=cost(2 * total * model * span * 2, 2 * total * model),
        name="rank",
    )(adapters, far(expand), shrink, other, *pieces, *after)


def product_kernel(first, depth, main, role, w_ref, *refs):
    outs = 1 if role is None else 2
    refs, outs = refs[:-outs], refs[-outs:]
    aside, pieces = (refs[:1], refs[1:-1]) if role == 1 else ((), refs[:-1])
    rows = pieces[0].shape[0]
    places = arrivals(lax.axis_index("tp"), len(pieces), rows)
    lhs = jnp.concatenate([piece[:, first : first + depth] for piece in pieces], axis=0)
    span = slice(first, first + depth)

    def store(out_ref, weights):
        part = jnp.dot(lhs, weights, preferred_element_type=F32)
        for index, place in enumerate(places):
            out_ref[pl.ds(place, rows), :] = part[index * rows : (index + 1) * rows]

    store(outs[0], w_ref[span, :main])
    if role == 0:
        outs[1][...] = w_ref[span, main:]
    elif role == 1:
        store(outs[1], jnp.concatenate([w_ref[span, main:], aside[0][...]], axis=1))


def product(pieces, matrix, part, parts, after, weight, aside):
    rows = pieces[0].shape[0]
    total = rows * len(pieces)
    model, width = matrix.shape
    depth = model // parts
    tail = 128 if width % 256 == 128 else 0
    main = width - tail
    out_shape = [jax.ShapeDtypeStruct((total, main), F32)]
    role, extra = None, []
    if tail and isinstance(aside, int):
        role = 0
        out_shape.append(jax.ShapeDtypeStruct((depth, tail), BF16))
    elif tail:
        role, extra = 1, [aside]
        out_shape.append(jax.ShapeDtypeStruct((total, 2 * tail), F32))
    return pl.pallas_call(
        functools.partial(product_kernel, part * depth, depth, main, role),
        in_specs=whole(len(pieces) + 2 + len(extra)),
        out_specs=whole(len(out_shape)),
        out_shape=out_shape,
        compiler_params=params(),
        cost_estimate=cost(weight * total * depth * width, 2 * depth * (width + total)),
        name="product",
    )(matrix, *extra, *pieces, after)


def finish_kernel(span, piece_rows, *refs):
    *products, rank_ref, expand_ref, out_ref, hidden_ref = refs
    gate_a, gate_b, up_a, up_b, *tails = products
    ranks = rank_ref.shape[0]
    chip = lax.axis_index("tp") // 2
    shape = (ranks, ranks)
    want = lax.broadcasted_iota(jnp.int32, shape, 0)
    have = lax.broadcasted_iota(jnp.int32, shape, 1)
    origin = ((have // span) ^ chip) * span + have % span
    order = jnp.where(want == origin, 1.0, 0.0).astype(BF16)
    rank = jnp.dot(order, rank_ref[...], preferred_element_type=F32).T.astype(BF16)
    half = ranks // 2
    blocks = expand_ref.shape[0]
    rows = hidden_ref.shape[0] // blocks
    main = gate_a.shape[1]
    tail = hidden_ref.shape[1] - main
    for b in range(blocks):
        part = slice(b * rows, (b + 1) * rows)
        expand = expand_ref[b]
        gate = jnp.dot(rank[part, :half], expand[:half], preferred_element_type=F32)
        up = jnp.dot(rank[part, half:], expand[half:], preferred_element_type=F32)
        gates = [gate[:, :main] + gate_a[part] + gate_b[part]]
        ups = [up[:, :main] + up_a[part] + up_b[part]]
        if tail:
            both = tails[0][part] + tails[1][part]
            gates.append(gate[:, main:] + both[:, tail:])
            ups.append(up[:, main:] + both[:, :tail])
        column = 0
        for gate, up in zip(gates, ups, strict=True):
            hidden = (gate / (1.0 + jnp.exp(-gate)) * up).astype(BF16)
            hidden_ref[part, column : column + gate.shape[1]] = hidden
            column += gate.shape[1]
    members = hidden_ref.shape[0] // piece_rows
    for index, place in enumerate(departures(lax.axis_index("tp"), members, piece_rows)):
        out_ref[index * piece_rows : (index + 1) * piece_rows, :] = hidden_ref[
            pl.ds(place, piece_rows), :
        ]


def finish(products, rank, expand, span, piece_rows):
    total, width = products[0].shape[0], expand.shape[2]
    return pl.pallas_call(
        functools.partial(finish_kernel, span, piece_rows),
        in_specs=whole(len(products) + 2),
        out_specs=whole(1)[0],
        out_shape=jax.ShapeDtypeStruct((total, width), BF16),
        scratch_shapes=[pltpu.VMEM((total, width), BF16)],
        compiler_params=params(),
        name="finish",
    )(*products, rank, expand)


def down_kernel(groups, rows, size, w_ref, hidden_ref, *outs):
    hidden = hidden_ref[...]
    for start in range(0, w_ref.shape[1], size):
        columns = slice(start, start + size)
        part = jnp.dot(hidden, w_ref[:, columns], preferred_element_type=F32)
        at = 0
        for out, group in zip(outs, groups, strict=True):
            out[:, columns] = part[at : at + group * rows].astype(BF16)
            at += group * rows


def down(hidden, down_matrix, groups, rows):
    total, depth = hidden.shape
    columns = down_matrix.shape[1]
    size = min(2048, columns)
    return pl.pallas_call(
        functools.partial(down_kernel, groups, rows, size),
        in_specs=whole(2),
        out_specs=whole(len(groups)),
        out_shape=[jax.ShapeDtypeStruct((group * rows, columns), BF16) for group in groups],
        compiler_params=params(),
        cost_estimate=cost(
            2 * total * depth * columns, 2 * depth * columns + 2 * total * columns
        ),
        name="down",
    )(down_matrix, hidden)


def last_kernel(blocks, members, parts, counts_ref, *refs):
    terms, out_ref = refs[:-1], refs[-1]
    rows = out_ref.shape[0]
    first = lax.axis_index("tp") * rows
    block_rows = members * rows // blocks
    counts = counts_ref[...]
    spots = lax.broadcasted_iota(jnp.int32, counts.shape, 1)
    live = jnp.sum(
        jnp.where(spots == first // block_rows, counts, 0), axis=1, keepdims=True
    ) - first % block_rows
    each = len(terms) // parts
    columns = out_ref.shape[1] // parts
    for part in range(parts):
        summed = 0.0
        for term in terms[part * each : (part + 1) * each]:
            summed += term[...].astype(F32)
        row = lax.broadcasted_iota(jnp.int32, summed.shape, 0)
        out_ref[:, part * columns : (part + 1) * columns] = jnp.where(
            row < live, summed, 0.0
        ).astype(BF16)


def last(members, counts, halves):
    terms = [term for half in halves for term in half]
    rows, columns = terms[0].shape
    return pl.pallas_call(
        functools.partial(last_kernel, counts.shape[1], members, len(halves)),
        in_specs=whole(1 + len(terms)),
        out_specs=whole(1)[0],
        out_shape=jax.ShapeDtypeStruct((rows, columns * len(halves)), BF16),
        compiler_params=params(),
        name="last",
    )(counts, *terms)


def add_kernel(starts, *refs):
    out_ref = refs[-1]
    rows = out_ref.shape[0]
    total = 0.0
    for start, ref in zip(starts, refs[:-1], strict=True):
        total += ref[start : start + rows, :].astype(F32)
    out_ref[...] = total.astype(BF16)


def added(rows, *terms):
    starts = [start for start, _ in terms]
    columns = terms[0][1].shape[1]
    return pl.pallas_call(
        functools.partial(add_kernel, starts),
        in_specs=whole(len(terms)),
        out_specs=whole(1)[0],
        out_shape=jax.ShapeDtypeStruct((rows, columns), BF16),
        compiler_params=params(),
        cost_estimate=cost(len(terms) * rows * columns, 2 * rows * columns),
        name="added",
    )(*[term for _, term in terms])


def per_device(
    members,
    tokens,
    gate_matrix,
    up_matrix,
    down_matrix,
    shrink_matrices,
    expand_matrices,
    adapter_per_block,
    block_token_count,
):
    rows = tokens.shape[0]
    span = shrink_matrices.shape[2]
    reach = members // 4
    ring = around(members)

    def step(x):
        return lax.ppermute(x, "tp", ring)

    def cross(x, bit=1):
        return lax.ppermute(x, "tp", crossing(members, bit))

    first = tokens
    own, second = anchor(tokens, cross(tokens))
    shrink = jnp.swapaxes(shrink_matrices, 1, 2)
    other_shrink = cross(shrink)
    pieces, mine, theirs = [own, second], [], []
    for distance in range(1, reach + 1):
        first = step(first)
        mine.append(first)
        theirs.append(cross(first))
        if distance < reach:
            second = step(second)
            mine.append(second)
            theirs.append(cross(second))
    pieces = pieces + mine + theirs

    adapters, counts = adapter_per_block[None], block_token_count[None]
    received = [0] + list(range(2, 2 + len(mine)))
    rank, expand = rank_of(
        adapters,
        members,
        received,
        [pieces[i] for i in received],
        shrink,
        other_shrink,
        expand_matrices,
        theirs[:-1],
    )
    work = [(gate_matrix, 0), (gate_matrix, 1), (up_matrix, 0), (up_matrix, 1)]
    products, aside, after, bit = [], [0, 0], rank, 1
    while bit < members or work:
        if work:
            matrix, part = work.pop(0)
            result, *left = product(
                pieces, matrix, part, 2, after, WEIGHTS[len(products)], aside[part]
            )
            aside[part] = left[0] if left else None
            products.append(result)
        if bit < members:
            after = cross(rank, bit)
            rank = rank + after if bit == 1 else jnp.concatenate([rank, after], axis=0)
            bit *= 2
    products += [x for x in aside if x is not None]
    hidden = finish(products, rank, expand, 2 * span, rows)

    slots = 2 * reach
    groups = [1] * slots + [1] + [2] * (reach - 1) + [1]
    outs = down(hidden, down_matrix, groups, rows)
    keep, give = outs[:slots], outs[slots:]
    came = [cross(give[0])]
    came += [cross(tie(x, came[0])) for x in give[1:]]
    first = step(added(rows, (0, keep[0]), (0, came[0])))
    second = None
    for index in range(1, reach):
        more = [] if second is None else [(0, second)]
        second = step(added(rows, (0, keep[2 * index]), (rows, came[index]), *more))
        first = step(added(rows, (0, keep[2 * index - 1]), (0, came[index]), (0, first)))
    return last(members, counts, [[keep[-1], came[-1], first, cross(second)]])


def solution(mesh):
    members = mesh.shape["tp"]
    return jax.shard_map(
        functools.partial(per_device, members),
        mesh=mesh,
        in_specs=(
            P(("rep", "tp"), None),
            P(None, "tp"),
            P(None, "tp"),
            P("tp", None),
            P("rep", None, "tp"),
            P("rep", None, "tp"),
            P("rep"),
            P("rep"),
        ),
        out_specs=P(("rep", "tp"), None),
        check_vma=False,
    )
```

```python
import functools

import jax
import jax.numpy as jnp
from jax import lax
from jax.experimental import pallas as pl
from jax.experimental.pallas import tpu as pltpu
from jax.sharding import PartitionSpec as P

F32 = jnp.float32
BF16 = jnp.bfloat16
VMEM_LIMIT = 8 * 1024 * 1024
WEIGHTS = (6, 6, 6, 6)


def largest_tile(size, limit):
    tile = limit
    while size % tile:
        tile //= 2
    return tile


def params():
    return pltpu.CompilerParams(vmem_limit_bytes=VMEM_LIMIT)


def cost(flops, moved):
    return pl.CostEstimate(flops=flops, bytes_accessed=moved, transcendentals=0)


def ring_of(chips):
    return list(range(0, chips, 2)) + list(range(chips - 1, 0, -2))


def piece_row(device, members, rows, side, distance, half):
    chips = members // 2
    chip = device // 2
    place = jnp.where(chip % 2 == 0, chip // 2, chips - (chip + 1) // 2)
    spot = (place + chips + jnp.where(side == 0, distance, -distance)) % chips
    there = jnp.where(spot < chips // 2, 2 * spot, 2 * (chips - spot) - 1)
    return pl.multiple_of((2 * there + half) * rows, rows)


def arrivals(device, members, rows):
    core, reach = device % 2, members // 4
    places = [(core, 0, core), (core, 0, 1 - core)]
    for side in (core, 1 - core):
        for step in range(1, reach + 1):
            places.append((1 - side, step, side))
            if step < reach:
                places.append((1 - side, step, 1 - side))
    return [piece_row(device, members, rows, *place) for place in places]


def departures(device, members, rows):
    core, reach = device % 2, members // 4
    places = []
    for side in (core, 1 - core):
        places.append((side, reach, side))
        for step in range(reach - 1, 0, -1):
            places += [(side, step, side), (side, step, 1 - side)]
        places.append((side, 0, side))
    return [piece_row(device, members, rows, *place) for place in places]


def around(members):
    ring = ring_of(members // 2)
    size = len(ring)
    pairs = []
    for i in range(size):
        pairs.append((2 * ring[i], 2 * ring[(i + 1) % size]))
        pairs.append((2 * ring[i] + 1, 2 * ring[i - 1] + 1))
    return pairs


def crossing(members, bit):
    return [(i, i ^ bit) for i in range(members)]


def whole(count):
    return [pl.BlockSpec(memory_space=pltpu.VMEM)] * count


FAR = pl.BlockSpec(memory_space=pl.ANY)


def far(x):
    return pltpu.with_memory_space_constraint(x, pltpu.HBM)


def picked(ref, index):
    row = ref[...]
    spots = lax.broadcasted_iota(jnp.int32, row.shape, 1)
    return jnp.sum(jnp.where(spots == index, row, 0))


def anchor_kernel(tokens_ref, passed_in, own_ref, passed_out, sem):
    copy = pltpu.make_async_copy(tokens_ref, own_ref, sem)
    copy.start()
    copy.wait()


def anchor(tokens, passed):
    return pl.pallas_call(
        anchor_kernel,
        in_specs=[FAR, FAR],
        out_specs=whole(1) + [FAR],
        out_shape=[jax.ShapeDtypeStruct(passed.shape, passed.dtype)] * 2,
        input_output_aliases={1: 1},
        scratch_shapes=[pltpu.SemaphoreType.DMA],
        compiler_params=params(),
        cost_estimate=cost(30_000_000_000, 0),
        name="anchor",
    )(far(tokens), passed)


def tie_kernel(x_ref, after_ref, out_ref):
    del x_ref, after_ref, out_ref


def tie(x, after):
    return pl.pallas_call(
        tie_kernel,
        in_specs=[FAR, FAR],
        out_specs=FAR,
        out_shape=jax.ShapeDtypeStruct(x.shape, x.dtype),
        input_output_aliases={0: 0},
        compiler_params=params(),
        name="tie",
    )(x, after)


def rank_kernel(members, numbers, ids_ref, expand_ref, own_ref, other_ref, *refs):
    pieces, (out_ref, chosen_ref, scratch, sems) = refs[: len(numbers)], refs[-4:]
    rows = pieces[0].shape[0]
    blocks, span = ids_ref.shape[1], own_ref.shape[1]
    block_rows = members * rows // blocks
    device = lax.axis_index("tp")
    places = arrivals(device, members, rows)
    ids = [picked(ids_ref, b) for b in range(blocks)]
    copies = [
        pltpu.make_async_copy(expand_ref.at[ids[b]], chosen_ref.at[b], sems.at[b])
        for b in range(blocks)
    ]
    for copy in copies:
        copy.start()
    weights = jnp.concatenate([ref[i] for ref in (own_ref, other_ref) for i in ids], axis=0)
    wanted = weights.shape[0]
    slices = max(1, 256 // wanted)
    depth = weights.shape[1] // slices
    spans = [slice(i * depth, (i + 1) * depth) for i in range(slices)]
    lhs = jnp.concatenate([piece[:, cut] for cut in spans for piece in pieces], axis=0)
    rhs = jnp.concatenate([weights[:, cut] for cut in spans], axis=0)
    squares = lax.dot_general(lhs, rhs, (((1,), (1,)), ((), ())), preferred_element_type=F32)
    height = len(pieces) * rows
    found = 0.0
    for i in range(slices):
        found += squares[i * height : (i + 1) * height, i * wanted : (i + 1) * wanted]
    scratch[...] = jnp.zeros_like(scratch)
    lower = device % 2 == 0
    for index, number in enumerate(numbers):
        part = found[index * rows : (index + 1) * rows]
        values = []
        for source in range(2):
            first = source * blocks * span
            value = part[:, first : first + span]
            for b in range(1, blocks):
                columns = part[:, first + b * span : first + (b + 1) * span]
                value = jnp.where(places[number] // block_rows == b, columns, value)
            values.append(value)
        own, other = values
        both = [jnp.where(lower, own, other), jnp.where(lower, other, own)]
        scratch[pl.ds(places[number], rows), : 2 * span] = jnp.concatenate(both, axis=1)
    out_ref[...] = scratch[...].T[: 2 * span].astype(BF16)
    for copy in copies:
        copy.wait()


def rank_of(adapters, members, numbers, pieces, shrink, other, expand, after):
    rows, model = pieces[0].shape
    span = shrink.shape[1]
    total = rows * members
    return pl.pallas_call(
        functools.partial(rank_kernel, members, numbers),
        in_specs=whole(1) + [FAR] + whole(2 + len(pieces)) + [FAR] * len(after),
        out_specs=whole(2),
        out_shape=[
            jax.ShapeDtypeStruct((2 * span, total), BF16),
            jax.ShapeDtypeStruct((adapters.shape[1],) + expand.shape[1:], BF16),
        ],
        scratch_shapes=[
            pltpu.VMEM((total, 128), F32),
            pltpu.SemaphoreType.DMA((adapters.shape[1],)),
        ],
        compiler_params=params(),
        cost_estimate=cost(2 * total * model * span * 2, 2 * total * model),
        name="rank",
    )(adapters, far(expand), shrink, other, *pieces, *after)


def product_kernel(first, depth, main, role, w_ref, *refs):
    outs = 1 if role is None else 2
    refs, outs = refs[:-outs], refs[-outs:]
    aside, pieces = (refs[:1], refs[1:-1]) if role == 1 else ((), refs[:-1])
    rows = pieces[0].shape[0]
    places = arrivals(lax.axis_index("tp"), len(pieces), rows)
    lhs = jnp.concatenate([piece[:, first : first + depth] for piece in pieces], axis=0)
    span = slice(first, first + depth)

    def store(out_ref, weights):
        part = jnp.dot(lhs, weights, preferred_element_type=F32)
        for index, place in enumerate(places):
            out_ref[pl.ds(place, rows), :] = part[index * rows : (index + 1) * rows]

    store(outs[0], w_ref[span, :main])
    if role == 0:
        outs[1][...] = w_ref[span, main:]
    elif role == 1:
        store(outs[1], jnp.concatenate([w_ref[span, main:], aside[0][...]], axis=1))


def product(pieces, matrix, part, parts, after, weight, aside):
    rows = pieces[0].shape[0]
    total = rows * len(pieces)
    model, width = matrix.shape
    depth = model // parts
    tail = 128 if width % 256 == 128 else 0
    main = width - tail
    out_shape = [jax.ShapeDtypeStruct((total, main), F32)]
    role, extra = None, []
    if tail and isinstance(aside, int):
        role = 0
        out_shape.append(jax.ShapeDtypeStruct((depth, tail), BF16))
    elif tail:
        role, extra = 1, [aside]
        out_shape.append(jax.ShapeDtypeStruct((total, 2 * tail), F32))
    return pl.pallas_call(
        functools.partial(product_kernel, part * depth, depth, main, role),
        in_specs=whole(len(pieces) + 2 + len(extra)),
        out_specs=whole(len(out_shape)),
        out_shape=out_shape,
        compiler_params=params(),
        cost_estimate=cost(weight * total * depth * width, 2 * depth * (width + total)),
        name="product",
    )(matrix, *extra, *pieces, after)


def finish_kernel(span, piece_rows, *refs):
    *products, rank_ref, expand_ref, out_ref, hidden_ref = refs
    gate_a, gate_b, up_a, up_b, *tails = products
    ranks = rank_ref.shape[0]
    chip = lax.axis_index("tp") // 2
    shape = (ranks, ranks)
    want = lax.broadcasted_iota(jnp.int32, shape, 0)
    have = lax.broadcasted_iota(jnp.int32, shape, 1)
    origin = ((have // span) ^ chip) * span + have % span
    order = jnp.where(want == origin, 1.0, 0.0).astype(BF16)
    rank = jnp.dot(order, rank_ref[...], preferred_element_type=F32).T.astype(BF16)
    half = ranks // 2
    blocks = expand_ref.shape[0]
    rows = hidden_ref.shape[0] // blocks
    main = gate_a.shape[1]
    tail = hidden_ref.shape[1] - main
    for b in range(blocks):
        part = slice(b * rows, (b + 1) * rows)
        expand = expand_ref[b]
        gate = jnp.dot(rank[part, :half], expand[:half], preferred_element_type=F32)
        up = jnp.dot(rank[part, half:], expand[half:], preferred_element_type=F32)
        gates = [gate[:, :main] + gate_a[part] + gate_b[part]]
        ups = [up[:, :main] + up_a[part] + up_b[part]]
        if tail:
            both = tails[0][part] + tails[1][part]
            gates.append(gate[:, main:] + both[:, tail:])
            ups.append(up[:, main:] + both[:, :tail])
        column = 0
        for gate, up in zip(gates, ups, strict=True):
            hidden = (gate / (1.0 + jnp.exp(-gate)) * up).astype(BF16)
            hidden_ref[part, column : column + gate.shape[1]] = hidden
            column += gate.shape[1]
    members = hidden_ref.shape[0] // piece_rows
    for index, place in enumerate(departures(lax.axis_index("tp"), members, piece_rows)):
        out_ref[index * piece_rows : (index + 1) * piece_rows, :] = hidden_ref[
            pl.ds(place, piece_rows), :
        ]


def finish(products, rank, expand, span, piece_rows):
    total, width = products[0].shape[0], expand.shape[2]
    return pl.pallas_call(
        functools.partial(finish_kernel, span, piece_rows),
        in_specs=whole(len(products) + 2),
        out_specs=whole(1)[0],
        out_shape=jax.ShapeDtypeStruct((total, width), BF16),
        scratch_shapes=[pltpu.VMEM((total, width), BF16)],
        compiler_params=params(),
        name="finish",
    )(*products, rank, expand)


def down_kernel(groups, rows, size, w_ref, hidden_ref, *outs):
    hidden = hidden_ref[...]
    for start in range(0, w_ref.shape[1], size):
        columns = slice(start, start + size)
        part = jnp.dot(hidden, w_ref[:, columns], preferred_element_type=F32)
        at = 0
        for out, group in zip(outs, groups, strict=True):
            out[:, columns] = part[at : at + group * rows].astype(BF16)
            at += group * rows


def down(hidden, down_matrix, groups, rows):
    total, depth = hidden.shape
    columns = down_matrix.shape[1]
    size = min(2048, columns)
    return pl.pallas_call(
        functools.partial(down_kernel, groups, rows, size),
        in_specs=whole(2),
        out_specs=whole(len(groups)),
        out_shape=[jax.ShapeDtypeStruct((group * rows, columns), BF16) for group in groups],
        compiler_params=params(),
        cost_estimate=cost(
            2 * total * depth * columns, 2 * depth * columns + 2 * total * columns
        ),
        name="down",
    )(down_matrix, hidden)


def last_kernel(blocks, members, parts, counts_ref, *refs):
    terms, out_ref = refs[:-1], refs[-1]
    rows = out_ref.shape[0]
    first = lax.axis_index("tp") * rows
    block_rows = members * rows // blocks
    counts = counts_ref[...]
    spots = lax.broadcasted_iota(jnp.int32, counts.shape, 1)
    live = jnp.sum(
        jnp.where(spots == first // block_rows, counts, 0), axis=1, keepdims=True
    ) - first % block_rows
    each = len(terms) // parts
    columns = out_ref.shape[1] // parts
    for part in range(parts):
        summed = 0.0
        for term in terms[part * each : (part + 1) * each]:
            summed += term[...].astype(F32)
        row = lax.broadcasted_iota(jnp.int32, summed.shape, 0)
        out_ref[:, part * columns : (part + 1) * columns] = jnp.where(
            row < live, summed, 0.0
        ).astype(BF16)


def last(members, counts, halves):
    terms = [term for half in halves for term in half]
    rows, columns = terms[0].shape
    return pl.pallas_call(
        functools.partial(last_kernel, counts.shape[1], members, len(halves)),
        in_specs=whole(1 + len(terms)),
        out_specs=whole(1)[0],
        out_shape=jax.ShapeDtypeStruct((rows, columns * len(halves)), BF16),
        compiler_params=params(),
        name="last",
    )(counts, *terms)


def add_kernel(starts, *refs):
    out_ref = refs[-1]
    rows = out_ref.shape[0]
    total = 0.0
    for start, ref in zip(starts, refs[:-1], strict=True):
        total += ref[start : start + rows, :].astype(F32)
    out_ref[...] = total.astype(BF16)


def added(rows, *terms):
    starts = [start for start, _ in terms]
    columns = terms[0][1].shape[1]
    return pl.pallas_call(
        functools.partial(add_kernel, starts),
        in_specs=whole(len(terms)),
        out_specs=whole(1)[0],
        out_shape=jax.ShapeDtypeStruct((rows, columns), BF16),
        compiler_params=params(),
        cost_estimate=cost(len(terms) * rows * columns, 2 * rows * columns),
        name="added",
    )(*[term for _, term in terms])


def per_device(
    members,
    tokens,
    gate_matrix,
    up_matrix,
    down_matrix,
    shrink_matrices,
    expand_matrices,
    adapter_per_block,
    block_token_count,
):
    rows = tokens.shape[0]
    span = shrink_matrices.shape[2]
    reach = members // 4
    ring = around(members)

    def step(x):
        return lax.ppermute(x, "tp", ring)

    def cross(x, bit=1):
        return lax.ppermute(x, "tp", crossing(members, bit))

    first = tokens
    own, second = anchor(tokens, cross(tokens))
    shrink = jnp.swapaxes(shrink_matrices, 1, 2)
    other_shrink = cross(shrink)
    pieces, mine, theirs = [own, second], [], []
    for distance in range(1, reach + 1):
        first = step(first)
        mine.append(first)
        theirs.append(cross(first))
        if distance < reach:
            second = step(second)
            mine.append(second)
            theirs.append(cross(second))
    pieces = pieces + mine + theirs

    adapters, counts = adapter_per_block[None], block_token_count[None]
    received = [0] + list(range(2, 2 + len(mine)))
    rank, expand = rank_of(
        adapters,
        members,
        received,
        [pieces[i] for i in received],
        shrink,
        other_shrink,
        expand_matrices,
        theirs[:-1],
    )
    work = [(gate_matrix, 0), (gate_matrix, 1), (up_matrix, 0), (up_matrix, 1)]
    products, aside, after, bit = [], [0, 0], rank, 1
    while bit < members or work:
        if work:
            matrix, part = work.pop(0)
            result, *left = product(
                pieces, matrix, part, 2, after, WEIGHTS[len(products)], aside[part]
            )
            aside[part] = left[0] if left else None
            products.append(result)
        if bit < members:
            after = cross(rank, bit)
            rank = rank + after if bit == 1 else jnp.concatenate([rank, after], axis=0)
            bit *= 2
    products += [x for x in aside if x is not None]
    hidden = finish(products, rank, expand, 2 * span, rows)

    slots = 2 * reach
    groups = [1] * slots + [1] + [2] * (reach - 1) + [1]
    outs = down(hidden, down_matrix, groups, rows)
    keep, give = outs[:slots], outs[slots:]
    came = [cross(give[0])]
    came += [cross(tie(x, came[0])) for x in give[1:]]
    first = step(added(rows, (0, keep[0]), (0, came[0])))
    second = None
    for index in range(1, reach):
        more = [] if second is None else [(0, second)]
        second = step(added(rows, (0, keep[2 * index]), (rows, came[index]), *more))
        first = step(added(rows, (0, keep[2 * index - 1]), (0, came[index]), (0, first)))
    return last(members, counts, [[keep[-1], came[-1], first, cross(second)]])


def solution(mesh):
    members = mesh.shape["tp"]
    return jax.shard_map(
        functools.partial(per_device, members),
        mesh=mesh,
        in_specs=(
            P(("rep", "tp"), None),
            P(None, "tp"),
            P(None, "tp"),
            P("tp", None),
            P("rep", None, "tp"),
            P("rep", None, "tp"),
            P("rep"),
            P("rep"),
        ),
        out_specs=P(("rep", "tp"), None),
        check_vma=False,
    )
```

```python
import functools

import jax
import jax.numpy as jnp
from jax import lax
from jax.experimental import pallas as pl
from jax.experimental.pallas import tpu as pltpu
from jax.sharding import PartitionSpec as P

F32 = jnp.float32
BF16 = jnp.bfloat16
VMEM_LIMIT = 8 * 1024 * 1024
WEIGHTS = (6, 6, 6, 6)


def largest_tile(size, limit):
    tile = limit
    while size % tile:
        tile //= 2
    return tile


def params():
    return pltpu.CompilerParams(vmem_limit_bytes=VMEM_LIMIT)


def cost(flops, moved):
    return pl.CostEstimate(flops=flops, bytes_accessed=moved, transcendentals=0)


def ring_of(chips):
    return list(range(0, chips, 2)) + list(range(chips - 1, 0, -2))


def piece_row(device, members, rows, side, distance, half):
    chips = members // 2
    chip = device // 2
    place = jnp.where(chip % 2 == 0, chip // 2, chips - (chip + 1) // 2)
    spot = (place + chips + jnp.where(side == 0, distance, -distance)) % chips
    there = jnp.where(spot < chips // 2, 2 * spot, 2 * (chips - spot) - 1)
    return pl.multiple_of((2 * there + half) * rows, rows)


def arrivals(device, members, rows):
    core, reach = device % 2, members // 4
    places = [(core, 0, core), (core, 0, 1 - core)]
    for side in (core, 1 - core):
        for step in range(1, reach + 1):
            places.append((1 - side, step, side))
            if step < reach:
                places.append((1 - side, step, 1 - side))
    return [piece_row(device, members, rows, *place) for place in places]


def departures(device, members, rows):
    core, reach = device % 2, members // 4
    places = []
    for side in (core, 1 - core):
        places.append((side, reach, side))
        for step in range(reach - 1, 0, -1):
            places += [(side, step, side), (side, step, 1 - side)]
        places.append((side, 0, side))
    return [piece_row(device, members, rows, *place) for place in places]


def around(members):
    ring = ring_of(members // 2)
    size = len(ring)
    pairs = []
    for i in range(size):
        pairs.append((2 * ring[i], 2 * ring[(i + 1) % size]))
        pairs.append((2 * ring[i] + 1, 2 * ring[i - 1] + 1))
    return pairs


def crossing(members, bit):
    return [(i, i ^ bit) for i in range(members)]


def whole(count):
    return [pl.BlockSpec(memory_space=pltpu.VMEM)] * count


FAR = pl.BlockSpec(memory_space=pl.ANY)


def far(x):
    return pltpu.with_memory_space_constraint(x, pltpu.HBM)


def picked(ref, index):
    row = ref[...]
    spots = lax.broadcasted_iota(jnp.int32, row.shape, 1)
    return jnp.sum(jnp.where(spots == index, row, 0))


def anchor_kernel(tokens_ref, passed_in, own_ref, passed_out, sem):
    copy = pltpu.make_async_copy(tokens_ref, own_ref, sem)
    copy.start()
    copy.wait()


def anchor(tokens, passed):
    return pl.pallas_call(
        anchor_kernel,
        in_specs=[FAR, FAR],
        out_specs=whole(1) + [FAR],
        out_shape=[jax.ShapeDtypeStruct(passed.shape, passed.dtype)] * 2,
        input_output_aliases={1: 1},
        scratch_shapes=[pltpu.SemaphoreType.DMA],
        compiler_params=params(),
        cost_estimate=cost(30_000_000_000, 0),
        name="anchor",
    )(far(tokens), passed)


def tie_kernel(x_ref, after_ref, out_ref):
    del x_ref, after_ref, out_ref


def tie(x, after):
    return pl.pallas_call(
        tie_kernel,
        in_specs=[FAR, FAR],
        out_specs=FAR,
        out_shape=jax.ShapeDtypeStruct(x.shape, x.dtype),
        input_output_aliases={0: 0},
        compiler_params=params(),
        name="tie",
    )(x, after)


def rank_kernel(members, numbers, ids_ref, expand_ref, own_ref, other_ref, *refs):
    pieces, (out_ref, chosen_ref, scratch, sems) = refs[: len(numbers)], refs[-4:]
    rows = pieces[0].shape[0]
    blocks, span = ids_ref.shape[1], own_ref.shape[1]
    block_rows = members * rows // blocks
    device = lax.axis_index("tp")
    places = arrivals(device, members, rows)
    ids = [picked(ids_ref, b) for b in range(blocks)]
    copies = [
        pltpu.make_async_copy(expand_ref.at[ids[b]], chosen_ref.at[b], sems.at[b])
        for b in range(blocks)
    ]
    for copy in copies:
        copy.start()
    weights = jnp.concatenate([ref[i] for ref in (own_ref, other_ref) for i in ids], axis=0)
    wanted = weights.shape[0]
    slices = max(1, 256 // wanted)
    depth = weights.shape[1] // slices
    spans = [slice(i * depth, (i + 1) * depth) for i in range(slices)]
    lhs = jnp.concatenate([piece[:, cut] for cut in spans for piece in pieces], axis=0)
    rhs = jnp.concatenate([weights[:, cut] for cut in spans], axis=0)
    squares = lax.dot_general(lhs, rhs, (((1,), (1,)), ((), ())), preferred_element_type=F32)
    height = len(pieces) * rows
    found = 0.0
    for i in range(slices):
        found += squares[i * height : (i + 1) * height, i * wanted : (i + 1) * wanted]
    scratch[...] = jnp.zeros_like(scratch)
    for index, number in enumerate(numbers):
        part = found[index * rows : (index + 1) * rows]
        for source in range(2):
            first = source * blocks * span
            value = part[:, first : first + span]
            for b in range(1, blocks):
                columns = part[:, first + b * span : first + (b + 1) * span]
                value = jnp.where(places[number] // block_rows == b, columns, value)
            scratch[source, pl.ds(places[number], rows), :span] = value
    own, other = scratch[0].T[:span], scratch[1].T[:span]
    lower = device % 2 == 0
    out_ref[...] = jnp.concatenate(
        [jnp.where(lower, own, other), jnp.where(lower, other, own)], axis=0
    ).astype(BF16)
    for copy in copies:
        copy.wait()


def rank_of(adapters, members, numbers, pieces, shrink, other, expand, after):
    rows, model = pieces[0].shape
    span = shrink.shape[1]
    total = rows * members
    return pl.pallas_call(
        functools.partial(rank_kernel, members, numbers),
        in_specs=whole(1) + [FAR] + whole(2 + len(pieces)) + [FAR] * len(after),
        out_specs=whole(2),
        out_shape=[
            jax.ShapeDtypeStruct((2 * span, total), BF16),
            jax.ShapeDtypeStruct((adapters.shape[1],) + expand.shape[1:], BF16),
        ],
        scratch_shapes=[
            pltpu.VMEM((2, total, 128), F32),
            pltpu.SemaphoreType.DMA((adapters.shape[1],)),
        ],
        compiler_params=params(),
        cost_estimate=cost(2 * total * model * span * 2, 2 * total * model),
        name="rank",
    )(adapters, far(expand), shrink, other, *pieces, *after)


def product_kernel(first, depth, main, role, w_ref, *refs):
    outs = 1 if role is None else 2
    refs, outs = refs[:-outs], refs[-outs:]
    aside, pieces = (refs[:1], refs[1:-1]) if role == 1 else ((), refs[:-1])
    rows = pieces[0].shape[0]
    places = arrivals(lax.axis_index("tp"), len(pieces), rows)
    lhs = jnp.concatenate([piece[:, first : first + depth] for piece in pieces], axis=0)
    span = slice(first, first + depth)

    def store(out_ref, weights):
        part = jnp.dot(lhs, weights, preferred_element_type=F32)
        for index, place in enumerate(places):
            out_ref[pl.ds(place, rows), :] = part[index * rows : (index + 1) * rows]

    store(outs[0], w_ref[span, :main])
    if role == 0:
        outs[1][...] = w_ref[span, main:]
    elif role == 1:
        store(outs[1], jnp.concatenate([w_ref[span, main:], aside[0][...]], axis=1))


def product(pieces, matrix, part, parts, after, weight, aside):
    rows = pieces[0].shape[0]
    total = rows * len(pieces)
    model, width = matrix.shape
    depth = model // parts
    tail = 128 if width % 256 == 128 else 0
    main = width - tail
    out_shape = [jax.ShapeDtypeStruct((total, main), F32)]
    role, extra = None, []
    if tail and isinstance(aside, int):
        role = 0
        out_shape.append(jax.ShapeDtypeStruct((depth, tail), BF16))
    elif tail:
        role, extra = 1, [aside]
        out_shape.append(jax.ShapeDtypeStruct((total, 2 * tail), F32))
    return pl.pallas_call(
        functools.partial(product_kernel, part * depth, depth, main, role),
        in_specs=whole(len(pieces) + 2 + len(extra)),
        out_specs=whole(len(out_shape)),
        out_shape=out_shape,
        compiler_params=params(),
        cost_estimate=cost(weight * total * depth * width, 2 * depth * (width + total)),
        name="product",
    )(matrix, *extra, *pieces, after)


def finish_kernel(span, piece_rows, steps, *refs):
    *products, rank_ref, expand_ref, out_ref, hidden_ref = refs
    gate_a, gate_b, up_a, up_b, *tails = products
    ranks = rank_ref.shape[0]
    chip = lax.axis_index("tp") // 2
    shape = (ranks, ranks)
    want = lax.broadcasted_iota(jnp.int32, shape, 0)
    have = lax.broadcasted_iota(jnp.int32, shape, 1)
    away = 0
    for place, step in enumerate(steps):
        away += ((have // span) >> place) % 2 * step
    origin = (away ^ chip) * span + have % span
    order = jnp.where(want == origin, 1.0, 0.0).astype(BF16)
    rank = jnp.dot(order, rank_ref[...], preferred_element_type=F32).T.astype(BF16)
    half = ranks // 2
    blocks = expand_ref.shape[0]
    rows = hidden_ref.shape[0] // blocks
    main = gate_a.shape[1]
    tail = hidden_ref.shape[1] - main
    for b in range(blocks):
        part = slice(b * rows, (b + 1) * rows)
        expand = expand_ref[b]
        gate = jnp.dot(rank[part, :half], expand[:half], preferred_element_type=F32)
        up = jnp.dot(rank[part, half:], expand[half:], preferred_element_type=F32)
        gates = [gate[:, :main] + gate_a[part] + gate_b[part]]
        ups = [up[:, :main] + up_a[part] + up_b[part]]
        if tail:
            both = tails[0][part] + tails[1][part]
            gates.append(gate[:, main:] + both[:, tail:])
            ups.append(up[:, main:] + both[:, :tail])
        column = 0
        for gate, up in zip(gates, ups, strict=True):
            hidden = (gate / (1.0 + jnp.exp(-gate)) * up).astype(BF16)
            hidden_ref[part, column : column + gate.shape[1]] = hidden
            column += gate.shape[1]
    members = hidden_ref.shape[0] // piece_rows
    for index, place in enumerate(departures(lax.axis_index("tp"), members, piece_rows)):
        out_ref[index * piece_rows : (index + 1) * piece_rows, :] = hidden_ref[
            pl.ds(place, piece_rows), :
        ]


def finish(products, rank, expand, span, piece_rows, steps):
    total, width = products[0].shape[0], expand.shape[2]
    return pl.pallas_call(
        functools.partial(finish_kernel, span, piece_rows, steps),
        in_specs=whole(len(products) + 2),
        out_specs=whole(1)[0],
        out_shape=jax.ShapeDtypeStruct((total, width), BF16),
        scratch_shapes=[pltpu.VMEM((total, width), BF16)],
        compiler_params=params(),
        name="finish",
    )(*products, rank, expand)


def down_kernel(groups, rows, size, w_ref, hidden_ref, *outs):
    hidden = hidden_ref[...]
    for start in range(0, w_ref.shape[1], size):
        columns = slice(start, start + size)
        part = jnp.dot(hidden, w_ref[:, columns], preferred_element_type=F32)
        at = 0
        for out, group in zip(outs, groups, strict=True):
            out[:, columns] = part[at : at + group * rows].astype(BF16)
            at += group * rows


def down(hidden, down_matrix, groups, rows):
    total, depth = hidden.shape
    columns = down_matrix.shape[1]
    size = min(2048, columns)
    return pl.pallas_call(
        functools.partial(down_kernel, groups, rows, size),
        in_specs=whole(2),
        out_specs=whole(len(groups)),
        out_shape=[jax.ShapeDtypeStruct((group * rows, columns), BF16) for group in groups],
        compiler_params=params(),
        cost_estimate=cost(
            2 * total * depth * columns, 2 * depth * columns + 2 * total * columns
        ),
        name="down",
    )(down_matrix, hidden)


def last_kernel(blocks, members, parts, counts_ref, *refs):
    terms, out_ref = refs[:-1], refs[-1]
    rows = out_ref.shape[0]
    first = lax.axis_index("tp") * rows
    block_rows = members * rows // blocks
    counts = counts_ref[...]
    spots = lax.broadcasted_iota(jnp.int32, counts.shape, 1)
    live = jnp.sum(
        jnp.where(spots == first // block_rows, counts, 0), axis=1, keepdims=True
    ) - first % block_rows
    each = len(terms) // parts
    columns = out_ref.shape[1] // parts
    for part in range(parts):
        summed = 0.0
        for term in terms[part * each : (part + 1) * each]:
            summed += term[...].astype(F32)
        row = lax.broadcasted_iota(jnp.int32, summed.shape, 0)
        out_ref[:, part * columns : (part + 1) * columns] = jnp.where(
            row < live, summed, 0.0
        ).astype(BF16)


def last(members, counts, halves):
    terms = [term for half in halves for term in half]
    rows, columns = terms[0].shape
    return pl.pallas_call(
        functools.partial(last_kernel, counts.shape[1], members, len(halves)),
        in_specs=whole(1 + len(terms)),
        out_specs=whole(1)[0],
        out_shape=jax.ShapeDtypeStruct((rows, columns * len(halves)), BF16),
        compiler_params=params(),
        name="last",
    )(counts, *terms)


def add_kernel(starts, *refs):
    out_ref = refs[-1]
    rows = out_ref.shape[0]
    total = 0.0
    for start, ref in zip(starts, refs[:-1], strict=True):
        total += ref[start : start + rows, :].astype(F32)
    out_ref[...] = total.astype(BF16)


def added(rows, *terms):
    starts = [start for start, _ in terms]
    columns = terms[0][1].shape[1]
    return pl.pallas_call(
        functools.partial(add_kernel, starts),
        in_specs=whole(len(terms)),
        out_specs=whole(1)[0],
        out_shape=jax.ShapeDtypeStruct((rows, columns), BF16),
        compiler_params=params(),
        cost_estimate=cost(len(terms) * rows * columns, 2 * rows * columns),
        name="added",
    )(*[term for _, term in terms])


def per_device(
    members,
    tokens,
    gate_matrix,
    up_matrix,
    down_matrix,
    shrink_matrices,
    expand_matrices,
    adapter_per_block,
    block_token_count,
):
    rows = tokens.shape[0]
    span = shrink_matrices.shape[2]
    reach = members // 4
    ring = around(members)

    def step(x):
        return lax.ppermute(x, "tp", ring)

    def cross(x, bit=1):
        return lax.ppermute(x, "tp", crossing(members, bit))

    first = tokens
    own, second = anchor(tokens, cross(tokens))
    shrink = jnp.swapaxes(shrink_matrices, 1, 2)
    other_shrink = cross(shrink)
    pieces, mine, theirs = [own, second], [], []
    for distance in range(1, reach + 1):
        first = step(first)
        mine.append(first)
        theirs.append(cross(first))
        if distance < reach:
            second = step(second)
            mine.append(second)
            theirs.append(cross(second))
    pieces = pieces + mine + theirs

    adapters, counts = adapter_per_block[None], block_token_count[None]
    received = [0] + list(range(2, 2 + len(mine)))
    rank, expand = rank_of(
        adapters,
        members,
        received,
        [pieces[i] for i in received],
        shrink,
        other_shrink,
        expand_matrices,
        theirs[:-1],
    )
    work = [(gate_matrix, 0), (gate_matrix, 1), (up_matrix, 0), (up_matrix, 1)]
    rounds = [1] + [1 << i for i in range(members.bit_length() - 2, 0, -1)]
    products, aside, after, left_over = [], [0, 0], rank, list(rounds)
    while left_over or work:
        if work:
            matrix, part = work.pop(0)
            result, *left = product(
                pieces, matrix, part, 2, after, WEIGHTS[len(products)], aside[part]
            )
            aside[part] = left[0] if left else None
            products.append(result)
        if left_over:
            bit = left_over.pop(0)
            after = cross(rank, bit)
            rank = rank + after if bit == 1 else jnp.concatenate([rank, after], axis=0)
    products += [x for x in aside if x is not None]
    hidden = finish(products, rank, expand, 2 * span, rows, [bit // 2 for bit in rounds[1:]])

    slots = 2 * reach
    groups = [1] * slots + [1] + [2] * (reach - 1) + [1]
    outs = down(hidden, down_matrix, groups, rows)
    keep, give = outs[:slots], outs[slots:]
    came = [cross(give[0])]
    came += [cross(tie(x, came[0])) for x in give[1:]]
    first = step(added(rows, (0, keep[0]), (0, came[0])))
    second = None
    for index in range(1, reach):
        more = [] if second is None else [(0, second)]
        second = step(added(rows, (0, keep[2 * index]), (rows, came[index]), *more))
        first = step(added(rows, (0, keep[2 * index - 1]), (0, came[index]), (0, first)))
    return last(members, counts, [[keep[-1], came[-1], first, cross(second)]])


def solution(mesh):
    members = mesh.shape["tp"]
    return jax.shard_map(
        functools.partial(per_device, members),
        mesh=mesh,
        in_specs=(
            P(("rep", "tp"), None),
            P(None, "tp"),
            P(None, "tp"),
            P("tp", None),
            P("rep", None, "tp"),
            P("rep", None, "tp"),
            P("rep"),
            P("rep"),
        ),
        out_specs=P(("rep", "tp"), None),
        check_vma=False,
    )
```
